128 devices in a mesh: section: 2 (over core), seq: 16 (over z, y), head: 4 (over x).
Axes of the slice: x: 4, y: 4, z: 4, core: 2. Of those that a mesh axis runs over, the one named last changes fastest.
Arguments:
- tokens_in: bfloat16 [2, 8192, 1536], P(None, ('seq', 'head')), may hold values from -6 to 6
- cotangent: bfloat16 [2, 8192, 1536], P(None, ('seq', 'head')), may hold values from -6 to 6
- input_gain: bfloat16 [2, 1536], P('section', ('seq', 'head')), may hold values from 0.25 to 1.75
- gate_inner: bfloat16 [2, 1536, 6144], P('section', ('seq', 'head')), may hold values from -0.15625 to 0.15625
- shared_bc: bfloat16 [2, 1536, 256], P('section', ('seq', 'head')), may hold values from -0.15625 to 0.15625
- step_proj: bfloat16 [2, 1536, 48], P('section', ('seq', 'head')), may hold values from -0.15625 to 0.15625
- conv_weight: bfloat16 [2, 4, 3328], P('section', None, ('seq', 'head')), may hold values from -3 to 3
- conv_bias: bfloat16 [2, 3328], P('section', ('seq', 'head')), may hold values from -0.5 to 0.5
- step_bias: float32 [2, 48], P('section'), may hold values from -9 to -3
- decay_log: float32 [2, 48], P('section'), may hold values from -1 to 0.5
- skip_gain: float32 [2, 48], P('section'), may hold values from 0.5 to 1.5
- output_gain: bfloat16 [2, 3072], P('section', ('seq', 'head')), may hold values from 0.25 to 1.75
- out_proj: bfloat16 [2, 3072, 1536], P('section', ('seq', 'head')), may hold values from -0.109375 to 0.109375
Outputs:
- layer_out: bfloat16 [2, 2, 8192, 1536], P('section', None, ('seq', 'head'))
- grad_in: bfloat16 [2, 2, 8192, 1536], P('section', None, ('seq', 'head'))
- grad_input_gain: float32 [2, 1536], P('section', ('seq', 'head'))
- grad_gate_inner: float32 [2, 1536, 6144], P('section', ('seq', 'head'))
- grad_shared_bc: float32 [2, 1536, 256], P('section', ('seq', 'head'))
- grad_step_proj: float32 [2, 1536, 48], P('section', ('seq', 'head'))
- grad_conv_weight: float32 [2, 4, 3328], P('section', None, ('seq', 'head'))
- grad_conv_bias: float32 [2, 3328], P('section', ('seq', 'head'))
- grad_step_bias: float32 [2, 48], P('section')
- grad_decay_log: float32 [2, 48], P('section')
- grad_skip_gain: float32 [2, 48], P('section')
- grad_output_gain: float32 [2, 3072], P('section', ('seq', 'head'))
- grad_out_proj: float32 [2, 3072, 1536], P('section', ('seq', 'head'))
The draws below stay inside these ranges and needn't reach their ends.
All inputs are finite; a program needn't handle non-finite values.
Results may differ from the reference program's by a relative error of at most 0.025.
Values may be sent and summed in bfloat16 or wider, within the bound.
No kernel may reach another device: no remote copies, remote signals or barrier semaphores. Data moves between devices by JAX's collectives and lax.ppermute only.
A program may use at most 320 MiB of HBM per device.

```python
import jax
import jax.numpy as jnp
from jax import lax

D = 1536
DI = 3072
H = 48
P_SIZE = 64
N = 128
K = 4
BLOCK = 256
MB = 2
L = 8192
N_HEAD = 4


def shard_levels(own_key, shape, split, least, high):
    level, own = 1.0, jax.random.fold_in(own_key, 6)
    for dim, parts in split:
        heights = jnp.exp(jax.random.uniform(jax.random.fold_in(own, dim), (parts,), jnp.float32, least / len(split), high / len(split)))
        level = level * jnp.repeat(heights, shape[dim] // parts).reshape([-1 if axis == dim else 1 for axis in range(len(shape))])
    return level


def centred(rng, extent, scale, most, cuts=(), dtype=jnp.bfloat16):
    drawn = jax.random.normal(rng, extent, jnp.float32) * scale
    if len(cuts) > 0:
        drawn = shard_levels(rng, extent, cuts, -0.22, 0.18) * drawn
    return jnp.clip(drawn, min=-most, max=most).astype(dtype)


def setup_inputs(seed: int = 0) -> dict:
    key_list = jax.random.split(jax.random.key(seed), 14)
    tokens_in = centred(key_list[0], (MB, L, D), 1.0, 6.0, ((1, 64),))
    cotangent = centred(key_list[1], (MB, L, D), 1.0, 6.0, ((1, 64),))
    input_gain = jnp.clip(1.0 + 0.15 * jax.random.normal(key_list[2], (2, D), jnp.float32), 0.25, 1.75).astype(jnp.bfloat16)
    gate_inner = centred(key_list[3], (2, D, 2 * DI), D ** -0.5, 0.15625, ((0, 2), (1, 64)))
    shared_bc = centred(key_list[4], (2, D, 2 * N), D ** -0.5, 0.15625, ((0, 2), (1, 64)))
    step_proj = centred(key_list[5], (2, D, H), D ** -0.5, 0.15625, ((0, 2), (1, 64)))
    conv_weight = centred(key_list[6], (2, K, DI + 2 * N), K ** -0.5, 3.0, ((0, 2), (2, 64)))
    conv_bias = jnp.clip(jax.random.uniform(key_list[7], (2, DI + 2 * N), jnp.float32, -0.5, 0.5) * shard_levels(key_list[7], (2, DI + 2 * N), ((0, 2), (1, 64)), -0.4, 0.0), -0.5, 0.5).astype(jnp.bfloat16)
    step_bias = jnp.clip(-9.0 + 6.0 * jax.random.uniform(key_list[8], (2, H), jnp.float32) ** shard_levels(key_list[8], (2, H), ((0, 2),), -0.2, 0.2), -9.0, -3.0)
    decay_log = jnp.clip(-1.0 + 1.5 * jax.random.uniform(key_list[9], (2, H), jnp.float32) ** shard_levels(key_list[9], (2, H), ((0, 2),), -0.2, 0.2), -1.0, 0.5)
    skip_gain = jnp.clip(0.5 + 1.0 * jax.random.uniform(key_list[10], (2, H), jnp.float32) ** shard_levels(key_list[10], (2, H), ((0, 2),), -0.2, 0.2), 0.5, 1.5)
    output_gain = jnp.clip(1.0 + 0.15 * jax.random.normal(key_list[11], (2, DI), jnp.float32), 0.25, 1.75).astype(jnp.bfloat16)
    out_proj = centred(key_list[12], (2, DI, D), DI ** -0.5, 0.109375, ((0, 2), (1, 64)))
    return dict(tokens_in=tokens_in, cotangent=cotangent, input_gain=input_gain, gate_inner=gate_inner, shared_bc=shared_bc, step_proj=step_proj, conv_weight=conv_weight, conv_bias=conv_bias, step_bias=step_bias, decay_log=decay_log, skip_gain=skip_gain, output_gain=output_gain, out_proj=out_proj)


epsilon = 1e-05
highest = lax.Precision.HIGHEST

@jax.custom_vjp
def low(v):
    return lax.optimization_barrier(v.astype(jnp.bfloat16)).astype(jnp.float32)

@jax.custom_vjp
def low_back(v):
    return v

def low_keep(v):
    return (low(v), None)

def low_pass(kept, grad):
    return (grad,)

def back_keep(v):
    return (v, None)

def back_low(kept, grad):
    return (low(grad),)
low.defvjp(low_keep, low_pass)
low_back.defvjp(back_keep, back_low)

def rms_scale(values):
    return lax.rsqrt(lax.optimization_barrier(jnp.mean(values * values, axis=-1, keepdims=True)) + epsilon)

def conv_causal(padded, weight, bias):
    width = weight.shape[0]
    length = padded.shape[0] - width + 1
    total = jnp.zeros((length, padded.shape[1]), jnp.float32) + bias[None, :]
    for offset in range(width):
        total = total + weight[offset][None, :] * padded[offset:offset + length]
    return total

def piece_step(carry_state, pieces):
    inner_heads, step_sizes, key_rows, queries, log_decay = pieces
    length = step_sizes.shape[0]
    running = jnp.cumsum(log_decay, axis=0)
    row_index = lax.broadcasted_iota(jnp.int32, (length, length), 0)
    col_index = lax.broadcasted_iota(jnp.int32, (length, length), 1)
    causal = (row_index >= col_index)[:, :, None]
    spread_log = jnp.where(causal, running[:, None, :] - running[None, :, :], 0.0)
    affinity = jnp.dot(queries, key_rows.T, precision=highest)
    weights = jnp.where(causal, jnp.exp(spread_log), 0.0) * affinity[:, :, None] * step_sizes[None, :, :]
    result = jnp.einsum('tsh,shp->thp', weights, inner_heads, precision=highest)
    result = result + jnp.exp(running)[:, :, None] * jnp.einsum('tn,hpn->thp', queries, carry_state, precision=highest)
    carried = jnp.exp(running[-1][None, :] - running) * step_sizes
    carry_state = jnp.exp(running[-1])[:, None, None] * carry_state + jnp.einsum('sh,shp,sn->hpn', carried, inner_heads, key_rows, precision=highest)
    return (carry_state, result)

def scan_heads(inner_act, step_sizes, key_rows, queries, log_decay, start_state, piece_len):
    length, head_count = step_sizes.shape
    pieces_count = length // piece_len

    def to_pieces(values):
        return values.reshape((pieces_count, piece_len) + values.shape[1:])
    inner_heads = inner_act.reshape(length, head_count, -1)
    final_state, outputs = lax.scan(jax.checkpoint(piece_step), start_state, (to_pieces(inner_heads), to_pieces(step_sizes), to_pieces(key_rows), to_pieces(queries), to_pieces(log_decay)))
    return (outputs.reshape(length, -1), final_state)

def layer(feed, input_gain, gate_inner, shared_bc, step_proj, conv_weight, conv_bias, step_bias, decay_log, skip_gain, output_gain, out_proj):
    normed = low(feed * rms_scale(feed) * input_gain[None, :])
    projected = jnp.dot(normed, gate_inner, precision=highest)
    gate_pre = low_back(projected[:, :DI])
    inner = low_back(low(projected[:, DI:]))
    shared = low_back(low(jnp.dot(normed, shared_bc, precision=highest)))
    step_raw = low_back(low(jnp.dot(normed, step_proj, precision=highest)))
    group_width = DI // N_HEAD
    head_count = H // N_HEAD
    mixed_parts = []
    for group_index in range(N_HEAD):
        columns = slice(group_index * group_width, (group_index + 1) * group_width)
        head_slice = slice(group_index * head_count, (group_index + 1) * head_count)
        block_in = jnp.concatenate([inner[:, columns], low_back(shared)], axis=1)
        conv_group = jnp.concatenate([conv_weight[:, columns], conv_weight[:, DI:]], axis=1)
        bias_group = jnp.concatenate([conv_bias[columns], conv_bias[DI:]])
        padded = jnp.pad(block_in, ((K - 1, 0), (0, 0)))
        active = jax.nn.silu(conv_causal(padded, conv_group, bias_group))
        inner_act = active[:, :group_width]
        key_rows = active[:, group_width:group_width + N]
        queries = active[:, group_width + N:]
        step_sizes = jax.nn.softplus(step_raw[:, head_slice] + step_bias[head_slice][None, :])
        log_decay = -jnp.exp(decay_log[head_slice])[None, :] * step_sizes
        start_state = jnp.zeros((head_count, P_SIZE, N), jnp.float32)
        mixed = scan_heads(inner_act, step_sizes, key_rows, queries, log_decay, start_state, BLOCK)[0]
        mixed_parts.append(mixed + jnp.repeat(skip_gain[head_slice], P_SIZE)[None, :] * inner_act)
    scan_out = low_back(low(jnp.concatenate(mixed_parts, axis=1)))
    gated = scan_out * jax.nn.silu(gate_pre)
    normed_out = low(gated * rms_scale(gated) * output_gain[None, :])
    branch = low_back(jnp.dot(normed_out, out_proj, precision=highest))
    return feed + branch

def reference(tokens_in, cotangent, input_gain, gate_inner, shared_bc, step_proj, conv_weight, conv_bias, step_bias, decay_log, skip_gain, output_gain, out_proj):
    stacked = tuple((values.astype(jnp.float32) for values in (input_gain, gate_inner, shared_bc, step_proj, conv_weight, conv_bias, step_bias, decay_log, skip_gain, output_gain, out_proj)))
    first_params = tuple((values[0] for values in stacked))
    second_params = tuple((values[1] for values in stacked))

    def lower_layer(feed, params):
        return low_back(low(layer(feed, *params)))

    def upper_layer(feed, params):
        return layer(feed, *params)

    def one_batch(totals, pair):
        feed, seed_grad = pair
        hidden, pull_lower = jax.vjp(lower_layer, feed.astype(jnp.float32), first_params)
        output, pull_upper = jax.vjp(upper_layer, hidden, second_params)
        grad_hidden, upper_grads = pull_upper(seed_grad.astype(jnp.float32))
        grad_feed, lower_grads = pull_lower(grad_hidden)
        totals = jax.tree.map(lambda total, lower_grad, upper_grad: total + jnp.stack([lower_grad, upper_grad]), totals, lower_grads, upper_grads)
        return (totals, (hidden.astype(jnp.bfloat16), output.astype(jnp.bfloat16), grad_feed.astype(jnp.bfloat16), grad_hidden.astype(jnp.bfloat16)))
    zeros = tuple((jnp.zeros_like(values) for values in stacked))
    totals, (hiddens, outputs, grad_feeds, grad_hiddens) = lax.scan(one_batch, zeros, (tokens_in, cotangent))
    layer_out = jnp.stack([hiddens, outputs])
    grad_in = jnp.stack([grad_feeds, grad_hiddens])
    return (layer_out, grad_in, totals[0], totals[1], totals[2], totals[3], totals[4], totals[5], totals[6], totals[7], totals[8], totals[9], totals[10])
```

```python
import jax
import jax.numpy as jnp
from jax import lax
from jax.experimental import pallas as pl
from jax.experimental.pallas import tpu as pltpu
from jax.sharding import PartitionSpec as P

bf16 = jnp.bfloat16
f32 = jnp.float32
HIGHEST = lax.Precision.HIGHEST

D = 1536
DI = 3072
N = 128
GROUP = 768
HALF = 384
HEADS = 12
PIECE = 128
PAIRS = 6
EXTRA = 256
ACT = GROUP + 2 * N
STEP_AT, SMALL_AT, SMALL = 0, 19, 13
VMEM = 40 * 1024 * 1024
epsilon = 1e-05


def from_head(a, k):
    return lax.ppermute(a, "head", [(i, (i - k) % 4) for i in range(4)])


def from_seq(a, dz, dy, wrap):
    pairs = []
    for z in range(4):
        for y in range(4):
            sz, sy = z + dz, y + dy
            if wrap:
                sz, sy = sz % 4, sy % 4
            if 0 <= sz < 4 and 0 <= sy < 4:
                pairs.append((sz * 4 + sy, z * 4 + y))
    return lax.ppermute(a, "seq", pairs)


def swap(a):
    return lax.ppermute(a, "section", [(0, 1), (1, 0)])


def gather_head(a):
    two = from_head(a, 2)
    one, three = from_head(a, 1), from_head(a, 3)
    return [a, one, two, three]


def scatter_head(parts):
    two = from_head(parts[2].astype(bf16), 2)
    one, three = from_head(parts[1].astype(bf16), 3), from_head(parts[3].astype(bf16), 1)
    return parts[0] + one.astype(f32) + two.astype(f32) + three.astype(f32)


def exchange_head(parts, place):
    got = [lax.dynamic_index_in_dim(parts, place, 0, False)]
    for k in (1, 2, 3):
        sent = lax.dynamic_index_in_dim(parts, lax.rem(place + 4 - k, 4), 0, False)
        got.append(from_head(sent, k))
    twice = jnp.stack(got + got)
    return lax.dynamic_slice_in_dim(twice, lax.rem(4 - place, 4), 4, 0)


def unpack_state(a):
    decay = a[N : N + 1].astype(f32) + a[N + 1 : N + 2].astype(f32)
    return decay, a[:N].astype(f32)


def join(earlier, later):
    return earlier[0] * later[0], earlier[1] * later[0] + later[1]


def carried(packed, sign):
    seq = lax.axis_index("seq")
    y = lax.rem(seq, 4)
    ahead = y if sign < 0 else 3 - y
    near = {k: unpack_state(from_seq(packed, 0, sign * k, True)) for k in (2, 1, 3)}
    own = unpack_state(packed)
    before = (jnp.ones_like(own[0]), jnp.zeros_like(own[1]))
    after = own
    for k in (3, 2, 1):
        decay, state = near[k]
        use = k <= ahead
        before = join(before, (jnp.where(use, decay, 1.0), jnp.where(use, state, 0.0)))
        after = join(after, (jnp.where(use, 1.0, decay), jnp.where(use, 0.0, state)))
    whole = join(before, after)
    packed_whole = pack_state(whole[0], whole[1])
    far = {k: unpack_state(from_seq(packed_whole, sign * k, 0, False)) for k in (2, 1, 3)}
    total = jnp.zeros_like(own[1])
    for k in (3, 2, 1):
        decay, state = far[k]
        total = total * decay + state
    return total * before[0] + before[1]


def pack_state(decay, state):
    high = decay.astype(bf16)
    low = (decay - high.astype(f32)).astype(bf16)
    fill = jnp.zeros((14, state.shape[1]), bf16)
    return jnp.concatenate([state.astype(bf16), high, low, fill], axis=0)


def dot(a, b):
    return jnp.dot(a.astype(bf16), b.astype(bf16), preferred_element_type=f32)


def dot_nt(a, b):
    return lax.dot_general(
        a.astype(bf16), b.astype(bf16), (((1,), (1,)), ((), ())), preferred_element_type=f32
    )


def dot_tn(a, b):
    return lax.dot_general(
        a.astype(bf16), b.astype(bf16), (((0,), (0,)), ((), ())), preferred_element_type=f32
    )


def dot_split(a, b):
    high = a.astype(bf16)
    low = (a - high.astype(f32)).astype(bf16)
    return dot(high, b) + dot(low, b)


def lanes(shape):
    return lax.broadcasted_iota(jnp.int32, shape, 1)


def rows(shape):
    return lax.broadcasted_iota(jnp.int32, shape, 0)


def spread(values, j, first):
    return jnp.where(first, values[:, 2 * j : 2 * j + 1], values[:, 2 * j + 1 : 2 * j + 2])


def step_parts(step, hp):
    raw = step + hp[0:1]
    live = lanes(raw.shape) < HEADS
    sizes = jnp.maximum(raw, 0.0) + jnp.log1p(jnp.exp(-jnp.abs(raw)))
    sizes = jnp.where(live, sizes, 0.0)
    return raw, sizes, -jnp.exp(hp[1:2]) * sizes


def scan_kernel(
    place, conv_in, step, rim, taps, hp, skip, pre_out, mixed, query, run, starts, last, packed,
    padded, act, state, carry
):
    k = pl.program_id(0)

    @pl.when(k == 0)
    def _():
        state[...] = jnp.zeros_like(state)
        carry[...] = jnp.zeros_like(carry)
        padded[0:8] = rim[...].astype(f32)

    @pl.when(k > 0)
    def _():
        padded[0:8] = padded[PIECE : PIECE + 8]

    padded[8 : PIECE + 8] = conv_in[...].astype(f32)
    for j in range(ACT // 128):
        cols = slice(128 * j, 128 * j + 128)
        pre = taps[4:5, cols] + taps[0:1, cols] * padded[5 : PIECE + 5, cols]
        for t in range(1, 4):
            pre = pre + taps[t : t + 1, cols] * padded[5 + t : PIECE + 5 + t, cols]
        pre_out[:, cols] = pre
        act[:, cols] = pre * jax.nn.sigmoid(pre)
    raw, sizes, log_decay = step_parts(step[...], hp[...])
    lower = rows((PIECE, PIECE)) >= lanes((PIECE, PIECE))
    start = carry[0:1]
    running = start + jnp.dot(
        lower.astype(f32), log_decay, precision=HIGHEST, preferred_element_type=f32
    )
    run[...] = running
    end = running[PIECE - 1 : PIECE]
    carry[...] = jnp.broadcast_to(end, carry.shape)
    running_t = running.T
    keys = act[:, GROUP : GROUP + N]
    queries = act[:, GROUP + N :].astype(bf16)
    query[...] = queries
    affinity = jnp.where(lower, dot_nt(queries, keys), 0.0)
    keys_t = keys.T.astype(bf16)
    from_start = jnp.exp(running - start)
    to_end = jnp.exp(end - running)
    whole = jnp.exp(end - start)
    total = jnp.exp(end)
    first = lanes((PIECE, 128)) < 64
    first_row = lanes((1, 128)) < 64
    row16 = rows((16, 128))
    for j in range(PAIRS):
        cols = slice(128 * j, 128 * j + 128)
        x = act[:, cols]
        scaled = x * spread(sizes, j, first)
        y = jnp.zeros((PIECE, 128), f32)
        for side in range(2):
            h = 2 * j + side
            gap = jnp.exp(jnp.minimum(running[:, h : h + 1] - running_t[h : h + 1, :], 0.0))
            mine = jnp.where(first if side == 0 else ~first, scaled, 0.0)
            y = y + dot(gap * affinity, mine)
        before = state[:, cols]
        starts[0, :, cols] = before
        y = y + spread(from_start, j, first) * dot(queries, before)
        mixed[:, cols] = y + skip[0:1, cols] * x
        after = spread(whole, j, first_row) * before + dot(
            keys_t, scaled * spread(to_end, j, first)
        )
        state[:, cols] = after
        last[:, cols] = after
        packed[0:N, cols] = after.astype(bf16)
        decay = jnp.broadcast_to(spread(total, j, first_row), (16, 128))
        high = decay.astype(bf16).astype(f32)
        packed[N : N + 16, cols] = jnp.where(
            row16 == 0, high, jnp.where(row16 == 1, decay - high, 0.0)
        ).astype(bf16)


def turned(k, place):
    return lax.rem(k + 4 - place[0], 4)


def scan_local(place, conv_in, step, rim, taps, hp, skip):
    tokens = conv_in.shape[0]

    def whole(shape):
        return pl.BlockSpec(shape, lambda k, place: (0,) * len(shape))

    def piece(width):
        return pl.BlockSpec((PIECE, width), lambda k, place: (turned(k, place), 0))

    return pl.pallas_call(
        scan_kernel,
        grid_spec=pltpu.PrefetchScalarGridSpec(
            num_scalar_prefetch=1,
            grid=(tokens // PIECE,),
            in_specs=[
                piece(ACT),
                piece(128),
                whole((8, ACT)),
                whole((8, ACT)),
                whole((8, 128)),
                whole((8, GROUP)),
            ],
            out_specs=[
                piece(ACT),
                piece(GROUP),
                piece(N),
                piece(128),
                pl.BlockSpec((1, N, GROUP), lambda k, place: (k, 0, 0)),
                whole((N, GROUP)),
                whole((N + 16, GROUP)),
            ],
            scratch_shapes=[
                pltpu.VMEM((PIECE + 8, ACT), f32),
                pltpu.VMEM((PIECE, ACT), f32),
                pltpu.VMEM((N, GROUP), f32),
                pltpu.VMEM((8, 128), f32),
            ],
        ),
        out_shape=[
            jax.ShapeDtypeStruct((tokens, ACT), f32),
            jax.ShapeDtypeStruct((tokens, GROUP), f32),
            jax.ShapeDtypeStruct((tokens, N), bf16),
            jax.ShapeDtypeStruct((tokens, 128), f32),
            jax.ShapeDtypeStruct((tokens // PIECE, N, GROUP), f32),
            jax.ShapeDtypeStruct((N, GROUP), f32),
            jax.ShapeDtypeStruct((N + 16, GROUP), bf16),
        ],
        compiler_params=pltpu.CompilerParams(vmem_limit_bytes=VMEM),
        cost_estimate=pl.CostEstimate(
            flops=1_000_000_000, bytes_accessed=8_000_000, transcendentals=1_500_000
        ),
        name="scan_local",
    )(place, conv_in, step, rim, taps, hp, skip)


def gate_kernel(mixed, run, query, entering, gate, gain, mixed_out, normed, square):
    decay = jnp.exp(run[...])
    queries = query[...]
    first = lanes((PIECE, 128)) < 64
    total = jnp.zeros((PIECE, 1), f32)
    for j in range(PAIRS):
        cols = slice(128 * j, 128 * j + 128)
        y = mixed[:, cols] + spread(decay, j, first) * dot(queries, entering[:, cols])
        mixed_out[:, cols] = y
        pre = gate[:, cols]
        gated = y.astype(bf16).astype(f32) * (pre * jax.nn.sigmoid(pre))
        total = total + jnp.sum(gated * gated, axis=1, keepdims=True)
        normed[:, cols] = (gated * gain[0:1, cols]).astype(bf16)
    square[...] = jnp.broadcast_to(total, square.shape)


def gate_out(mixed, run, query, entering, gate, gain):
    tokens = mixed.shape[0]

    def whole(shape):
        return pl.BlockSpec(shape, lambda k: (0, 0))

    def piece(width):
        return pl.BlockSpec((PIECE, width), lambda k: (k, 0))

    return pl.pallas_call(
        gate_kernel,
        grid=(tokens // PIECE,),
        in_specs=[
            piece(GROUP),
            piece(128),
            piece(N),
            whole((N, GROUP)),
            piece(GROUP),
            whole((8, GROUP)),
        ],
        out_specs=[piece(GROUP), piece(GROUP), piece(128)],
        out_shape=[
            jax.ShapeDtypeStruct((tokens, GROUP), f32),
            jax.ShapeDtypeStruct((tokens, GROUP), bf16),
            jax.ShapeDtypeStruct((tokens, 128), f32),
        ],
        compiler_params=pltpu.CompilerParams(vmem_limit_bytes=VMEM),
        cost_estimate=pl.CostEstimate(
            flops=110_000_000, bytes_accessed=6_500_000, transcendentals=400_000
        ),
        name="gate_out",
    )(mixed, run, query, entering, gate, gain)


def gate_back_kernel(
    grad, gate, mixed, scale, run, query, gain, decay, grad_scan, grad_gate, normed, packed, state
):
    k = pl.program_id(0)

    @pl.when(k == 0)
    def _():
        state[...] = jnp.zeros_like(state)

    grown = jnp.exp(run[...])
    queries_t = query[...].astype(f32).T.astype(bf16)
    first = lanes((PIECE, 128)) < 64
    s_out, mean = scale[:, 0:1], scale[:, 1:2]
    row16 = rows((16, 128))
    for j in range(PAIRS):
        cols = slice(128 * j, 128 * j + 128)
        pre = gate[:, cols]
        sig = jax.nn.sigmoid(pre)
        out = mixed[:, cols].astype(bf16).astype(f32)
        unit = out * (pre * sig) * s_out
        gain_j = gain[0:1, cols]
        gated = s_out * (grad[:, cols] * gain_j - unit * mean)
        scan = (gated * (pre * sig)).astype(bf16)
        grad_scan[:, cols] = scan
        grad_gate[:, cols] = (gated * out * sig * (1.0 + pre * (1.0 - sig))).astype(bf16)
        normed[:, cols] = (unit * gain_j).astype(bf16)
        total = state[:, cols] + dot(queries_t, spread(grown, j, first) * scan.astype(f32))
        state[:, cols] = total
        packed[0:N, cols] = total.astype(bf16)
        fall = jnp.broadcast_to(decay[0:1, cols], (16, 128))
        high = fall.astype(bf16).astype(f32)
        packed[N : N + 16, cols] = jnp.where(
            row16 == 0, high, jnp.where(row16 == 1, fall - high, 0.0)
        ).astype(bf16)


def gate_back(grad, gate, mixed, scale, run, query, gain, decay):
    tokens = mixed.shape[0]

    def whole(shape):
        return pl.BlockSpec(shape, lambda k: (0, 0))

    def piece(width):
        return pl.BlockSpec((PIECE, width), lambda k: (k, 0))

    return pl.pallas_call(
        gate_back_kernel,
        grid=(tokens // PIECE,),
        in_specs=[
            piece(GROUP),
            piece(GROUP),
            piece(GROUP),
            piece(128),
            piece(128),
            piece(N),
            whole((8, GROUP)),
            whole((8, GROUP)),
        ],
        out_specs=[piece(GROUP), piece(GROUP), piece(GROUP), whole((N + 16, GROUP))],
        out_shape=[
            jax.ShapeDtypeStruct((tokens, GROUP), bf16),
            jax.ShapeDtypeStruct((tokens, GROUP), bf16),
            jax.ShapeDtypeStruct((tokens, GROUP), bf16),
            jax.ShapeDtypeStruct((N + 16, GROUP), bf16),
        ],
        scratch_shapes=[pltpu.VMEM((N, GROUP), f32)],
        compiler_params=pltpu.CompilerParams(vmem_limit_bytes=VMEM),
        cost_estimate=pl.CostEstimate(
            flops=120_000_000, bytes_accessed=8_000_000, transcendentals=400_000
        ),
        name="gate_back",
    )(grad, gate, mixed, scale, run, query, gain, decay)


def scan_back_kernel(
    place, conv_in, pre_in, step, run, grad, mixed, starts, last, entering, leaving, rim, taps, hp,
    skip, grad_in, tail, grad_step, rim_grad, grad_taps, grad_hp, act, delta, state, after, skip_sum
):
    k = pl.program_id(0)
    count = pl.num_programs(0)
    first = lanes((PIECE, 128)) < 64
    first_row = lanes((1, 128)) < 64
    raw, sizes, log_decay = step_parts(step[...], hp[...])
    running = run[...]
    start = running[0:1] - log_decay[0:1]
    end = running[PIECE - 1 : PIECE]
    from_start = jnp.exp(running - start)
    to_end = jnp.exp(end - running)
    whole = jnp.exp(end - start)
    before_all = jnp.exp(start)
    until_end = jnp.exp(end)

    @pl.when(k == 0)
    def _():
        delta[PIECE : PIECE + 8] = jnp.zeros((8, ACT), f32)
        grad_taps[...] = jnp.zeros_like(grad_taps)
        grad_hp[...] = jnp.zeros_like(grad_hp)
        skip_sum[...] = jnp.zeros_like(skip_sum)
        for j in range(PAIRS):
            cols = slice(128 * j, 128 * j + 128)
            state[:, cols] = leaving[:, cols]
            after[:, cols] = spread(until_end, j, first_row) * entering[:, cols] + last[:, cols]

    @pl.when(k > 0)
    def _():
        delta[PIECE : PIECE + 8] = delta[0:8]

    for j in range(ACT // 128):
        cols = slice(128 * j, 128 * j + 128)
        pre = pre_in[:, cols]
        act[:, cols] = pre * jax.nn.sigmoid(pre)

    upper = rows((PIECE, PIECE)) <= lanes((PIECE, PIECE))
    keys = act[:, GROUP : GROUP + N].astype(bf16)
    queries32 = act[:, GROUP + N :]
    queries = queries32.astype(bf16)
    queries_t = queries32.T.astype(bf16)
    affinity = jnp.where(upper, dot_nt(keys, queries), 0.0)
    running_t = running.T
    grad_affinity = jnp.zeros((PIECE, PIECE), f32)
    grad_keys = jnp.zeros((PIECE, N), f32)
    grad_queries = jnp.zeros((PIECE, N), f32)
    inner_sum = jnp.zeros((PIECE, 128), f32)
    outer_sum = jnp.zeros((PIECE, 128), f32)
    bound = jnp.zeros((8, 128), f32)
    for j in range(PAIRS):
        cols = slice(128 * j, 128 * j + 128)
        x = act[:, cols]
        sizes_j = spread(sizes, j, first)
        scaled = x * sizes_j
        dm = grad[:, cols]
        dm32 = dm.astype(f32)
        to_end_j = spread(to_end, j, first)
        back = state[:, cols]
        z = to_end_j * dot(keys, back)
        for side in range(2):
            h = 2 * j + side
            half = first if side == 0 else ~first
            gap = jnp.exp(jnp.minimum(running_t[h : h + 1, :] - running[:, h : h + 1], 0.0))
            mine = jnp.where(half, dm32, 0.0)
            z = z + dot(gap * affinity, mine)
            grad_affinity = grad_affinity + gap * dot_nt(jnp.where(half, scaled, 0.0), dm)
        skip_j = skip[0:1, cols]
        delta[0:PIECE, cols] = sizes_j * z + skip_j * dm32
        skip_sum[0:1, cols] += jnp.sum(dm32 * x, axis=0, keepdims=True)
        heads = (lanes((128, 128)) == 2 * j + (rows((128, 128)) >= 64)).astype(bf16)
        inner_sum = inner_sum + dot_split(x * z, heads)
        outer_sum = outer_sum + dot_split(dm32 * (mixed[:, cols] - skip_j * x), heads)
        after_j = after[:, cols]
        inside = jnp.sum(back * after_j, axis=0, keepdims=True)
        bound = bound + dot_split(jnp.broadcast_to(inside, (8, 128)), heads)
        before = spread(before_all, j, first_row) * entering[:, cols] + starts[0, :, cols]
        after[:, cols] = before
        weighted = spread(from_start, j, first) * dm32
        grad_queries = grad_queries + dot_nt(weighted, before)
        grad_keys = grad_keys + dot_nt(scaled * to_end_j, back)
        state[:, cols] = spread(whole, j, first_row) * back + dot(queries_t, weighted)
    grad_affinity = jnp.where(upper, grad_affinity, 0.0)
    delta[0:PIECE, GROUP : GROUP + N] = grad_keys + dot(grad_affinity, queries)
    delta[0:PIECE, GROUP + N :] = grad_queries + dot(grad_affinity.T, keys)

    flow = outer_sum - sizes * inner_sum
    grad_log = bound[0:1] + jnp.dot(
        upper.astype(f32), flow, precision=HIGHEST, preferred_element_type=f32
    )
    rate = jnp.exp(hp[1:2])
    live = lanes((PIECE, 128)) < HEADS
    grad_raw = jnp.where(live, (inner_sum - rate * grad_log) * jax.nn.sigmoid(raw), 0.0)
    grad_step[...] = grad_raw.astype(bf16)
    grad_hp[0:1] += jnp.sum(grad_raw, axis=0, keepdims=True)
    grad_hp[1:2] += jnp.sum(jnp.where(live, grad_log * log_decay, 0.0), axis=0, keepdims=True)

    for j in range(ACT // 128):
        cols = slice(128 * j, 128 * j + 128)
        pre = pre_in[:, cols]
        sig = jax.nn.sigmoid(pre)
        grown = delta[0:PIECE, cols] * sig * (1.0 + pre * (1.0 - sig))
        delta[0:PIECE, cols] = grown
        grad_taps[4:5, cols] += jnp.sum(grown, axis=0, keepdims=True)
        taken = conv_in[:, cols].astype(f32)
        total = jnp.zeros((PIECE, 128), f32)
        for t in range(4):
            moved = delta[3 - t : 3 - t + PIECE, cols]
            total = total + taps[t : t + 1, cols] * moved
            grad_taps[t : t + 1, cols] += jnp.sum(taken * moved, axis=0, keepdims=True)
        grad_in[:, cols] = total.astype(bf16)

        @pl.when(k == 0)
        def _():
            tail[:, cols] = total[PIECE - 8 :]

    @pl.when(k == count - 1)
    def _():
        for j in range(PAIRS):
            cols = slice(128 * j, 128 * j + 128)
            heads = (lanes((128, 128)) == 2 * j + (rows((128, 128)) >= 64)).astype(bf16)
            sums = dot_split(jnp.broadcast_to(skip_sum[0:1, cols], (8, 128)), heads)
            grad_hp[2:3] += sums[0:1]
        for j in range(ACT // 128):
            cols = slice(128 * j, 128 * j + 128)
            edge = jnp.concatenate([jnp.zeros((8, 128), f32), delta[0:8, cols]], axis=0)
            taken = rim[:, cols].astype(f32)
            total = jnp.zeros((8, 128), f32)
            for t in range(4):
                moved = edge[3 - t : 11 - t]
                total = total + taps[t : t + 1, cols] * moved
                grad_taps[t : t + 1, cols] += jnp.sum(taken * moved, axis=0, keepdims=True)
            rim_grad[:, cols] = total


def scan_back(
    place, conv_in, pre, step, run, grad, mixed, starts, last, entering, leaving, rim, taps, hp, skip
):
    tokens = conv_in.shape[0]
    count = tokens // PIECE

    def whole(shape):
        return pl.BlockSpec(shape, lambda k, place: (0,) * len(shape))

    def piece(width):
        return pl.BlockSpec((PIECE, width), lambda k, place: (turned(count - 1 - k, place), 0))

    return pl.pallas_call(
        scan_back_kernel,
        grid_spec=pltpu.PrefetchScalarGridSpec(
            num_scalar_prefetch=1,
            grid=(count,),
            in_specs=[
                piece(ACT),
                piece(ACT),
                piece(128),
                piece(128),
                piece(GROUP),
                piece(GROUP),
                pl.BlockSpec((1, N, GROUP), lambda k, place: (count - 1 - k, 0, 0)),
                whole((N, GROUP)),
                whole((N, GROUP)),
                whole((N, GROUP)),
                whole((8, ACT)),
                whole((8, ACT)),
                whole((8, 128)),
                whole((8, GROUP)),
            ],
            out_specs=[
                piece(ACT),
                whole((8, ACT)),
                piece(128),
                whole((8, ACT)),
                whole((8, ACT)),
                whole((8, 128)),
            ],
            scratch_shapes=[
                pltpu.VMEM((PIECE, ACT), f32),
                pltpu.VMEM((PIECE + 8, ACT), f32),
                pltpu.VMEM((N, GROUP), f32),
                pltpu.VMEM((N, GROUP), f32),
                pltpu.VMEM((8, GROUP), f32),
            ],
        ),
        out_shape=[
            jax.ShapeDtypeStruct((tokens, ACT), bf16),
            jax.ShapeDtypeStruct((8, ACT), f32),
            jax.ShapeDtypeStruct((tokens, 128), bf16),
            jax.ShapeDtypeStruct((8, ACT), f32),
            jax.ShapeDtypeStruct((8, ACT), f32),
            jax.ShapeDtypeStruct((8, 128), f32),
        ],
        compiler_params=pltpu.CompilerParams(vmem_limit_bytes=VMEM),
        cost_estimate=pl.CostEstimate(
            flops=2_000_000_000, bytes_accessed=9_000_000, transcendentals=2_500_000
        ),
        name="scan_back",
    )(place, conv_in, pre, step, run, grad, mixed, starts, last, entering, leaving, rim, taps, hp,
      skip)


def pick(core, first, second):
    return jnp.where(core == 0, first, second)


def spread_weights(core, head, gate_inner, shared_bc, step_proj, input_gain, small):
    gate = gate_inner[:, :DI].reshape(24, 4, 2, HALF)
    inner = gate_inner[:, DI:].reshape(24, 4, 2, HALF)
    heads = step_proj.reshape(24, 4, HEADS)
    slots = []
    for g in range(4):
        own = heads[:, g]
        slots.append(
            jnp.concatenate(
                [own, own[:, :6], input_gain[:, None], small, jnp.zeros((24, EXTRA - 32), bf16)],
                axis=1,
            )
        )
    halves = []
    for q in range(2):
        pieces = [
            jnp.concatenate(
                [inner[:, g, q], shared_bc if q == 0 else slots[g], gate[:, g, q]], axis=1
            )
            for g in range(4)
        ]
        halves.append(jnp.stack(pieces))
    kept = pick(core, halves[0], halves[1])
    got = swap(pick(core, halves[1], halves[0]))
    layers = [pick(core, kept, got), pick(core, got, kept)]
    return [exchange_head(values, head).reshape(96, HALF + EXTRA + HALF) for values in layers]


def out_pairs():
    pairs = []
    for layer in range(2):
        for z in range(4):
            for y in range(4):
                for x in range(4):
                    source = (layer * 16 + z * 4 + y) * 4 + x
                    place = layer * 8 + (y % 2) * 4 + x
                    pairs.append((source, ((y // 2) * 16 + place) * 4 + z))
    return pairs


def out_back_pairs(layer, part):
    pairs = []
    for core in range(2):
        for j in range(8):
            for group in range(4):
                source = (core * 16 + 2 * j + part) * 4 + group
                target = (layer * 16 + group * 4 + 2 * core + j // 4) * 4 + j % 4
                pairs.append((source, target))
    return pairs


EVERY = ("section", "seq", "head")


def gather_seq(a):
    return lax.all_gather(a, "seq", axis=0, tiled=True)


def layer_params(core, head, slot, step_bias, decay_log, skip_gain):
    small = slot[:, SMALL_AT : SMALL_AT + SMALL].reshape(64, 24 * SMALL).astype(f32)
    conv = small[:, :208].reshape(64, 4, 52).transpose(1, 0, 2).reshape(4, DI + 2 * N)
    bias = small[:, 208:260].reshape(1, DI + 2 * N)
    gain = small[:, 260:308].reshape(1, DI)
    taps = jnp.concatenate([conv, bias, jnp.zeros((3, DI + 2 * N), f32)], axis=0)

    def grouped(values, width):
        own = lax.dynamic_slice_in_dim(values, (2 * head + core) * width, width, 1)
        other = lax.dynamic_slice_in_dim(values, (2 * head + 1 - core) * width, width, 1)
        return [own, other]

    taps = jnp.concatenate(grouped(taps, HALF) + [taps[:, DI:]], axis=1)
    gain = jnp.broadcast_to(jnp.concatenate(grouped(gain, HALF), axis=1), (8, GROUP))
    per_head = jnp.concatenate([step_bias, decay_log, skip_gain], axis=0)
    per_head = jnp.concatenate(grouped(per_head, 6), axis=1)
    hp = jnp.pad(per_head, ((0, 5), (0, 128 - HEADS)))
    skip = jnp.broadcast_to(jnp.repeat(per_head[2:3], 64, axis=1), (8, GROUP))
    return dict(taps=taps, gain=gain, hp=hp, skip=skip)


def rms_scale(values):
    return lax.rsqrt(jnp.mean(values * values, axis=-1, keepdims=True) + epsilon)


def piece_rows(values, k):
    return values[PIECE * k : PIECE * (k + 1)]


def layer_forward(core, head, feed, normed, weights):
    place = head.reshape(1)
    own = dot(normed, weights["x_own"]).astype(bf16)
    other = dot(normed, weights["x_other"]).astype(bf16)
    shared = pick(core, own[:, HALF:], other[:, HALF:])
    conv_in = jnp.concatenate([own[:, :HALF], other[:, :HALF], shared], axis=1)
    slot = pick(core, other[:, HALF : HALF + 128], own[:, HALF + 6 : HALF + 134]).astype(f32)
    last_row = PIECE * lax.rem(7 - head, 4) + PIECE - 8
    rim = lax.ppermute(
        lax.dynamic_slice_in_dim(conv_in, last_row, 8, 0), "seq", [(i, i + 1) for i in range(15)]
    )
    pre, mixed0, query, run, starts, last, packed = scan_local(
        place, conv_in, slot, rim, weights["taps"], weights["hp"], weights["skip"]
    )
    entering = carried(packed, -1)
    gate = jnp.concatenate([dot(normed, weights["g_own"]), dot(normed, weights["g_other"])], axis=1)
    mixed, normed_out, square = gate_out(mixed0, run, query, entering, gate, weights["gain"])
    square = square[:, 0].reshape(4, PIECE)
    total = square
    for k in (2, 1, 3):
        total = total + from_head(jnp.roll(square, k, axis=0), k)
    s_out = lax.rsqrt(total / DI + epsilon)
    parts = {}
    for k in (2, 1, 3, 0):
        piece = piece_rows(normed_out, k)
        parts[k] = dot(piece[:, :HALF], weights["o_own"]) + dot(piece[:, HALF:], weights["o_other"])
    branch = s_out[0][:, None] * scatter_head(parts)
    result = (feed.astype(f32) + branch).astype(bf16)
    kept = dict(
        feed=feed, normed=normed, gate=gate, conv_in=conv_in, rim=rim, step=slot, pre=pre,
        mixed=mixed, query=query, run=run, starts=starts, last=last, entering=entering,
        s_out=s_out, branch=branch, packed=packed,
    )
    return result, kept


def layer_backward(core, head, incoming, gathered, kept, weights):
    place = head.reshape(1)
    grad_new = incoming.astype(f32)
    mean_own = jnp.sum(kept["branch"] * grad_new, axis=1) / DI
    mean = jnp.stack(gather_head(mean_own))
    scale = jnp.stack([kept["s_out"].reshape(-1), mean.reshape(-1)], axis=1)
    scale = jnp.pad(scale, ((0, 0), (0, 126)))
    grad_normed_out = jnp.concatenate(
        [dot_nt(gathered, weights["o_own"]), dot_nt(gathered, weights["o_other"])], axis=1
    )
    decay = jnp.broadcast_to(
        kept["packed"][N : N + 1].astype(f32) + kept["packed"][N + 1 : N + 2].astype(f32),
        (8, GROUP),
    )
    grad_scan, grad_gate, normed_out, packed = gate_back(
        grad_normed_out, kept["gate"], kept["mixed"], scale, kept["run"], kept["query"],
        weights["gain"], decay,
    )
    leaving = carried(packed, 1)
    grad_out = (dot_tn(normed_out[:, :HALF], gathered), dot_tn(normed_out[:, HALF:], gathered))
    normed = kept["normed"]
    grad_g = (dot_tn(normed, grad_gate[:, :HALF]), dot_tn(normed, grad_gate[:, HALF:]))
    grad_conv, tail, grad_step, rim_grad, grad_taps, grad_hp = scan_back(
        place, kept["conv_in"], kept["pre"], kept["step"], kept["run"], grad_scan, kept["mixed"],
        kept["starts"], kept["last"], kept["entering"], leaving, kept["rim"], weights["taps"],
        weights["hp"], weights["skip"],
    )
    from_next = lax.ppermute(rim_grad, "seq", [(i + 1, i) for i in range(15)])
    last_row = PIECE * lax.rem(7 - head, 4) + PIECE - 8
    grad_conv = lax.dynamic_update_slice_in_dim(
        grad_conv, (tail + from_next).astype(bf16), last_row, 0
    )
    shared = grad_conv[:, GROUP:]
    first, second = grad_step[:, :6], grad_step[:, 6:12]
    step = jnp.concatenate(
        [
            pick(core, first, second),
            pick(core, second, first),
            jnp.zeros((grad_step.shape[0], EXTRA - HEADS), bf16),
        ],
        axis=1,
    )
    use_own = jnp.concatenate([grad_conv[:, :HALF], pick(core, shared, step)], axis=1)
    use_other = jnp.concatenate([grad_conv[:, HALF:GROUP], pick(core, step, shared)], axis=1)
    parts = {}
    for k in (2, 1, 3, 0):
        parts[k] = (
            dot_nt(piece_rows(use_own, k), weights["x_own"])
            + dot_nt(piece_rows(use_other, k), weights["x_other"])
            + dot_nt(piece_rows(grad_gate, k)[:, :HALF], weights["g_own"])
            + dot_nt(piece_rows(grad_gate, k)[:, HALF:], weights["g_other"])
        )
    grad_normed = scatter_head(parts)
    grad_x = (dot_tn(normed, use_own), dot_tn(normed, use_other))
    feed = kept["feed"].astype(f32)
    s_in = rms_scale(feed)
    unit = feed * s_in
    grad_unit = grad_normed * weights["input_gain"]
    grad_feed = grad_new + s_in * (
        grad_unit - unit * jnp.mean(unit * grad_unit, axis=-1, keepdims=True)
    )
    return grad_feed.astype(bf16), (grad_x, grad_g, grad_out, grad_taps, grad_hp)


def small_columns(core, head, grad_taps, grad_hp):
    taps = grad_taps[:5]
    full = jnp.zeros((5, DI), f32)
    full = lax.dynamic_update_slice_in_dim(full, taps[:, :HALF], (2 * head + core) * HALF, 1)
    full = lax.dynamic_update_slice_in_dim(
        full, taps[:, HALF:GROUP], (2 * head + 1 - core) * HALF, 1
    )
    full = jnp.concatenate([full, taps[:, GROUP:]], axis=1)
    full = full.reshape(5, 64, 52).transpose(1, 0, 2).reshape(64, 260)
    first, second = grad_hp[:3, :6], grad_hp[:3, 6:HEADS]
    sums = jnp.concatenate([pick(core, first, second), pick(core, second, first)], axis=1)
    sums = jnp.broadcast_to(sums.reshape(1, 36), (64, 36))
    return jnp.concatenate([full, sums, jnp.zeros((64, 16), f32)], axis=1).reshape(D, SMALL)


def summed(own, other):
    return own + swap(other.astype(bf16)).astype(f32)


def scatter_seq(a):
    return lax.psum_scatter(a, "seq", scatter_dimension=0, tiled=True)


def reduce_layer(core, head, layer, grads):
    grad_x, grad_g, grad_out, grad_taps, grad_hp = grads
    out = scatter_seq(summed(*grad_out))
    gate = scatter_seq(summed(*grad_g))
    small = small_columns(core, head, grad_taps, grad_hp)
    small = jnp.pad(small, ((0, 0), (HALF + SMALL_AT, EXTRA - SMALL_AT - SMALL)))
    own = grad_x[0] + jnp.where(core == 1, small, 0.0)
    other = grad_x[1] + jnp.where(core == 0, small, 0.0)
    x = scatter_seq(summed(own, other))
    both = jnp.concatenate([x, gate], axis=1).reshape(4, 24, HALF + EXTRA + HALF)
    mine = exchange_head(both, head)
    theirs = lax.ppermute(mine, "section", [(1 - layer, layer)])
    rows_out = [lax.ppermute(out, EVERY, out_back_pairs(layer, part)) for part in range(2)]
    return mine, theirs, rows_out


def per_device(
    tokens_in, cotangent, input_gain, gate_inner, shared_bc, step_proj, conv_weight, conv_bias,
    step_bias, decay_log, skip_gain, output_gain, out_proj
):
    core = lax.axis_index("section")
    head = lax.axis_index("head")
    tokens = lax.dynamic_index_in_dim(tokens_in, core, 0, False)
    grad_top = lax.dynamic_index_in_dim(cotangent, core, 0, False)

    small = jnp.concatenate(
        [conv_weight[0].reshape(208), conv_bias[0], output_gain[0], jnp.zeros((4,), bf16)]
    ).reshape(24, SMALL)
    pieces = spread_weights(
        core, head, gate_inner[0], shared_bc[0], step_proj[0], input_gain[0], small
    )
    out_piece = lax.ppermute(out_proj[0], EVERY, out_pairs())
    per_head = jnp.concatenate([step_bias, decay_log, skip_gain], axis=0)
    other_head = swap(per_head)
    head_values = [pick(core, per_head, other_head), pick(core, other_head, per_head)]

    feed_all = jnp.concatenate(gather_head(tokens), axis=0)
    weights = [{}, {}]
    for layer in range(2):
        own = gather_seq(pieces[layer][:, : HALF + EXTRA])
        weights[layer].update(x_own=own, x_other=swap(own))
        gate = gather_seq(pieces[layer][:, HALF + EXTRA :])
        weights[layer].update(g_own=gate, g_other=swap(gate))
        if layer == 0:
            out = gather_seq(out_piece)
            out_other = swap(out)
        weights[layer].update(
            o_own=out[HALF * layer : HALF * (layer + 1)],
            o_other=out_other[HALF * layer : HALF * (layer + 1)],
        )
        slot = pick(core, weights[layer]["x_other"], own)[:, HALF : HALF + 128]
        values = head_values[layer]
        weights[layer].update(
            layer_params(core, head, slot, values[0:1], values[1:2], values[2:3])
        )
        weights[layer]["input_gain"] = slot[:, 18].astype(f32)[None, :]

    def normalised(feed, gain):
        values = feed.astype(f32)
        return (values * rms_scale(values) * gain).astype(bf16)

    normed = normalised(feed_all, weights[0]["input_gain"])
    hidden, kept0 = layer_forward(core, head, tokens, normed, weights[0])
    normed_own = normalised(hidden, weights[1]["input_gain"])
    normed = jnp.concatenate(gather_head(normed_own), axis=0)
    result, kept1 = layer_forward(core, head, hidden, normed, weights[1])
    got = swap(pick(core, result, hidden))
    layer_out = jnp.stack([pick(core, hidden, got), pick(core, got, result)])

    grad_all = jnp.concatenate(gather_head(grad_top), axis=0)
    grad_hidden, grads1 = layer_backward(core, head, grad_top, grad_all, kept1, weights[1])
    grad_all = jnp.concatenate(gather_head(grad_hidden), axis=0)
    mine1, theirs1, out1 = reduce_layer(core, head, 1, grads1)
    grad_feed, grads0 = layer_backward(core, head, grad_hidden, grad_all, kept0, weights[0])
    mine0, theirs0, out0 = reduce_layer(core, head, 0, grads0)
    got = swap(pick(core, grad_hidden, grad_feed))
    grad_in = jnp.stack([pick(core, grad_feed, got), pick(core, got, grad_hidden)])

    mine = pick(core, mine0, mine1)
    theirs = theirs0 + theirs1
    low, high = pick(core, mine, theirs), pick(core, theirs, mine)
    columns = []
    for start in (HALF + EXTRA, 0):
        for g in range(4):
            for half in (low, high):
                columns.append(half[g, :, start : start + HALF])
    grad_gate_inner = jnp.concatenate(columns, axis=1)
    grad_shared = jnp.sum(low[:, :, HALF : HALF + EXTRA], axis=0)
    slot = high[:, :, HALF : HALF + 128]
    grad_step = jnp.concatenate([slot[g, :, :HEADS] for g in range(4)], axis=1)
    small = slot[:, :, SMALL_AT : SMALL_AT + SMALL].reshape(4, 24 * SMALL)
    taps = jnp.sum(small[:, :260], axis=0)
    sums = small[:, 260:296].reshape(4, 3, HEADS).transpose(1, 0, 2).reshape(3, 48)
    grad_out = jnp.concatenate([out0[0] + out1[0], out0[1] + out1[1]], axis=0)
    grad_output_gain = jnp.sum(grad_out * out_proj[0].astype(f32), axis=1) / output_gain[0].astype(
        f32
    )
    grad_input_gain = (
        jnp.sum(grad_gate_inner * gate_inner[0].astype(f32), axis=1)
        + jnp.sum(grad_shared * shared_bc[0].astype(f32), axis=1)
        + jnp.sum(grad_step * step_proj[0].astype(f32), axis=1)
    ) / input_gain[0].astype(f32)
    return (
        layer_out[None],
        grad_in[None],
        grad_input_gain[None],
        grad_gate_inner[None],
        grad_shared[None],
        grad_step[None],
        taps[:208].reshape(1, 4, 52),
        taps[208:260][None],
        sums[0:1],
        sums[1:2],
        sums[2:3],
        grad_output_gain[None],
        grad_out[None],
    )


def solution(mesh):
    both = ("seq", "head")
    return jax.shard_map(
        per_device,
        mesh=mesh,
        in_specs=(
            P(None, both, None),
            P(None, both, None),
            P("section", both),
            P("section", both, None),
            P("section", both, None),
            P("section", both, None),
            P("section", None, both),
            P("section", both),
            P("section", None),
            P("section", None),
            P("section", None),
            P("section", both),
            P("section", both, None),
        ),
        out_specs=(
            P("section", None, both, None),
            P("section", None, both, None),
            P("section", both),
            P("section", both, None),
            P("section", both, None),
            P("section", both, None),
            P("section", None, both),
            P("section", both),
            P("section", None),
            P("section", None),
            P("section", None),
            P("section", both),
            P("section", both, None),
        ),
        check_vma=False,
    )
```

```python
import jax
import jax.numpy as jnp
from jax import lax
from jax.experimental import pallas as pl
from jax.experimental.pallas import tpu as pltpu
from jax.sharding import PartitionSpec as P

bf16 = jnp.bfloat16
f32 = jnp.float32
HIGHEST = lax.Precision.HIGHEST

D = 1536
DI = 3072
N = 128
GROUP = 768
HALF = 384
HEADS = 12
PIECE = 128
PAIRS = 6
EXTRA = 256
ACT = GROUP + 2 * N
SMALL_AT, SMALL = 19, 13
WIDE = HALF + EXTRA + HALF
VMEM = 24 * 1024 * 1024
epsilon = 1e-05


def from_head(a, k):
    return lax.ppermute(a, "head", [(i, (i - k) % 4) for i in range(4)])


def from_seq(a, dz, dy, wrap):
    pairs = []
    for z in range(4):
        for y in range(4):
            sz, sy = z + dz, y + dy
            if wrap:
                sz, sy = sz % 4, sy % 4
            if 0 <= sz < 4 and 0 <= sy < 4:
                pairs.append((sz * 4 + sy, z * 4 + y))
    return lax.ppermute(a, "seq", pairs)


def swap(a):
    return lax.ppermute(a, "section", [(0, 1), (1, 0)])


def gather_head(a):
    one, three = from_head(a, 1), from_head(a, 3)
    two = from_head(a, 2)
    return [a, one, two, three]


def scatter_head(parts):
    one, three = from_head(parts[1], 3), from_head(parts[3], 1)
    two = from_head(parts[2], 2)
    return [parts[0], one, two, three]


def exchange_head(parts, place):
    got = [lax.dynamic_index_in_dim(parts, place, 0, False)]
    for k in (1, 3, 2):
        sent = lax.dynamic_index_in_dim(parts, lax.rem(place + 4 - k, 4), 0, False)
        got.append(from_head(sent, k))
    got = [got[0], got[1], got[3], got[2]]
    twice = jnp.stack(got + got)
    return lax.dynamic_slice_in_dim(twice, lax.rem(4 - place, 4), 4, 0)


def unpack_state(a):
    decay = a[N : N + 1].astype(f32) + a[N + 1 : N + 2].astype(f32)
    return decay, a[:N].astype(f32)


def join(earlier, later):
    return earlier[0] * later[0], earlier[1] * later[0] + later[1]


def carried(packed, sign):
    seq = lax.axis_index("seq")
    y = lax.rem(seq, 4)
    ahead = y if sign < 0 else 3 - y
    near = {k: unpack_state(from_seq(packed, 0, sign * k, True)) for k in (1, 3, 2)}
    own = unpack_state(packed)
    before = (jnp.ones_like(own[0]), jnp.zeros_like(own[1]))
    after = own
    for k in (3, 2, 1):
        decay, state = near[k]
        use = k <= ahead
        before = join(before, (jnp.where(use, decay, 1.0), jnp.where(use, state, 0.0)))
        after = join(after, (jnp.where(use, 1.0, decay), jnp.where(use, 0.0, state)))
    whole = join(before, after)
    packed_whole = pack_state(whole[0], whole[1])
    far = {k: unpack_state(from_seq(packed_whole, sign * k, 0, False)) for k in (1, 3, 2)}
    total = jnp.zeros_like(own[1])
    for k in (3, 2, 1):
        decay, state = far[k]
        total = total * decay + state
    return total * before[0] + before[1]


def pack_state(decay, state):
    high = decay.astype(bf16)
    low = (decay - high.astype(f32)).astype(bf16)
    fill = jnp.zeros((14, state.shape[1]), bf16)
    return jnp.concatenate([state.astype(bf16), high, low, fill], axis=0)


def dot(a, b):
    return jnp.dot(a.astype(bf16), b.astype(bf16), preferred_element_type=f32)


def dot_nt(a, b):
    return lax.dot_general(
        a.astype(bf16), b.astype(bf16), (((1,), (1,)), ((), ())), preferred_element_type=f32
    )


def dot_tn(a, b):
    return lax.dot_general(
        a.astype(bf16), b.astype(bf16), (((0,), (0,)), ((), ())), preferred_element_type=f32
    )


def dot_split(a, b):
    high = a.astype(bf16)
    low = (a - high.astype(f32)).astype(bf16)
    return dot(high, b) + dot(low, b)


def lanes(shape):
    return lax.broadcasted_iota(jnp.int32, shape, 1)


def rows(shape):
    return lax.broadcasted_iota(jnp.int32, shape, 0)


def spread(values, j, first):
    return jnp.where(first, values[:, 2 * j : 2 * j + 1], values[:, 2 * j + 1 : 2 * j + 2])


def step_parts(step, hp):
    raw = step + hp[0:1]
    live = lanes(raw.shape) < HEADS
    sizes = jnp.maximum(raw, 0.0) + jnp.log1p(jnp.exp(-jnp.abs(raw)))
    sizes = jnp.where(live, sizes, 0.0)
    return raw, sizes, -jnp.exp(hp[1:2]) * sizes


def scan_kernel(
    place, conv_in, step, rim, taps, hp, skip, pre_out, mixed, query, run, starts, last, packed,
    padded, act, state, carry
):
    k = pl.program_id(0)

    @pl.when(k == 0)
    def _():
        state[...] = jnp.zeros_like(state)
        carry[...] = jnp.zeros_like(carry)
        padded[0:8] = rim[...].astype(f32)

    @pl.when(k > 0)
    def _():
        padded[0:8] = padded[PIECE : PIECE + 8]

    padded[8 : PIECE + 8] = conv_in[...].astype(f32)
    for j in range(ACT // 128):
        cols = slice(128 * j, 128 * j + 128)
        pre = taps[4:5, cols] + taps[0:1, cols] * padded[5 : PIECE + 5, cols]
        for t in range(1, 4):
            pre = pre + taps[t : t + 1, cols] * padded[5 + t : PIECE + 5 + t, cols]
        pre_out[:, cols] = pre
        act[:, cols] = pre * jax.nn.sigmoid(pre)
    raw, sizes, log_decay = step_parts(step[...], hp[...])
    lower = rows((PIECE, PIECE)) >= lanes((PIECE, PIECE))
    start = carry[0:1]
    running = start + jnp.dot(
        lower.astype(f32), log_decay, precision=HIGHEST, preferred_element_type=f32
    )
    run[...] = running
    end = running[PIECE - 1 : PIECE]
    carry[...] = jnp.broadcast_to(end, carry.shape)
    running_t = running.T
    keys = act[:, GROUP : GROUP + N]
    queries = act[:, GROUP + N :].astype(bf16)
    query[...] = queries
    affinity = jnp.where(lower, dot_nt(queries, keys), 0.0)
    keys_t = keys.T.astype(bf16)
    from_start = jnp.exp(running - start)
    to_end = jnp.exp(end - running)
    whole = jnp.exp(end - start)
    total = jnp.exp(end)
    first = lanes((PIECE, 128)) < 64
    first_row = lanes((1, 128)) < 64
    row16 = rows((16, 128))
    for j in range(PAIRS):
        cols = slice(128 * j, 128 * j + 128)
        x = act[:, cols]
        scaled = x * spread(sizes, j, first)
        y = jnp.zeros((PIECE, 128), f32)
        for side in range(2):
            h = 2 * j + side
            gap = jnp.exp(jnp.minimum(running[:, h : h + 1] - running_t[h : h + 1, :], 0.0))
            mine = jnp.where(first if side == 0 else ~first, scaled, 0.0)
            y = y + dot(gap * affinity, mine)
        before = state[:, cols]
        starts[0, :, cols] = before
        y = y + spread(from_start, j, first) * dot(queries, before)
        mixed[:, cols] = y + skip[0:1, cols] * x
        after = spread(whole, j, first_row) * before + dot(
            keys_t, scaled * spread(to_end, j, first)
        )
        state[:, cols] = after
        last[:, cols] = after
        packed[0:N, cols] = after.astype(bf16)
        decay = jnp.broadcast_to(spread(total, j, first_row), (16, 128))
        high = decay.astype(bf16).astype(f32)
        packed[N : N + 16, cols] = jnp.where(
            row16 == 0, high, jnp.where(row16 == 1, decay - high, 0.0)
        ).astype(bf16)


def turned(k, place):
    return lax.rem(k + 4 - place[0], 4)


def scan_local(place, conv_in, step, rim, taps, hp, skip):
    tokens = conv_in.shape[0]

    def whole(shape):
        return pl.BlockSpec(shape, lambda k, place: (0,) * len(shape))

    def piece(width):
        return pl.BlockSpec((PIECE, width), lambda k, place: (turned(k, place), 0))

    return pl.pallas_call(
        scan_kernel,
        grid_spec=pltpu.PrefetchScalarGridSpec(
            num_scalar_prefetch=1,
            grid=(tokens // PIECE,),
            in_specs=[
                piece(ACT),
                piece(128),
                whole((8, ACT)),
                whole((8, ACT)),
                whole((8, 128)),
                whole((8, GROUP)),
            ],
            out_specs=[
                piece(ACT),
                piece(GROUP),
                piece(N),
                piece(128),
                pl.BlockSpec((1, N, GROUP), lambda k, place: (k, 0, 0)),
                whole((N, GROUP)),
                whole((N + 16, GROUP)),
            ],
            scratch_shapes=[
                pltpu.VMEM((PIECE + 8, ACT), f32),
                pltpu.VMEM((PIECE, ACT), f32),
                pltpu.VMEM((N, GROUP), f32),
                pltpu.VMEM((8, 128), f32),
            ],
        ),
        out_shape=[
            jax.ShapeDtypeStruct((tokens, ACT), f32),
            jax.ShapeDtypeStruct((tokens, GROUP), f32),
            jax.ShapeDtypeStruct((tokens, N), bf16),
            jax.ShapeDtypeStruct((tokens, 128), f32),
            jax.ShapeDtypeStruct((tokens // PIECE, N, GROUP), f32),
            jax.ShapeDtypeStruct((N, GROUP), f32),
            jax.ShapeDtypeStruct((N + 16, GROUP), bf16),
        ],
        compiler_params=pltpu.CompilerParams(vmem_limit_bytes=VMEM),
        cost_estimate=pl.CostEstimate(
            flops=1_000_000_000, bytes_accessed=8_000_000, transcendentals=1_500_000
        ),
        name="scan_local",
    )(place, conv_in, step, rim, taps, hp, skip)


def project_kernel(core, feed, gain, own, other, normed, conv_in, step, gate):
    values = feed[...].astype(f32)
    scale = lax.rsqrt(jnp.mean(values * values, axis=1, keepdims=True) + epsilon)
    low = (values * scale * gain[0:1]).astype(bf16)
    normed[...] = low
    mine = dot(low, own[...])
    theirs = dot(low, other[...])
    is_first = core[0] == 0
    edge = HALF + EXTRA
    conv_in[:, :HALF] = mine[:, :HALF].astype(bf16)
    conv_in[:, HALF:GROUP] = theirs[:, :HALF].astype(bf16)
    conv_in[:, GROUP:] = jnp.where(is_first, mine[:, HALF:edge], theirs[:, HALF:edge]).astype(bf16)
    slot = jnp.where(is_first, theirs[:, HALF : HALF + 128], mine[:, HALF + 128 : edge])
    step[...] = slot.astype(bf16).astype(f32)
    gate[:, :HALF] = mine[:, edge:]
    gate[:, HALF:] = theirs[:, edge:]


def project(core, feed, gain, own, other):
    tokens = feed.shape[0]

    def whole(shape):
        return pl.BlockSpec(shape, lambda k, core: (0, 0))

    def piece(width):
        return pl.BlockSpec((2 * PIECE, width), lambda k, core: (k, 0))

    return pl.pallas_call(
        project_kernel,
        grid_spec=pltpu.PrefetchScalarGridSpec(
            num_scalar_prefetch=1,
            grid=(tokens // (2 * PIECE),),
            in_specs=[piece(D), whole((8, D)), whole((D, WIDE)), whole((D, WIDE))],
            out_specs=[piece(D), piece(ACT), piece(128), piece(GROUP)],
        ),
        out_shape=[
            jax.ShapeDtypeStruct((tokens, D), bf16),
            jax.ShapeDtypeStruct((tokens, ACT), bf16),
            jax.ShapeDtypeStruct((tokens, 128), f32),
            jax.ShapeDtypeStruct((tokens, GROUP), f32),
        ],
        compiler_params=pltpu.CompilerParams(vmem_limit_bytes=VMEM),
        cost_estimate=pl.CostEstimate(
            flops=3_200_000_000, bytes_accessed=12_000_000, transcendentals=1000
        ),
        name="project",
    )(core, feed, gain, own, other)


def gate_kernel(
    mixed, run, query, entering, gate, gain, out_own, out_other, mixed_out, sent0, sent1, sent2, sent3
):
    k = pl.program_id(0)
    decay = jnp.exp(run[...])
    queries = query[...]
    first = lanes((PIECE, 128)) < 64
    total = jnp.zeros((PIECE, 1), f32)
    normed = []
    for j in range(PAIRS):
        cols = slice(128 * j, 128 * j + 128)
        y = mixed[:, cols] + spread(decay, j, first) * dot(queries, entering[:, cols])
        mixed_out[:, cols] = y
        pre = gate[:, cols]
        gated = y.astype(bf16).astype(f32) * (pre * jax.nn.sigmoid(pre))
        total = total + jnp.sum(gated * gated, axis=1, keepdims=True)
        normed.append((gated * gain[0:1, cols]).astype(bf16))
    part = dot(jnp.concatenate(normed[:3], axis=1), out_own[...])
    part = part + dot(jnp.concatenate(normed[3:], axis=1), out_other[...])
    lane = lanes((PIECE, 128))
    high = total.astype(bf16).astype(f32)
    split = jnp.where(lane == 0, high, jnp.where(lane == 1, total - high, 0.0))
    for index, sent in enumerate((sent0, sent1, sent2, sent3)):

        @pl.when(k == index)
        def _():
            sent[:, :D] = part.astype(sent.dtype)
            sent[:, D:] = split.astype(sent.dtype)


def gate_out(mixed, run, query, entering, gate, gain, out_own, out_other):
    tokens = mixed.shape[0]

    def whole(shape):
        return pl.BlockSpec(shape, lambda k: (0, 0))

    def piece(width):
        return pl.BlockSpec((PIECE, width), lambda k: (k, 0))

    return pl.pallas_call(
        gate_kernel,
        grid=(tokens // PIECE,),
        in_specs=[
            piece(GROUP),
            piece(128),
            piece(N),
            whole((N, GROUP)),
            piece(GROUP),
            whole((8, GROUP)),
            whole((HALF, D)),
            whole((HALF, D)),
        ],
        out_specs=[piece(GROUP)] + [whole((PIECE, D + 128))] * 4,
        out_shape=[jax.ShapeDtypeStruct((tokens, GROUP), f32)]
        + [jax.ShapeDtypeStruct((PIECE, D + 128), f32 if k == 0 else bf16) for k in range(4)],
        compiler_params=pltpu.CompilerParams(vmem_limit_bytes=VMEM),
        cost_estimate=pl.CostEstimate(
            flops=1_300_000_000, bytes_accessed=9_000_000, transcendentals=400_000
        ),
        name="gate_out",
    )(mixed, run, query, entering, gate, gain, out_own, out_other)


def gate_back_kernel(
    grad_new, out_own, out_other, gate, mixed, scale, run, query, gain, decay,
    grad_scan, grad_gate, normed, packed, state, product
):
    k = pl.program_id(0)

    @pl.when(k == 0)
    def _():
        state[...] = jnp.zeros_like(state)
        product[:, :HALF] = dot_nt(grad_new[...], out_own[...])
        product[:, HALF:] = dot_nt(grad_new[...], out_other[...])

    token = pl.ds(pl.multiple_of(k * PIECE, PIECE), PIECE)
    grown = jnp.exp(run[...])
    queries_t = query[...].astype(f32).T.astype(bf16)
    first = lanes((PIECE, 128)) < 64
    parts = scale[...].astype(f32)
    s_out, mean = parts[:, 0:1] + parts[:, 1:2], parts[:, 2:3] + parts[:, 3:4]
    row16 = rows((16, 128))
    for j in range(PAIRS):
        cols = slice(128 * j, 128 * j + 128)
        grad = product[token, cols]
        pre = gate[:, cols]
        sig = jax.nn.sigmoid(pre)
        out = mixed[:, cols].astype(bf16).astype(f32)
        unit = out * (pre * sig) * s_out
        gain_j = gain[0:1, cols]
        gated = s_out * (grad * gain_j - unit * mean)
        scan = (gated * (pre * sig)).astype(bf16)
        grad_scan[:, cols] = scan
        grad_gate[:, cols] = (gated * out * sig * (1.0 + pre * (1.0 - sig))).astype(bf16)
        normed[:, cols] = (unit * gain_j).astype(bf16)
        total = state[:, cols] + dot(queries_t, spread(grown, j, first) * scan.astype(f32))
        state[:, cols] = total
        packed[0:N, cols] = total.astype(bf16)
        fall = jnp.broadcast_to(decay[0:1, cols], (16, 128))
        high = fall.astype(bf16).astype(f32)
        packed[N : N + 16, cols] = jnp.where(
            row16 == 0, high, jnp.where(row16 == 1, fall - high, 0.0)
        ).astype(bf16)


def gate_back(grad_new, out_own, out_other, gate, mixed, scale, run, query, gain, decay):
    tokens = mixed.shape[0]

    def whole(shape):
        return pl.BlockSpec(shape, lambda k: (0, 0))

    def piece(width):
        return pl.BlockSpec((PIECE, width), lambda k: (k, 0))

    return pl.pallas_call(
        gate_back_kernel,
        grid=(tokens // PIECE,),
        in_specs=[
            whole((tokens, D)),
            whole((HALF, D)),
            whole((HALF, D)),
            piece(GROUP),
            piece(GROUP),
            piece(128),
            piece(128),
            piece(N),
            whole((8, GROUP)),
            whole((8, GROUP)),
        ],
        out_specs=[piece(GROUP), piece(GROUP), piece(GROUP), whole((N + 16, GROUP))],
        out_shape=[
            jax.ShapeDtypeStruct((tokens, GROUP), bf16),
            jax.ShapeDtypeStruct((tokens, GROUP), bf16),
            jax.ShapeDtypeStruct((tokens, GROUP), bf16),
            jax.ShapeDtypeStruct((N + 16, GROUP), bf16),
        ],
        scratch_shapes=[pltpu.VMEM((N, GROUP), f32), pltpu.VMEM((tokens, GROUP), f32)],
        compiler_params=pltpu.CompilerParams(vmem_limit_bytes=VMEM),
        cost_estimate=pl.CostEstimate(
            flops=1_400_000_000, bytes_accessed=12_000_000, transcendentals=400_000
        ),
        name="gate_back",
    )(grad_new, out_own, out_other, gate, mixed, scale, run, query, gain, decay)


def scan_back_kernel(
    place, conv_in, pre_in, step, run, grad, grad_gate, mixed, starts, last, entering, leaving, rim,
    taps, hp, skip, use_own, use_other, tail, rim_grad, grad_taps, grad_hp, act, delta, state, after,
    skip_sum
):
    k = pl.program_id(0)
    count = pl.num_programs(0)
    first = lanes((PIECE, 128)) < 64
    first_row = lanes((1, 128)) < 64
    raw, sizes, log_decay = step_parts(step[...], hp[...])
    running = run[...]
    start = running[0:1] - log_decay[0:1]
    end = running[PIECE - 1 : PIECE]
    from_start = jnp.exp(running - start)
    to_end = jnp.exp(end - running)
    whole = jnp.exp(end - start)
    before_all = jnp.exp(start)
    until_end = jnp.exp(end)

    @pl.when(k == 0)
    def _():
        delta[PIECE : PIECE + 8] = jnp.zeros((8, ACT), f32)
        grad_taps[...] = jnp.zeros_like(grad_taps)
        grad_hp[...] = jnp.zeros_like(grad_hp)
        skip_sum[...] = jnp.zeros_like(skip_sum)
        for j in range(PAIRS):
            cols = slice(128 * j, 128 * j + 128)
            state[:, cols] = leaving[:, cols]
            after[:, cols] = spread(until_end, j, first_row) * entering[:, cols] + last[:, cols]

    @pl.when(k > 0)
    def _():
        delta[PIECE : PIECE + 8] = delta[0:8]

    for j in range(ACT // 128):
        cols = slice(128 * j, 128 * j + 128)
        pre = pre_in[:, cols]
        act[:, cols] = pre * jax.nn.sigmoid(pre)

    upper = rows((PIECE, PIECE)) <= lanes((PIECE, PIECE))
    keys = act[:, GROUP : GROUP + N].astype(bf16)
    queries32 = act[:, GROUP + N :]
    queries = queries32.astype(bf16)
    queries_t = queries32.T.astype(bf16)
    affinity = jnp.where(upper, dot_nt(keys, queries), 0.0)
    running_t = running.T
    grad_affinity = jnp.zeros((PIECE, PIECE), f32)
    grad_keys = jnp.zeros((PIECE, N), f32)
    grad_queries = jnp.zeros((PIECE, N), f32)
    inner_sum = jnp.zeros((PIECE, 128), f32)
    outer_sum = jnp.zeros((PIECE, 128), f32)
    bound = jnp.zeros((8, 128), f32)
    for j in range(PAIRS):
        cols = slice(128 * j, 128 * j + 128)
        x = act[:, cols]
        sizes_j = spread(sizes, j, first)
        scaled = x * sizes_j
        dm = grad[:, cols]
        dm32 = dm.astype(f32)
        to_end_j = spread(to_end, j, first)
        back = state[:, cols]
        z = to_end_j * dot(keys, back)
        for side in range(2):
            h = 2 * j + side
            half = first if side == 0 else ~first
            gap = jnp.exp(jnp.minimum(running_t[h : h + 1, :] - running[:, h : h + 1], 0.0))
            mine = jnp.where(half, dm32, 0.0)
            z = z + dot(gap * affinity, mine)
            grad_affinity = grad_affinity + gap * dot_nt(jnp.where(half, scaled, 0.0), dm)
        skip_j = skip[0:1, cols]
        delta[0:PIECE, cols] = sizes_j * z + skip_j * dm32
        skip_sum[0:1, cols] += jnp.sum(dm32 * x, axis=0, keepdims=True)
        heads = (lanes((128, 128)) == 2 * j + (rows((128, 128)) >= 64)).astype(bf16)
        inner_sum = inner_sum + dot_split(x * z, heads)
        outer_sum = outer_sum + dot_split(dm32 * (mixed[:, cols] - skip_j * x), heads)
        after_j = after[:, cols]
        inside = jnp.sum(back * after_j, axis=0, keepdims=True)
        bound = bound + dot_split(jnp.broadcast_to(inside, (8, 128)), heads)
        before = spread(before_all, j, first_row) * entering[:, cols] + starts[0, :, cols]
        after[:, cols] = before
        weighted = spread(from_start, j, first) * dm32
        grad_queries = grad_queries + dot_nt(weighted, before)
        grad_keys = grad_keys + dot_nt(scaled * to_end_j, back)
        state[:, cols] = spread(whole, j, first_row) * back + dot(queries_t, weighted)
    grad_affinity = jnp.where(upper, grad_affinity, 0.0)
    delta[0:PIECE, GROUP : GROUP + N] = grad_keys + dot(grad_affinity, queries)
    delta[0:PIECE, GROUP + N :] = grad_queries + dot(grad_affinity.T, keys)

    flow = outer_sum - sizes * inner_sum
    grad_log = bound[0:1] + jnp.dot(
        upper.astype(f32), flow, precision=HIGHEST, preferred_element_type=f32
    )
    rate = jnp.exp(hp[1:2])
    live = lanes((PIECE, 128)) < HEADS
    grad_raw = jnp.where(live, (inner_sum - rate * grad_log) * jax.nn.sigmoid(raw), 0.0)
    is_first = place[1] == 0
    edge = HALF + EXTRA
    step_first = jnp.where(is_first, grad_raw, 0.0)
    step_second = jnp.where(is_first, 0.0, grad_raw)
    for use, gate_cols in ((use_own, slice(0, HALF)), (use_other, slice(HALF, GROUP))):
        use[:, edge:] = grad_gate[:, gate_cols]

    @pl.when(k == 0)
    def _():
        for side, gate_cols in ((0, slice(0, HALF)), (1, slice(HALF, GROUP))):
            tail[:, WIDE * side + edge : WIDE * side + WIDE] = grad_gate[
                PIECE - 16 :, gate_cols
            ].astype(f32)[8:]
    grad_hp[0:1] += jnp.sum(grad_raw, axis=0, keepdims=True)
    grad_hp[1:2] += jnp.sum(jnp.where(live, grad_log * log_decay, 0.0), axis=0, keepdims=True)

    for j in range(ACT // 128):
        cols = slice(128 * j, 128 * j + 128)
        pre = pre_in[:, cols]
        sig = jax.nn.sigmoid(pre)
        grown = delta[0:PIECE, cols] * sig * (1.0 + pre * (1.0 - sig))
        delta[0:PIECE, cols] = grown
        grad_taps[4:5, cols] += jnp.sum(grown, axis=0, keepdims=True)
        taken = conv_in[:, cols].astype(f32)
        total = jnp.zeros((PIECE, 128), f32)
        for t in range(4):
            moved = delta[3 - t : 3 - t + PIECE, cols]
            total = total + taps[t : t + 1, cols] * moved
            grad_taps[t : t + 1, cols] += jnp.sum(taken * moved, axis=0, keepdims=True)
        if j < PAIRS:
            use = use_own if j < 3 else use_other
            at = 128 * (j % 3)
            use[:, at : at + 128] = total.astype(bf16)
            targets = [(WIDE * (j // 3) + at, total)]
        else:
            at = HALF + 128 * (j - PAIRS)
            slot = step_first if j == PAIRS else step_second
            first_use = jnp.where(is_first, total, slot)
            second_use = jnp.where(is_first, slot, total)
            use_own[:, at : at + 128] = first_use.astype(bf16)
            use_other[:, at : at + 128] = second_use.astype(bf16)
            targets = [(at, first_use), (WIDE + at, second_use)]

        @pl.when(k == 0)
        def _():
            for at, values in targets:
                tail[:, at : at + 128] = values[PIECE - 8 :]

    @pl.when(k == count - 1)
    def _():
        for j in range(PAIRS):
            cols = slice(128 * j, 128 * j + 128)
            heads = (lanes((128, 128)) == 2 * j + (rows((128, 128)) >= 64)).astype(bf16)
            sums = dot_split(jnp.broadcast_to(skip_sum[0:1, cols], (8, 128)), heads)
            grad_hp[2:3] += sums[0:1]
        for j in range(ACT // 128):
            cols = slice(128 * j, 128 * j + 128)
            border = jnp.concatenate([jnp.zeros((8, 128), f32), delta[0:8, cols]], axis=0)
            taken = rim[:, cols].astype(f32)
            total = jnp.zeros((8, 128), f32)
            for t in range(4):
                moved = border[3 - t : 11 - t]
                total = total + taps[t : t + 1, cols] * moved
                grad_taps[t : t + 1, cols] += jnp.sum(taken * moved, axis=0, keepdims=True)
            if j < PAIRS:
                at = WIDE * (j // 3) + 128 * (j % 3)
                rim_grad[:, at : at + 128] = total
            else:
                at = HALF + 128 * (j - PAIRS)
                rim_grad[:, at : at + 128] = jnp.where(is_first, total, 0.0)
                rim_grad[:, WIDE + at : WIDE + at + 128] = jnp.where(is_first, 0.0, total)
        for side in range(2):
            rim_grad[:, WIDE * side + edge : WIDE * side + WIDE] = jnp.zeros((8, HALF), f32)


def scan_back(
    place, conv_in, pre, step, run, grad, grad_gate, mixed, starts, last, entering, leaving, rim,
    taps, hp, skip
):
    tokens = conv_in.shape[0]
    count = tokens // PIECE

    def whole(shape):
        return pl.BlockSpec(shape, lambda k, place: (0,) * len(shape))

    def piece(width):
        return pl.BlockSpec((PIECE, width), lambda k, place: (turned(count - 1 - k, place), 0))

    return pl.pallas_call(
        scan_back_kernel,
        grid_spec=pltpu.PrefetchScalarGridSpec(
            num_scalar_prefetch=1,
            grid=(count,),
            in_specs=[
                piece(ACT),
                piece(ACT),
                piece(128),
                piece(128),
                piece(GROUP),
                piece(GROUP),
                piece(GROUP),
                pl.BlockSpec((1, N, GROUP), lambda k, place: (count - 1 - k, 0, 0)),
                whole((N, GROUP)),
                whole((N, GROUP)),
                whole((N, GROUP)),
                whole((8, ACT)),
                whole((8, ACT)),
                whole((8, 128)),
                whole((8, GROUP)),
            ],
            out_specs=[
                piece(WIDE),
                piece(WIDE),
                whole((8, 2 * WIDE)),
                whole((8, 2 * WIDE)),
                whole((8, ACT)),
                whole((8, 128)),
            ],
            scratch_shapes=[
                pltpu.VMEM((PIECE, ACT), f32),
                pltpu.VMEM((PIECE + 8, ACT), f32),
                pltpu.VMEM((N, GROUP), f32),
                pltpu.VMEM((N, GROUP), f32),
                pltpu.VMEM((8, GROUP), f32),
            ],
        ),
        out_shape=[
            jax.ShapeDtypeStruct((tokens, WIDE), bf16),
            jax.ShapeDtypeStruct((tokens, WIDE), bf16),
            jax.ShapeDtypeStruct((8, 2 * WIDE), f32),
            jax.ShapeDtypeStruct((8, 2 * WIDE), f32),
            jax.ShapeDtypeStruct((8, ACT), f32),
            jax.ShapeDtypeStruct((8, 128), f32),
        ],
        compiler_params=pltpu.CompilerParams(vmem_limit_bytes=VMEM),
        cost_estimate=pl.CostEstimate(
            flops=2_000_000_000, bytes_accessed=9_000_000, transcendentals=2_500_000
        ),
        name="scan_back",
    )(place, conv_in, pre, step, run, grad, grad_gate, mixed, starts, last, entering, leaving, rim,
      taps, hp, skip)


def parts_kernel(use_own, use_other, own, other, sent0, sent1, sent2, sent3):
    part = dot_nt(use_own[...], own[...]) + dot_nt(use_other[...], other[...])
    for index, sent in enumerate((sent0, sent1, sent2, sent3)):
        sent[...] = part[PIECE * index : PIECE * index + PIECE].astype(sent.dtype)


def project_back(use_own, use_other, own, other):
    tokens = use_own.shape[0]
    width = 256

    def whole(shape):
        return pl.BlockSpec(shape, lambda k: (0, 0))

    return pl.pallas_call(
        parts_kernel,
        grid=(D // width,),
        in_specs=[whole((tokens, WIDE))] * 2 + [pl.BlockSpec((width, WIDE), lambda k: (k, 0))] * 2,
        out_specs=[pl.BlockSpec((PIECE, width), lambda k: (0, k))] * 4,
        out_shape=[jax.ShapeDtypeStruct((PIECE, D), f32 if k == 0 else bf16) for k in range(4)],
        compiler_params=pltpu.CompilerParams(vmem_limit_bytes=VMEM),
        cost_estimate=pl.CostEstimate(
            flops=3_200_000_000, bytes_accessed=9_000_000, transcendentals=0
        ),
        name="project_back",
    )(use_own, use_other, own, other)


def early_kernel(normed, grad_gate, normed_out, grad_new, own, other, sums):
    i = pl.program_id(0)

    @pl.when(i == 0)
    def _():
        sums[0] = dot_tn(normed_out[:, :HALF], grad_new[...])
        sums[1] = dot_tn(normed_out[:, HALF:], grad_new[...])

    block = dot_tn(normed[...], grad_gate[...])
    for side, sent in enumerate((own, other)):
        sent[:, :HALF] = block[:, HALF * side : HALF * side + HALF].astype(bf16)
        for s in range(4):
            row = pl.ds(pl.multiple_of(96 * i + 24 * s, 8), 24)
            pieces = [sums[side, row, HALF * q : HALF * q + HALF] for q in range(4)]
            sent[96 * s : 96 * s + 96, HALF:] = jnp.concatenate(pieces, axis=0).astype(bf16)


def early_grads(normed, grad_gate, normed_out, grad_new):
    tokens = normed.shape[0]

    def whole(shape):
        return pl.BlockSpec(shape, lambda i: (0, 0))

    return pl.pallas_call(
        early_kernel,
        grid=(4,),
        in_specs=[
            pl.BlockSpec((tokens, HALF), lambda i: (0, i)),
            whole((tokens, GROUP)),
            whole((tokens, GROUP)),
            whole((tokens, D)),
        ],
        out_specs=[pl.BlockSpec((HALF, GROUP), lambda i: (i, 0))] * 2,
        out_shape=[jax.ShapeDtypeStruct((D, GROUP), bf16)] * 2,
        scratch_shapes=[pltpu.VMEM((2, HALF, D), f32)],
        compiler_params=pltpu.CompilerParams(vmem_limit_bytes=VMEM),
        cost_estimate=pl.CostEstimate(
            flops=2_400_000_000, bytes_accessed=9_000_000, transcendentals=0
        ),
        name="early_grads",
    )(normed, grad_gate, normed_out, grad_new)


def split_pair(values, lane, at):
    high = values.astype(bf16).astype(f32)
    return jnp.where(lane == at, high, jnp.where(lane == at + 1, values - high, 0.0))


def receive_kernel(part, one, two, three, feed, target, branch_out, result, scale):
    total = part[...] + one[...].astype(f32) + two[...].astype(f32) + three[...].astype(f32)
    square = total[:, D : D + 1] + total[:, D + 1 : D + 2]
    s_out = lax.rsqrt(square / DI + epsilon)
    branch = s_out * total[:, :D]
    branch_out[...] = branch
    result[...] = (feed[...].astype(f32) + branch).astype(bf16)
    mean = jnp.sum(branch * target[...].astype(f32), axis=1, keepdims=True) / DI
    lane = lanes((PIECE, 128))
    scale[...] = (split_pair(s_out, lane, 0) + split_pair(mean, lane, 2)).astype(bf16)


def receive(parts, feed, target):
    return pl.pallas_call(
        receive_kernel,
        out_shape=[
            jax.ShapeDtypeStruct((PIECE, D), f32),
            jax.ShapeDtypeStruct((PIECE, D), bf16),
            jax.ShapeDtypeStruct((PIECE, 128), bf16),
        ],
        compiler_params=pltpu.CompilerParams(vmem_limit_bytes=VMEM),
        cost_estimate=pl.CostEstimate(
            flops=3_000_000, bytes_accessed=4_500_000, transcendentals=1000
        ),
        name="receive",
    )(*parts, feed, target)


def receive_back_kernel(
    part, one, two, three, feed, grad_new, gain, branch, scale_in, grad_out, scale_out
):
    total = part[...] + one[...].astype(f32) + two[...].astype(f32) + three[...].astype(f32)
    values = feed[...].astype(f32)
    s_in = lax.rsqrt(jnp.mean(values * values, axis=1, keepdims=True) + epsilon)
    unit = values * s_in
    grad_unit = total * gain[0:1]
    grad = grad_new[...].astype(f32) + s_in * (
        grad_unit - unit * jnp.mean(unit * grad_unit, axis=1, keepdims=True)
    )
    low = grad.astype(bf16)
    grad_out[...] = low
    mean = jnp.sum(branch[...] * low.astype(f32), axis=1, keepdims=True) / DI
    lane = lanes((PIECE, 128))
    kept = jnp.where(lane < 2, scale_in[...].astype(f32), 0.0)
    scale_out[...] = (kept + split_pair(mean, lane, 2)).astype(bf16)


def receive_back(parts, feed, grad_new, gain, branch, scale):
    return pl.pallas_call(
        receive_back_kernel,
        out_shape=[
            jax.ShapeDtypeStruct((PIECE, D), bf16),
            jax.ShapeDtypeStruct((PIECE, 128), bf16),
        ],
        compiler_params=pltpu.CompilerParams(vmem_limit_bytes=VMEM),
        cost_estimate=pl.CostEstimate(
            flops=4_000_000, bytes_accessed=4_500_000, transcendentals=1000
        ),
        name="receive_back",
    )(*parts, feed, grad_new, gain, branch, scale)


def pick(core, first, second):
    return jnp.where(core == 0, first, second)


def spread_weights(core, head, gate_inner, shared_bc, step_proj):
    gate = gate_inner[:, :DI].reshape(24, 4, 2, HALF)
    inner = gate_inner[:, DI:].reshape(24, 4, 2, HALF)
    heads = step_proj.reshape(24, 4, HEADS)
    fill = jnp.zeros((24, 128 - HEADS), bf16)
    halves = []
    for q in range(2):
        pieces = []
        for g in range(4):
            own = heads[:, g]
            slot = [own, fill, own[:, 6:], own[:, :6], fill]
            extra = [shared_bc] if q == 0 else slot
            pieces.append(jnp.concatenate([inner[:, g, q]] + extra + [gate[:, g, q]], axis=1))
        halves.append(jnp.stack(pieces))
    kept = pick(core, halves[0], halves[1])
    got = swap(pick(core, halves[1], halves[0]))
    layers = [pick(core, kept, got), pick(core, got, kept)]
    return [exchange_head(values, head).reshape(96, WIDE) for values in layers]


def out_pairs():
    pairs = []
    for layer in range(2):
        for z in range(4):
            for y in range(4):
                for x in range(4):
                    source = (layer * 16 + z * 4 + y) * 4 + x
                    place = layer * 8 + (y % 2) * 4 + x
                    pairs.append((source, ((y // 2) * 16 + place) * 4 + z))
    return pairs


def out_back_pairs(part):
    pairs = []
    for core in range(2):
        for place in range(16):
            layer = (place + part) % 2
            for group in range(4):
                j = place // 2
                target = (layer * 16 + group * 4 + 2 * core + j // 4) * 4 + j % 4
                pairs.append(((core * 16 + place) * 4 + group, target))
    return pairs


EVERY = ("section", "seq", "head")


def gather_seq(a):
    return lax.all_gather(a, "seq", axis=0, tiled=True)


def gather_small(core, a):
    other = swap(a)
    both = jnp.concatenate([pick(core, a, other), pick(core, other, a)], axis=1)
    width = a.shape[1]
    both = jnp.pad(both.reshape(2 * width // 128, 128), ((0, 8 - 2 * width // 128), (0, 0)))
    sent = jnp.broadcast_to(both[None], (64, 8, 128)).reshape(512, 128)
    got = lax.all_to_all(sent, ("seq", "head"), 0, 0, tiled=True).reshape(64, 1024)
    return got[:, :width], got[:, width : 2 * width]


def layer_params(core, head, small, per_head):
    gain_in = small[:, :24].reshape(1, D)
    conv = small[:, 24:232].reshape(64, 4, 52).transpose(1, 0, 2).reshape(4, DI + 2 * N)
    bias = small[:, 232:284].reshape(1, DI + 2 * N)
    gain = small[:, 284:332].reshape(1, DI)
    taps = jnp.concatenate([conv, bias, jnp.zeros((3, DI + 2 * N), f32)], axis=0)

    def grouped(values, width):
        own = lax.dynamic_slice_in_dim(values, (2 * head + core) * width, width, 1)
        other = lax.dynamic_slice_in_dim(values, (2 * head + 1 - core) * width, width, 1)
        return [own, other]

    taps = jnp.concatenate(grouped(taps, HALF) + [taps[:, DI:]], axis=1)
    gain = jnp.broadcast_to(jnp.concatenate(grouped(gain, HALF), axis=1), (8, GROUP))
    per_head = jnp.concatenate(grouped(per_head, 6), axis=1)
    hp = jnp.pad(per_head, ((0, 5), (0, 128 - HEADS)))
    skip = jnp.broadcast_to(jnp.repeat(per_head[2:3], 64, axis=1), (8, GROUP))
    return dict(
        taps=taps, gain=gain, hp=hp, skip=skip, gain_in=jnp.broadcast_to(gain_in, (8, D))
    )


def tied(values, anchor):
    return lax.optimization_barrier((values, anchor))[0]


def layer_forward(core, head, feed, feed_all, target, weights, out_weights):
    place = jnp.stack([head, core])
    own, other = weights["own"], weights["other"]
    normed, conv_in, step, gate = project(core.reshape(1), feed_all, weights["gain_in"], own, other)
    last_row = PIECE * lax.rem(7 - head, 4) + PIECE - 8
    rim = lax.ppermute(
        lax.dynamic_slice_in_dim(conv_in, last_row, 8, 0), "seq", [(i, i + 1) for i in range(15)]
    )
    pre, mixed0, query, run, starts, last, packed = scan_local(
        place, conv_in, step, rim, weights["taps"], weights["hp"], weights["skip"]
    )
    entering = carried(packed, -1)
    entering, out_own, out_other = out_weights(packed, entering)
    mixed, *sent = gate_out(
        mixed0, run, query, entering, gate, weights["gain"], out_own, out_other
    )
    branch, result, scale = receive(scatter_head(sent), feed, target)
    kept = dict(
        feed=feed, normed=normed, gate=gate, conv_in=conv_in, rim=rim, step=step, pre=pre,
        mixed=mixed, query=query, run=run, starts=starts, last=last, entering=entering,
        scale=scale, branch=branch, packed=packed, out_own=out_own, out_other=out_other,
    )
    return result, kept


def layer_backward(
    core, head, incoming, gathered, scale, kept, below, weights, after_gate, before_receive
):
    place = jnp.stack([head, core])
    own, other = weights["own"], weights["other"]
    decay = jnp.broadcast_to(
        kept["packed"][N : N + 1].astype(f32) + kept["packed"][N + 1 : N + 2].astype(f32),
        (8, GROUP),
    )
    grad_scan, grad_gate, normed_out, packed = gate_back(
        gathered, kept["out_own"], kept["out_other"], kept["gate"], kept["mixed"], scale,
        kept["run"], kept["query"], weights["gain"], decay,
    )
    leaving = carried(packed, 1)
    normed = kept["normed"]
    early, leaving = after_gate(early_grads(normed, grad_gate, normed_out, gathered), leaving)
    use_own, use_other, tail, rim_grad, grad_taps, grad_hp = scan_back(
        place, kept["conv_in"], kept["pre"], kept["step"], kept["run"], grad_scan, grad_gate,
        kept["mixed"], kept["starts"], kept["last"], kept["entering"], leaving, kept["rim"],
        weights["taps"], weights["hp"], weights["skip"],
    )
    from_next = lax.ppermute(rim_grad, "seq", [(i + 1, i) for i in range(15)])
    last_row = PIECE * lax.rem(7 - head, 4) + PIECE - 8
    tail = (tail + from_next).astype(bf16)
    use_own = lax.dynamic_update_slice_in_dim(use_own, tail[:, :WIDE], last_row, 0)
    use_other = lax.dynamic_update_slice_in_dim(use_other, tail[:, WIDE:], last_row, 0)
    sent = project_back(use_own, use_other, own, other)
    edge = HALF + EXTRA
    use_own, use_other = tied((use_own, use_other), sent[1])
    small = small_columns(core, head, grad_taps, grad_hp)
    small = jnp.pad(small, ((0, 0), (HALF + SMALL_AT, EXTRA - SMALL_AT - SMALL)))
    grad_x = (
        (dot_tn(normed, use_own[:, :edge]) + jnp.where(core == 1, small, 0.0)).astype(bf16),
        (dot_tn(normed, use_other[:, :edge]) + jnp.where(core == 0, small, 0.0)).astype(bf16),
    )
    grad_feed, scale_below = receive_back(
        before_receive(scatter_head(sent), grad_x), kept["feed"], incoming, weights["gain_in"], below["branch"],
        below["scale"],
    )
    return grad_feed, scale_below, grad_x, early


def small_columns(core, head, grad_taps, grad_hp):
    taps = grad_taps[:5]
    full = jnp.zeros((5, DI), f32)
    full = lax.dynamic_update_slice_in_dim(full, taps[:, :HALF], (2 * head + core) * HALF, 1)
    full = lax.dynamic_update_slice_in_dim(
        full, taps[:, HALF:GROUP], (2 * head + 1 - core) * HALF, 1
    )
    full = jnp.concatenate([full, taps[:, GROUP:]], axis=1)
    full = full.reshape(5, 64, 52).transpose(1, 0, 2).reshape(64, 260)
    first, second = grad_hp[:3, :6], grad_hp[:3, 6:HEADS]
    sums = jnp.concatenate([pick(core, first, second), pick(core, second, first)], axis=1)
    sums = jnp.broadcast_to(sums.reshape(1, 36), (64, 36))
    return jnp.concatenate([full, sums, jnp.zeros((64, 16), f32)], axis=1).reshape(D, SMALL)


def summed(own, other):
    return (own.astype(f32) + swap(other).astype(f32)).astype(bf16)


def scatter_seq(a):
    return lax.psum_scatter(a, "seq", scatter_dimension=0, tiled=True)


def scatter_seq_now(a):
    got = lax.all_to_all(a, "seq", 0, 0, tiled=True).astype(f32)
    return jnp.sum(got.reshape(16, 96, a.shape[1]), axis=0).astype(bf16)


def per_device(
    tokens_in, cotangent, input_gain, gate_inner, shared_bc, step_proj, conv_weight, conv_bias,
    step_bias, decay_log, skip_gain, output_gain, out_proj
):
    core = lax.axis_index("section")
    head = lax.axis_index("head")
    tokens = lax.dynamic_index_in_dim(tokens_in, core, 0, False)
    grad_top = lax.dynamic_index_in_dim(cotangent, core, 0, False)
    edge = HALF + EXTRA

    pieces = spread_weights(core, head, gate_inner[0], shared_bc[0], step_proj[0])
    own0 = gather_seq(pieces[0])
    out_piece = lax.ppermute(out_proj[0], EVERY, out_pairs())
    small = jnp.concatenate(
        [input_gain, conv_weight[0].reshape(1, 208), conv_bias, output_gain], axis=1
    ).astype(f32)
    small = gather_small(core, tied(jnp.pad(small, ((0, 0), (0, 52))), pieces[0]))
    per_head = jnp.concatenate([step_bias, decay_log, skip_gain], axis=0)
    other_head = swap(tied(per_head, pieces[0]))
    head_values = [pick(core, per_head, other_head), pick(core, other_head, per_head)]
    weights = [layer_params(core, head, small[l], head_values[l]) for l in range(2)]
    feed_all = jnp.concatenate(gather_head(tied(tokens, pieces[0])), axis=0)
    feed_all, weights, own0, out_piece = lax.optimization_barrier(
        (feed_all, weights, own0, out_piece)
    )
    weights[0].update(own=own0, other=swap(own0))
    out = gather_seq(out_piece)
    own1 = gather_seq(tied(pieces[1], weights[0]["other"]))

    later = {}

    def out_first(packed, entering):
        mine = tied(out, packed)
        later["out"] = (mine, swap(mine))
        grad_all = jnp.concatenate(gather_head(tied(grad_top, packed)), axis=0)
        entering, later["grad_all"] = lax.optimization_barrier((entering, grad_all))
        return [entering] + [a[:HALF] for a in later["out"]]

    def out_second(packed, entering):
        return [entering] + [a[HALF:] for a in later["out"]]

    hidden, kept0 = layer_forward(core, head, tokens, feed_all, tokens, weights[0], out_first)
    feed_all = jnp.concatenate(gather_head(hidden), axis=0)
    own1 = tied(own1, hidden)
    weights[1].update(own=own1, other=swap(own1))
    result, kept1 = layer_forward(core, head, hidden, feed_all, grad_top, weights[1], out_second)
    scale = jnp.concatenate(gather_head(kept1["scale"]), axis=0)

    def after_gate1(values, leaving):
        later["sum"] = summed(*values)
        return later["sum"], leaving

    def before_receive1(sent, grad_x):
        return tied(sent, later["sum"])

    grad_hidden, scale, grad_x1, early1 = layer_backward(
        core, head, grad_top, later["grad_all"], scale, kept1, kept0, weights[1], after_gate1, before_receive1
    )
    chunks = gather_head(jnp.concatenate([grad_hidden, scale], axis=1))
    early1 = scatter_seq_now(tied(early1, grad_hidden))
    chunks, grad_x1, early1 = lax.optimization_barrier((chunks, grad_x1, early1))
    grad_all = jnp.concatenate([a[:, :D] for a in chunks], axis=0)
    scale = jnp.concatenate([a[:, D:] for a in chunks], axis=0)

    def after_gate0(values, leaving):
        values = [jnp.concatenate([grad_x1[i], values[i]], axis=1) for i in range(2)]
        later["sum"] = summed(*values)
        return scatter_seq(later["sum"]), leaving

    def before_receive0(sent, grad_x):
        return tied(sent, later["sum"])

    grad_feed, _, grad_x0, early0 = layer_backward(
        core, head, grad_hidden, grad_all, scale, kept0, kept0, weights[0], after_gate0, before_receive0
    )
    x0 = scatter_seq_now(summed(*grad_x0))
    got = swap(pick(core, result, hidden))
    layer_out = jnp.stack([pick(core, hidden, got), pick(core, got, result)])
    got = swap(pick(core, grad_hidden, grad_feed))
    grad_in = jnp.stack([pick(core, grad_feed, got), pick(core, got, grad_hidden)])

    def out_rows(a):
        return a.reshape(4, 24, HALF).transpose(1, 0, 2).reshape(24, D)

    out0, out1 = out_rows(early0[:, WIDE:]), out_rows(early1[:, HALF:])
    even = lax.rem(lax.axis_index("seq"), 2)
    rows_out = [
        lax.ppermute(pick(even, out0, out1), EVERY, out_back_pairs(0)),
        lax.ppermute(pick(even, out1, out0), EVERY, out_back_pairs(1)),
    ]
    grad_out = jnp.concatenate(
        [pick(core, rows_out[0], rows_out[1]), pick(core, rows_out[1], rows_out[0])], axis=0
    ).astype(f32)
    both = jnp.concatenate(
        [x0, early0[:, edge:WIDE], early0[:, :edge], early1[:, :HALF]], axis=1
    ).reshape(4, 24, 2 * WIDE)
    both = exchange_head(both, head)
    first, second = both[:, :, :WIDE], both[:, :, WIDE:]
    mine = pick(core, first, second)
    theirs = swap(pick(core, second, first))
    low, high = pick(core, mine, theirs).astype(f32), pick(core, theirs, mine).astype(f32)
    columns = []
    for start in (edge, 0):
        for g in range(4):
            for half in (low, high):
                columns.append(half[g, :, start : start + HALF])
    grad_gate_inner = jnp.concatenate(columns, axis=1)
    grad_shared = jnp.sum(low[:, :, HALF:edge], axis=0)
    slot, turned_slot = high[:, :, HALF : HALF + 128], high[:, :, HALF + 128 : edge]
    steps = slot[:, :, :HEADS] + jnp.concatenate(
        [turned_slot[:, :, 6:HEADS], turned_slot[:, :, :6]], axis=2
    )
    grad_step = jnp.concatenate([steps[g] for g in range(4)], axis=1)
    small = slot[:, :, SMALL_AT : SMALL_AT + SMALL].reshape(4, 24 * SMALL)
    taps = jnp.sum(small[:, :260], axis=0)
    sums = small[:, 260:296].reshape(4, 3, HEADS).transpose(1, 0, 2).reshape(3, 48)
    grad_output_gain = jnp.sum(grad_out * out_proj[0].astype(f32), axis=1) / output_gain[0].astype(
        f32
    )
    grad_input_gain = (
        jnp.sum(grad_gate_inner * gate_inner[0].astype(f32), axis=1)
        + jnp.sum(grad_shared * shared_bc[0].astype(f32), axis=1)
        + jnp.sum(grad_step * step_proj[0].astype(f32), axis=1)
    ) / input_gain[0].astype(f32)
    return (
        layer_out[None],
        grad_in[None],
        grad_input_gain[None],
        grad_gate_inner[None],
        grad_shared[None],
        grad_step[None],
        taps[:208].reshape(1, 4, 52),
        taps[208:260][None],
        sums[0:1],
        sums[1:2],
        sums[2:3],
        grad_output_gain[None],
        grad_out[None],
    )


def solution(mesh):
    both = ("seq", "head")
    return jax.shard_map(
        per_device,
        mesh=mesh,
        in_specs=(
            P(None, both, None),
            P(None, both, None),
            P("section", both),
            P("section", both, None),
            P("section", both, None),
            P("section", both, None),
            P("section", None, both),
            P("section", both),
            P("section", None),
            P("section", None),
            P("section", None),
            P("section", both),
            P("section", both, None),
        ),
        out_specs=(
            P("section", None, both, None),
            P("section", None, both, None),
            P("section", both),
            P("section", both, None),
            P("section", both, None),
            P("section", both, None),
            P("section", None, both),
            P("section", both),
            P("section", None),
            P("section", None),
            P("section", None),
            P("section", both),
            P("section", both, None),
        ),
        check_vma=False,
    )
```

```python
import jax
import jax.numpy as jnp
from jax import lax
from jax.experimental import pallas as pl
from jax.experimental.pallas import tpu as pltpu
from jax.sharding import PartitionSpec as P

bf16 = jnp.bfloat16
f32 = jnp.float32
HIGHEST = lax.Precision.HIGHEST

D = 1536
DI = 3072
N = 128
GROUP = 768
HALF = 384
HEADS = 12
PIECE = 128
PAIRS = 6
EXTRA = 256
ACT = GROUP + 2 * N
WIDE = HALF + EXTRA + HALF
SMALL_AT = 32
VMEM = 24 * 1024 * 1024
epsilon = 1e-05


def from_head(a, k):
    return lax.ppermute(a, "head", [(i, (i - k) % 4) for i in range(4)])


def from_seq(a, dz, dy, wrap):
    pairs = []
    for z in range(4):
        for y in range(4):
            sz, sy = z + dz, y + dy
            if wrap:
                sz, sy = sz % 4, sy % 4
            if 0 <= sz < 4 and 0 <= sy < 4:
                pairs.append((sz * 4 + sy, z * 4 + y))
    return lax.ppermute(a, "seq", pairs)


def swap(a):
    return lax.ppermute(a, "section", [(0, 1), (1, 0)])


def gather_head(a):
    one, three = from_head(a, 1), from_head(a, 3)
    two = from_head(a, 2)
    return [a, one, two, three]


def scatter_head(parts):
    one, three = from_head(parts[1], 3), from_head(parts[3], 1)
    two = from_head(parts[2], 2)
    return [parts[0], one, two, three]


def exchange_head(parts, place):
    got = [lax.dynamic_index_in_dim(parts, place, 0, False)]
    for k in (1, 3, 2):
        sent = lax.dynamic_index_in_dim(parts, lax.rem(place + 4 - k, 4), 0, False)
        got.append(from_head(sent, k))
    got = [got[0], got[1], got[3], got[2]]
    twice = jnp.stack(got + got)
    return lax.dynamic_slice_in_dim(twice, lax.rem(4 - place, 4), 4, 0)


def unpack_state(a):
    decay = a[N : N + 1].astype(f32) + a[N + 1 : N + 2].astype(f32)
    return decay, a[:N].astype(f32)


def join(earlier, later):
    return earlier[0] * later[0], earlier[1] * later[0] + later[1]


def carried(packed, sign):
    seq = lax.axis_index("seq")
    y = lax.rem(seq, 4)
    ahead = y if sign < 0 else 3 - y
    near = {k: unpack_state(from_seq(packed, 0, sign * k, True)) for k in (1, 3, 2)}
    own = unpack_state(packed)
    before = (jnp.ones_like(own[0]), jnp.zeros_like(own[1]))
    after = own
    for k in (3, 2, 1):
        decay, state = near[k]
        use = k <= ahead
        before = join(before, (jnp.where(use, decay, 1.0), jnp.where(use, state, 0.0)))
        after = join(after, (jnp.where(use, 1.0, decay), jnp.where(use, 0.0, state)))
    whole = join(before, after)
    packed_whole = pack_state(whole[0], whole[1])
    far = {k: unpack_state(from_seq(packed_whole, sign * k, 0, False)) for k in (1, 3, 2)}
    total = jnp.zeros_like(own[1])
    for k in (3, 2, 1):
        decay, state = far[k]
        total = total * decay + state
    return total * before[0] + before[1]


def pack_state(decay, state):
    high = decay.astype(bf16)
    low = (decay - high.astype(f32)).astype(bf16)
    fill = jnp.zeros((14, state.shape[1]), bf16)
    return jnp.concatenate([state.astype(bf16), high, low, fill], axis=0)


def stored(shape, dtype):
    return pltpu.HBM(shape, dtype)


def far(pinned, *arrays):
    if not pinned:
        return list(arrays)
    return [pltpu.with_memory_space_constraint(a, pltpu.HBM) for a in arrays]


def dot(a, b):
    return jnp.dot(a.astype(bf16), b.astype(bf16), preferred_element_type=f32)


def dot_nt(a, b):
    return lax.dot_general(
        a.astype(bf16), b.astype(bf16), (((1,), (1,)), ((), ())), preferred_element_type=f32
    )


def dot_tn(a, b):
    return lax.dot_general(
        a.astype(bf16), b.astype(bf16), (((0,), (0,)), ((), ())), preferred_element_type=f32
    )


def dot_split(a, b):
    high = a.astype(bf16)
    low = (a - high.astype(f32)).astype(bf16)
    return dot(high, b) + dot(low, b)


def lanes(shape):
    return lax.broadcasted_iota(jnp.int32, shape, 1)


def rows(shape):
    return lax.broadcasted_iota(jnp.int32, shape, 0)


def spread(values, j, first):
    return jnp.where(first, values[:, 2 * j : 2 * j + 1], values[:, 2 * j + 1 : 2 * j + 2])


def apart(values, first):
    return jnp.concatenate(
        [jnp.where(first, values, 0.0), jnp.where(first, 0.0, values)], axis=0
    ).astype(bf16)


def step_parts(step, hp):
    raw = step + hp[0:1]
    live = lanes(raw.shape) < HEADS
    sizes = jnp.maximum(raw, 0.0) + jnp.log1p(jnp.exp(-jnp.abs(raw)))
    sizes = jnp.where(live, sizes, 0.0)
    return raw, sizes, -jnp.exp(hp[1:2]) * sizes


def scan_kernel(
    place, conv_in, step, rim, taps, hp, skip, pre_out, mixed, query, run, starts, last, packed,
    padded, act, state, carry, entered, weighted
):
    k = pl.program_id(0)

    @pl.when(k == 0)
    def _():
        state[...] = jnp.zeros_like(state)
        carry[...] = jnp.zeros_like(carry)
        padded[0:8] = rim[...].astype(f32)

    @pl.when(k > 0)
    def _():
        padded[0:8] = padded[PIECE : PIECE + 8]

    padded[8 : PIECE + 8] = conv_in[...].astype(f32)
    for j in range(ACT // 128):
        cols = slice(128 * j, 128 * j + 128)
        pre = taps[4:5, cols] + taps[0:1, cols] * padded[5 : PIECE + 5, cols]
        for t in range(1, 4):
            pre = pre + taps[t : t + 1, cols] * padded[5 + t : PIECE + 5 + t, cols]
        pre_out[:, cols] = pre
        act[:, cols] = pre * jax.nn.sigmoid(pre)
    raw, sizes, log_decay = step_parts(step[...], hp[...])
    lower = rows((PIECE, PIECE)) >= lanes((PIECE, PIECE))
    start = carry[0:1]
    running = start + jnp.dot(
        lower.astype(f32), log_decay, precision=HIGHEST, preferred_element_type=f32
    )
    run[...] = running
    end = running[PIECE - 1 : PIECE]
    carry[...] = jnp.broadcast_to(end, carry.shape)
    running_t = running.T
    keys = act[:, GROUP : GROUP + N]
    queries = act[:, GROUP + N :].astype(bf16)
    query[...] = queries
    affinity = jnp.where(lower, dot_nt(queries, keys), 0.0)
    keys_t = keys.T.astype(bf16)
    from_start = jnp.exp(running - start)
    to_end = jnp.exp(end - running)
    whole = jnp.exp(end - start)
    total = jnp.exp(end)
    first = lanes((PIECE, 128)) < 64
    first_row = lanes((1, 128)) < 64
    row16 = rows((16, 128))
    entered[...] = dot(queries, state[...])
    for j in range(PAIRS):
        cols = slice(128 * j, 128 * j + 128)
        x = act[:, cols]
        scaled = x * spread(sizes, j, first)
        weighted[:, cols] = (scaled * spread(to_end, j, first)).astype(bf16)
        gaps = []
        for h in (2 * j, 2 * j + 1):
            gap = jnp.exp(jnp.minimum(running[:, h : h + 1] - running_t[h : h + 1, :], 0.0))
            gaps.append(gap * affinity)
        y = spread(from_start, j, first) * entered[:, cols] + dot(
            jnp.concatenate(gaps, axis=1), apart(scaled, first)
        )
        mixed[:, cols] = y + skip[0:1, cols] * x
    entered[...] = dot(keys_t, weighted[...])
    for j in range(PAIRS):
        cols = slice(128 * j, 128 * j + 128)
        before = state[:, cols]
        starts[0, :, cols] = before.astype(bf16)
        after = spread(whole, j, first_row) * before + entered[:, cols]
        state[:, cols] = after
        last[:, cols] = after
        packed[0:N, cols] = after.astype(bf16)
        decay = jnp.broadcast_to(spread(total, j, first_row), (16, 128))
        high = decay.astype(bf16).astype(f32)
        packed[N : N + 16, cols] = jnp.where(
            row16 == 0, high, jnp.where(row16 == 1, decay - high, 0.0)
        ).astype(bf16)


def turned(k, place):
    return lax.rem(k + 4 - place[0], 4)


def scan_local(place, conv_in, step, rim, taps, hp, skip, pinned):
    tokens = conv_in.shape[0]
    kept = stored if pinned else jax.ShapeDtypeStruct

    def whole(shape):
        return pl.BlockSpec(shape, lambda k, place: (0,) * len(shape))

    def piece(width):
        return pl.BlockSpec((PIECE, width), lambda k, place: (turned(k, place), 0))

    return pl.pallas_call(
        scan_kernel,
        grid_spec=pltpu.PrefetchScalarGridSpec(
            num_scalar_prefetch=1,
            grid=(tokens // PIECE,),
            in_specs=[
                piece(ACT),
                piece(128),
                whole((8, ACT)),
                whole((8, ACT)),
                whole((8, 128)),
                whole((8, GROUP)),
            ],
            out_specs=[
                piece(ACT),
                piece(GROUP),
                piece(N),
                piece(128),
                pl.BlockSpec((1, N, GROUP), lambda k, place: (k, 0, 0)),
                whole((N, GROUP)),
                whole((N + 16, GROUP)),
            ],
            scratch_shapes=[
                pltpu.VMEM((PIECE + 8, ACT), f32),
                pltpu.VMEM((PIECE, ACT), f32),
                pltpu.VMEM((N, GROUP), f32),
                pltpu.VMEM((8, 128), f32),
                pltpu.VMEM((PIECE, GROUP), f32),
                pltpu.VMEM((PIECE, GROUP), bf16),
            ],
        ),
        out_shape=[
            kept((tokens, ACT), f32),
            jax.ShapeDtypeStruct((tokens, GROUP), f32),
            jax.ShapeDtypeStruct((tokens, N), bf16),
            jax.ShapeDtypeStruct((tokens, 128), f32),
            kept((tokens // PIECE, N, GROUP), bf16),
            kept((N, GROUP), f32),
            stored((N + 16, GROUP), bf16),
        ],
        compiler_params=pltpu.CompilerParams(vmem_limit_bytes=VMEM),
        cost_estimate=pl.CostEstimate(
            flops=1_000_000_000, bytes_accessed=8_000_000, transcendentals=1_500_000
        ),
        name="scan_local",
    )(place, conv_in, step, rim, taps, hp, skip)


def project_kernel(core, feed, gain, own, other, normed, conv_in, step, gate):
    values = feed[...].astype(f32)
    scale = lax.rsqrt(jnp.mean(values * values, axis=1, keepdims=True) + epsilon)
    low = (values * scale * gain[0:1]).astype(bf16)
    normed[...] = low
    mine = dot(low, own[...])
    theirs = dot(low, other[...])
    is_first = core[0] == 0
    edge = HALF + EXTRA
    conv_in[:, :HALF] = mine[:, :HALF].astype(bf16)
    conv_in[:, HALF:GROUP] = theirs[:, :HALF].astype(bf16)
    conv_in[:, GROUP:] = jnp.where(is_first, mine[:, HALF:edge], theirs[:, HALF:edge]).astype(bf16)
    slot = jnp.where(is_first, theirs[:, HALF : HALF + 128], mine[:, HALF + 128 : edge])
    step[...] = slot.astype(bf16).astype(f32)
    gate[:, :HALF] = mine[:, edge:].astype(bf16)
    gate[:, HALF:] = theirs[:, edge:].astype(bf16)


def project(core, feed, gain, own, other, pinned):
    tokens = feed.shape[0]

    def whole(shape):
        return pl.BlockSpec(shape, lambda k, core: (0, 0))

    def piece(width):
        return pl.BlockSpec((2 * PIECE, width), lambda k, core: (k, 0))

    return pl.pallas_call(
        project_kernel,
        grid_spec=pltpu.PrefetchScalarGridSpec(
            num_scalar_prefetch=1,
            grid=(tokens // (2 * PIECE),),
            in_specs=[piece(D), whole((8, D)), whole((D, WIDE)), whole((D, WIDE))],
            out_specs=[piece(D), piece(ACT), piece(128), piece(GROUP)],
        ),
        out_shape=[
            stored((tokens, D), bf16),
            jax.ShapeDtypeStruct((tokens, ACT), bf16),
            jax.ShapeDtypeStruct((tokens, 128), f32),
            stored((tokens, GROUP), bf16),
        ],
        compiler_params=pltpu.CompilerParams(vmem_limit_bytes=VMEM),
        cost_estimate=pl.CostEstimate(
            flops=3_200_000_000, bytes_accessed=12_000_000, transcendentals=1000
        ),
        name="project",
    )(core, feed, gain, *far(pinned, own, other))


def gate_kernel(
    mixed, run, query, entering, gate, gain, out_own, out_other, grad, mixed_out, sums0, sums1,
    sums2, sums3, sent0, sent1, sent2, sent3, entered
):
    k = pl.program_id(0)
    entered[...] = dot(query[...], entering[...])
    inner = jnp.zeros((PIECE, 1), f32)
    decay = jnp.exp(run[...])
    first = lanes((PIECE, 128)) < 64
    total = jnp.zeros((PIECE, 1), f32)
    normed = []
    for j in range(PAIRS):
        cols = slice(128 * j, 128 * j + 128)
        y = mixed[:, cols] + spread(decay, j, first) * entered[:, cols]
        mixed_out[:, cols] = y
        pre = gate[:, cols].astype(f32)
        gated = y.astype(bf16).astype(f32) * (pre * jax.nn.sigmoid(pre))
        total = total + jnp.sum(gated * gated, axis=1, keepdims=True)
        scaled = gated * gain[0:1, cols]
        inner = inner + jnp.sum(scaled * grad[:, cols], axis=1, keepdims=True)
        normed.append(scaled.astype(bf16))
    lane = lanes((PIECE, 128))
    both = jnp.where(lane == 0, total, jnp.where(lane == 1, inner, 0.0)).T[0:8]
    for sums in (sums0, sums1, sums2, sums3):
        sums[...] = both
    part = dot(jnp.concatenate(normed[:3], axis=1), out_own[...])
    part = part + dot(jnp.concatenate(normed[3:], axis=1), out_other[...])
    high = total.astype(bf16).astype(f32)
    split = jnp.where(lane == 0, high, jnp.where(lane == 1, total - high, 0.0))
    for index, sent in enumerate((sent0, sent1, sent2, sent3)):

        @pl.when(k == index)
        def _():
            sent[:, :D] = part.astype(sent.dtype)
            sent[:, D:] = split.astype(sent.dtype)


def gate_out(mixed, run, query, entering, gate, gain, out_own, out_other, grad):
    tokens = mixed.shape[0]

    def whole(shape):
        return pl.BlockSpec(shape, lambda k: (0, 0))

    def piece(width):
        return pl.BlockSpec((PIECE, width), lambda k: (k, 0))

    return pl.pallas_call(
        gate_kernel,
        grid=(tokens // PIECE,),
        in_specs=[
            piece(GROUP),
            piece(128),
            piece(N),
            whole((N, GROUP)),
            piece(GROUP),
            whole((8, GROUP)),
            whole((HALF, D)),
            whole((HALF, D)),
            piece(GROUP),
        ],
        out_specs=[piece(GROUP)]
        + [pl.BlockSpec((8, PIECE), lambda k, by=by: (0, lax.rem(k + by, 4))) for by in range(4)]
        + [whole((PIECE, D + 128))] * 4,
        out_shape=[stored((tokens, GROUP), f32)]
        + [stored((8, tokens), f32)] * 4
        + [stored((PIECE, D + 128), f32 if k == 0 else bf16) for k in range(4)],
        scratch_shapes=[pltpu.VMEM((PIECE, GROUP), f32)],
        compiler_params=pltpu.CompilerParams(vmem_limit_bytes=VMEM),
        cost_estimate=pl.CostEstimate(
            flops=1_300_000_000, bytes_accessed=9_000_000, transcendentals=400_000
        ),
        name="gate_out",
    )(mixed, run, query, entering, gate, gain, out_own, out_other, grad)


def scales_kernel(one, two, three, four, scale):
    total = one[...] + two[...] + three[...] + four[...]
    lane = lanes((PIECE, 128))
    for k in range(total.shape[1] // PIECE):
        block = total[:, PIECE * k : PIECE * k + PIECE]
        columns = jnp.concatenate([block, jnp.zeros((120, PIECE), f32)], axis=0).T
        s_out = lax.rsqrt(columns[:, 0:1] / DI + epsilon)
        mean = s_out * columns[:, 1:2] / DI
        scale[PIECE * k : PIECE * k + PIECE] = (
            split_pair(s_out, lane, 0) + split_pair(mean, lane, 2)
        ).astype(bf16)


def scales(parts):
    tokens = parts[0].shape[1]
    return pl.pallas_call(
        scales_kernel,
        out_shape=jax.ShapeDtypeStruct((tokens, 128), bf16),
        cost_estimate=pl.CostEstimate(
            flops=1_000_000, bytes_accessed=200_000, transcendentals=1000
        ),
        name="scales",
    )(*parts)


def out_back_kernel(grad_new, out_own, out_other, product):
    product[:, :HALF] = dot_nt(grad_new[...], out_own[...])
    product[:, HALF:] = dot_nt(grad_new[...], out_other[...])


def out_back(grad_new, out_own, out_other):
    tokens = grad_new.shape[0]
    return pl.pallas_call(
        out_back_kernel,
        out_shape=jax.ShapeDtypeStruct((tokens, GROUP), f32),
        compiler_params=pltpu.CompilerParams(vmem_limit_bytes=VMEM),
        cost_estimate=pl.CostEstimate(
            flops=1_200_000_000, bytes_accessed=5_500_000, transcendentals=0
        ),
        name="out_back",
    )(grad_new, out_own, out_other)


def gate_back_kernel(
    product, gate, mixed, scale, run, query, gain, decay, grad_scan, grad_gate, normed, packed, state
):
    k = pl.program_id(0)

    @pl.when(k == 0)
    def _():
        state[...] = jnp.zeros_like(state)
    grown = jnp.exp(run[...])
    queries_t = query[...].astype(f32).T.astype(bf16)
    first = lanes((PIECE, 128)) < 64
    parts = scale[...].astype(f32)
    s_out, mean = parts[:, 0:1] + parts[:, 1:2], parts[:, 2:3] + parts[:, 3:4]
    row16 = rows((16, 128))
    for j in range(PAIRS):
        cols = slice(128 * j, 128 * j + 128)
        grad = product[:, cols]
        pre = gate[:, cols].astype(f32)
        sig = jax.nn.sigmoid(pre)
        out = mixed[:, cols].astype(bf16).astype(f32)
        unit = out * (pre * sig) * s_out
        gain_j = gain[0:1, cols]
        gated = s_out * (grad * gain_j - unit * mean)
        scan = (gated * (pre * sig)).astype(bf16)
        grad_scan[:, cols] = scan
        grad_gate[:, cols] = (gated * out * sig * (1.0 + pre * (1.0 - sig))).astype(bf16)
        normed[:, cols] = (unit * gain_j).astype(bf16)
        total = state[:, cols] + dot(queries_t, spread(grown, j, first) * scan.astype(f32))
        state[:, cols] = total
        packed[0:N, cols] = total.astype(bf16)
        fall = jnp.broadcast_to(decay[0:1, cols], (16, 128))
        high = fall.astype(bf16).astype(f32)
        packed[N : N + 16, cols] = jnp.where(
            row16 == 0, high, jnp.where(row16 == 1, fall - high, 0.0)
        ).astype(bf16)


def gate_back(product, gate, mixed, scale, run, query, gain, decay, pinned):
    tokens = mixed.shape[0]

    def whole(shape):
        return pl.BlockSpec(shape, lambda k: (0, 0))

    def piece(width):
        return pl.BlockSpec((PIECE, width), lambda k: (k, 0))

    return pl.pallas_call(
        gate_back_kernel,
        grid=(tokens // PIECE,),
        in_specs=[
            piece(GROUP),
            piece(GROUP),
            piece(GROUP),
            piece(128),
            piece(128),
            piece(N),
            whole((8, GROUP)),
            whole((8, GROUP)),
        ],
        out_specs=[piece(GROUP), piece(GROUP), piece(GROUP), whole((N + 16, GROUP))],
        out_shape=[
            jax.ShapeDtypeStruct((tokens, GROUP), bf16),
            jax.ShapeDtypeStruct((tokens, GROUP), bf16),
            jax.ShapeDtypeStruct((tokens, GROUP), bf16),
            stored((N + 16, GROUP), bf16),
        ],
        scratch_shapes=[pltpu.VMEM((N, GROUP), f32)],
        compiler_params=pltpu.CompilerParams(vmem_limit_bytes=VMEM),
        cost_estimate=pl.CostEstimate(
            flops=120_000_000, bytes_accessed=8_000_000, transcendentals=400_000
        ),
        name="gate_back",
    )(product, *far(pinned, gate, mixed), scale, *far(pinned, run, query), gain, decay)


def scan_back_kernel(
    place, conv_in, pre_in, step, run, grad, grad_gate, mixed, starts, last, entering, leaving, rim,
    taps, hp, skip, use_own, use_other, tail, rim_grad, laid, act, delta, state, after, skip_sum,
    product, flows, weighted, ended, grad_taps, grad_hp, spots
):
    k = pl.program_id(0)
    count = pl.num_programs(0)
    first = lanes((PIECE, 128)) < 64
    first_row = lanes((1, 128)) < 64
    raw, sizes, log_decay = step_parts(step[...], hp[...])
    running = run[...]
    start = running[0:1] - log_decay[0:1]
    end = running[PIECE - 1 : PIECE]
    from_start = jnp.exp(running - start)
    to_end = jnp.exp(end - running)
    whole = jnp.exp(end - start)
    before_all = jnp.exp(start)
    until_end = jnp.exp(end)

    @pl.when(k == 0)
    def _():
        delta[PIECE : PIECE + 8] = jnp.zeros((8, ACT), f32)
        grad_taps[...] = jnp.zeros_like(grad_taps)
        grad_hp[...] = jnp.zeros_like(grad_hp)
        skip_sum[...] = jnp.zeros_like(skip_sum)
        for j in range(PAIRS):
            cols = slice(128 * j, 128 * j + 128)
            state[:, cols] = leaving[:, cols]
            after[:, cols] = spread(until_end, j, first_row) * entering[:, cols] + last[:, cols]

    @pl.when(k > 0)
    def _():
        delta[PIECE : PIECE + 8] = delta[0:8]

    for j in range(ACT // 128):
        cols = slice(128 * j, 128 * j + 128)
        pre = pre_in[:, cols]
        act[:, cols] = pre * jax.nn.sigmoid(pre)

    upper = rows((PIECE, PIECE)) <= lanes((PIECE, PIECE))
    keys = act[:, GROUP : GROUP + N].astype(bf16)
    queries32 = act[:, GROUP + N :]
    queries = queries32.astype(bf16)
    queries_t = queries32.T.astype(bf16)
    affinity = jnp.where(upper, dot_nt(keys, queries), 0.0)
    running_t = running.T
    grad_affinity = jnp.zeros((PIECE, PIECE), f32)
    product[...] = dot(keys, state[...])
    for j in range(PAIRS):
        cols = slice(128 * j, 128 * j + 128)
        x = act[:, cols]
        sizes_j = spread(sizes, j, first)
        scaled = x * sizes_j
        dm = grad[:, cols]
        dm32 = dm.astype(f32)
        to_end_j = spread(to_end, j, first)
        gaps = [
            jnp.exp(jnp.minimum(running_t[h : h + 1, :] - running[:, h : h + 1], 0.0))
            for h in (2 * j, 2 * j + 1)
        ]
        z = to_end_j * product[:, cols] + dot(
            jnp.concatenate([gap * affinity for gap in gaps], axis=1), apart(dm32, first)
        )
        crossed = dot_nt(apart(scaled, first), dm)
        grad_affinity = grad_affinity + gaps[0] * crossed[:PIECE] + gaps[1] * crossed[PIECE:]
        skip_j = skip[0:1, cols]
        delta[0:PIECE, cols] = sizes_j * z + skip_j * dm32
        skip_sum[0:1, cols] += jnp.sum(dm32 * x, axis=0, keepdims=True)
        flows[0:PIECE, cols] = x * z
        flows[PIECE : 2 * PIECE, cols] = dm32 * (mixed[:, cols] - skip_j * x)
        inside = jnp.sum(state[:, cols] * after[:, cols], axis=0, keepdims=True)
        flows[2 * PIECE :, cols] = jnp.broadcast_to(inside, (16, 128))
        after[:, cols] = spread(before_all, j, first_row) * entering[:, cols] + starts[
            0, :, cols
        ].astype(f32)
        weighted[:, cols] = (spread(from_start, j, first) * dm32).astype(bf16)
        ended[:, cols] = (scaled * to_end_j).astype(bf16)
    heads = (lanes((GROUP, 128)) == lax.shift_right_logical(rows((GROUP, 128)), 6)).astype(bf16)
    sums = dot_split(flows[...], heads)
    inner_sum, outer_sum = sums[:PIECE], sums[PIECE : 2 * PIECE]
    bound = sums[2 * PIECE :]
    grad_queries = dot_nt(weighted[...], after[...])
    grad_keys = dot_nt(ended[...], state[...])
    product[...] = dot(queries_t, weighted[...])
    for j in range(PAIRS):
        cols = slice(128 * j, 128 * j + 128)
        state[:, cols] = spread(whole, j, first_row) * state[:, cols] + product[:, cols]
    grad_affinity = jnp.where(upper, grad_affinity, 0.0)
    delta[0:PIECE, GROUP : GROUP + N] = grad_keys + dot(grad_affinity, queries)
    delta[0:PIECE, GROUP + N :] = grad_queries + dot(grad_affinity.T, keys)

    flow = outer_sum - sizes * inner_sum
    grad_log = bound[0:1] + jnp.dot(
        upper.astype(f32), flow, precision=HIGHEST, preferred_element_type=f32
    )
    rate = jnp.exp(hp[1:2])
    live = lanes((PIECE, 128)) < HEADS
    grad_raw = jnp.where(live, (inner_sum - rate * grad_log) * jax.nn.sigmoid(raw), 0.0)
    is_first = place[1] == 0
    edge = HALF + EXTRA
    step_first = jnp.where(is_first, grad_raw, 0.0)
    step_second = jnp.where(is_first, 0.0, grad_raw)
    for use, gate_cols in ((use_own, slice(0, HALF)), (use_other, slice(HALF, GROUP))):
        use[:, edge:] = grad_gate[:, gate_cols]

    @pl.when(k == 0)
    def _():
        for side, gate_cols in ((0, slice(0, HALF)), (1, slice(HALF, GROUP))):
            tail[:, WIDE * side + edge : WIDE * side + WIDE] = grad_gate[
                PIECE - 16 :, gate_cols
            ].astype(f32)[8:]
    grad_hp[0:1] += jnp.sum(grad_raw, axis=0, keepdims=True)
    grad_hp[1:2] += jnp.sum(jnp.where(live, grad_log * log_decay, 0.0), axis=0, keepdims=True)

    for j in range(ACT // 128):
        cols = slice(128 * j, 128 * j + 128)
        pre = pre_in[:, cols]
        sig = jax.nn.sigmoid(pre)
        grown = delta[0:PIECE, cols] * sig * (1.0 + pre * (1.0 - sig))
        delta[0:PIECE, cols] = grown
        grad_taps[4:5, cols] += jnp.sum(grown, axis=0, keepdims=True)
        taken = conv_in[:, cols].astype(f32)
        total = jnp.zeros((PIECE, 128), f32)
        for t in range(4):
            moved = delta[3 - t : 3 - t + PIECE, cols]
            total = total + taps[t : t + 1, cols] * moved
            grad_taps[t : t + 1, cols] += jnp.sum(taken * moved, axis=0, keepdims=True)
        if j < PAIRS:
            use = use_own if j < 3 else use_other
            at = 128 * (j % 3)
            use[:, at : at + 128] = total.astype(bf16)
            targets = [(WIDE * (j // 3) + at, total)]
        else:
            at = HALF + 128 * (j - PAIRS)
            slot = step_first if j == PAIRS else step_second
            first_use = jnp.where(is_first, total, slot)
            second_use = jnp.where(is_first, slot, total)
            use_own[:, at : at + 128] = first_use.astype(bf16)
            use_other[:, at : at + 128] = second_use.astype(bf16)
            targets = [(at, first_use), (WIDE + at, second_use)]

        @pl.when(k == 0)
        def _():
            for at, values in targets:
                tail[:, at : at + 128] = values[PIECE - 8 :]

    @pl.when(k == count - 1)
    def _():
        for j in range(PAIRS):
            cols = slice(128 * j, 128 * j + 128)
            heads = (lanes((128, 128)) == 2 * j + (rows((128, 128)) >= 64)).astype(bf16)
            sums = dot_split(jnp.broadcast_to(skip_sum[0:1, cols], (8, 128)), heads)
            grad_hp[2:3] += sums[0:1]
        for j in range(ACT // 128):
            cols = slice(128 * j, 128 * j + 128)
            border = jnp.concatenate([jnp.zeros((8, 128), f32), delta[0:8, cols]], axis=0)
            taken = rim[:, cols].astype(f32)
            total = jnp.zeros((8, 128), f32)
            for t in range(4):
                moved = border[3 - t : 11 - t]
                total = total + taps[t : t + 1, cols] * moved
                grad_taps[t : t + 1, cols] += jnp.sum(taken * moved, axis=0, keepdims=True)
            if j < PAIRS:
                at = WIDE * (j // 3) + 128 * (j % 3)
                rim_grad[:, at : at + 128] = total
            else:
                at = HALF + 128 * (j - PAIRS)
                rim_grad[:, at : at + 128] = jnp.where(is_first, total, 0.0)
                rim_grad[:, WIDE + at : WIDE + at + 128] = jnp.where(is_first, 0.0, total)
        for side in range(2):
            rim_grad[:, WIDE * side + edge : WIDE * side + WIDE] = jnp.zeros((8, HALF), f32)
        spots[...] = jnp.zeros_like(spots)
        for j in range(PAIRS):
            half = 2 * place[0] + (place[1] if j < 3 else 1 - place[1])
            at = pl.ds(pl.multiple_of(half * HALF + 128 * (j % 3), 128), 128)
            spots[:, at] = grad_taps[:, 128 * j : 128 * j + 128]
        spots[:, DI : DI + 2 * N] = grad_taps[:, GROUP:]
        lane = lanes((8, 128))
        sums = grad_hp[...]
        crossed = jnp.where(lane < 6, pltpu.roll(sums, 122, 1), pltpu.roll(sums, 6, 1))
        sums = pltpu.roll(jnp.where(is_first, sums, crossed), SMALL_AT, 1)
        sums = pltpu.roll(sums, 5, 0)
        is_sum = (rows((8, 128)) >= 5) & (lane >= SMALL_AT) & (lane < SMALL_AT + HEADS)
        is_tap = (rows((8, 128)) < 5) & (lane >= SMALL_AT) & (lane < SMALL_AT + 52)
        sums = jnp.where(is_sum, sums, 0.0)
        laid[...] = jnp.zeros_like(laid)
        for d in range(64):
            at = 52 * d // 128 * 128
            window = pltpu.roll(spots[:, at : at + 256], (256 + SMALL_AT - 52 * d + at) % 256, 1)
            laid[24 * d : 24 * d + 8] = jnp.where(is_tap, window[:, :128], sums)


def scan_back(
    place, conv_in, pre, step, run, grad, grad_gate, mixed, starts, last, entering, leaving, rim,
    taps, hp, skip, pinned
):
    tokens = conv_in.shape[0]
    count = tokens // PIECE

    def whole(shape):
        return pl.BlockSpec(shape, lambda k, place: (0,) * len(shape))

    def piece(width):
        return pl.BlockSpec((PIECE, width), lambda k, place: (turned(count - 1 - k, place), 0))

    return pl.pallas_call(
        scan_back_kernel,
        grid_spec=pltpu.PrefetchScalarGridSpec(
            num_scalar_prefetch=1,
            grid=(count,),
            in_specs=[
                piece(ACT),
                piece(ACT),
                piece(128),
                piece(128),
                piece(GROUP),
                piece(GROUP),
                piece(GROUP),
                pl.BlockSpec((1, N, GROUP), lambda k, place: (count - 1 - k, 0, 0)),
                whole((N, GROUP)),
                whole((N, GROUP)),
                whole((N, GROUP)),
                whole((8, ACT)),
                whole((8, ACT)),
                whole((8, 128)),
                whole((8, GROUP)),
            ],
            out_specs=[
                piece(WIDE),
                piece(WIDE),
                whole((8, 2 * WIDE)),
                whole((8, 2 * WIDE)),
                whole((D, 128)),
            ],
            scratch_shapes=[
                pltpu.VMEM((PIECE, ACT), f32),
                pltpu.VMEM((PIECE + 8, ACT), f32),
                pltpu.VMEM((N, GROUP), f32),
                pltpu.VMEM((N, GROUP), f32),
                pltpu.VMEM((8, GROUP), f32),
                pltpu.VMEM((PIECE, GROUP), f32),
                pltpu.VMEM((2 * PIECE + 16, GROUP), f32),
                pltpu.VMEM((PIECE, GROUP), bf16),
                pltpu.VMEM((PIECE, GROUP), bf16),
                pltpu.VMEM((8, ACT), f32),
                pltpu.VMEM((8, 128), f32),
                pltpu.VMEM((8, DI + 2 * N + 128), f32),
            ],
        ),
        out_shape=[
            jax.ShapeDtypeStruct((tokens, WIDE), bf16),
            jax.ShapeDtypeStruct((tokens, WIDE), bf16),
            jax.ShapeDtypeStruct((8, 2 * WIDE), f32),
            jax.ShapeDtypeStruct((8, 2 * WIDE), f32),
            jax.ShapeDtypeStruct((D, 128), f32),
        ],
        compiler_params=pltpu.CompilerParams(vmem_limit_bytes=VMEM),
        cost_estimate=pl.CostEstimate(
            flops=2_000_000_000, bytes_accessed=9_000_000, transcendentals=2_500_000
        ),
        name="scan_back",
    )(place, *far(pinned, conv_in, pre, step, run), grad, grad_gate,
      *far(pinned, mixed, starts, last, entering), leaving, rim, taps, hp, skip)


def parts_kernel(use_own, use_other, own, other, sent0, sent1, sent2, sent3):
    part = dot_nt(use_own[...], own[...]) + dot_nt(use_other[...], other[...])
    for index, sent in enumerate((sent0, sent1, sent2, sent3)):
        sent[...] = part[PIECE * index : PIECE * index + PIECE].astype(sent.dtype)


def project_back(use_own, use_other, own, other, pinned):
    tokens = use_own.shape[0]
    width = 256

    def whole(shape):
        return pl.BlockSpec(shape, lambda k: (0, 0))

    return pl.pallas_call(
        parts_kernel,
        grid=(D // width,),
        in_specs=[whole((tokens, WIDE))] * 2 + [pl.BlockSpec((width, WIDE), lambda k: (k, 0))] * 2,
        out_specs=[pl.BlockSpec((PIECE, width), lambda k: (0, k))] * 4,
        out_shape=[stored((PIECE, D), f32 if k == 0 else bf16) for k in range(4)],
        compiler_params=pltpu.CompilerParams(vmem_limit_bytes=VMEM),
        cost_estimate=pl.CostEstimate(
            flops=3_200_000_000, bytes_accessed=9_000_000, transcendentals=0
        ),
        name="project_back",
    )(use_own, use_other, *far(pinned, own, other))


def early_kernel(normed, grad_gate, normed_out, grad_new, own, other, sums):
    i = pl.program_id(0)

    @pl.when(i == 0)
    def _():
        sums[0] = dot_tn(normed_out[:, :HALF], grad_new[...])
        sums[1] = dot_tn(normed_out[:, HALF:], grad_new[...])

    block = dot_tn(normed[...], grad_gate[...])
    for side, sent in enumerate((own, other)):
        sent[:, :HALF] = block[:, HALF * side : HALF * side + HALF].astype(bf16)
        for s in range(4):
            row = pl.ds(pl.multiple_of(96 * i + 24 * s, 8), 24)
            pieces = [sums[side, row, HALF * q : HALF * q + HALF] for q in range(4)]
            sent[96 * s : 96 * s + 96, HALF:] = jnp.concatenate(pieces, axis=0).astype(bf16)


def early_grads(normed, grad_gate, normed_out, grad_new):
    tokens = normed.shape[0]

    def whole(shape):
        return pl.BlockSpec(shape, lambda i: (0, 0))

    return pl.pallas_call(
        early_kernel,
        grid=(4,),
        in_specs=[
            pl.BlockSpec((tokens, HALF), lambda i: (0, i)),
            whole((tokens, GROUP)),
            whole((tokens, GROUP)),
            whole((tokens, D)),
        ],
        out_specs=[pl.BlockSpec((HALF, GROUP), lambda i: (i, 0))] * 2,
        out_shape=[stored((D, GROUP), bf16)] * 2,
        scratch_shapes=[pltpu.VMEM((2, HALF, D), f32)],
        compiler_params=pltpu.CompilerParams(vmem_limit_bytes=VMEM),
        cost_estimate=pl.CostEstimate(
            flops=2_400_000_000, bytes_accessed=9_000_000, transcendentals=0
        ),
        name="early_grads",
    )(normed, grad_gate, normed_out, grad_new)


def inner_kernel(place, normed, use_own, use_other, slot, own, other):
    is_first = place[1] == 0
    for use, sent, holds in ((use_own, own, ~is_first), (use_other, other, is_first)):
        block = dot_tn(normed[...], use[...])
        sent[:, :HALF] = block[:, :HALF].astype(bf16)
        middle = block[:, HALF : HALF + 128] + jnp.where(holds, slot[...], 0.0)
        sent[:, HALF : HALF + 128] = middle.astype(bf16)
        sent[:, HALF + 128 :] = block[:, HALF + 128 :].astype(bf16)


def inner_grads(place, normed, use_own, use_other, slot):
    tokens = normed.shape[0]
    edge = HALF + EXTRA

    def whole(shape):
        return pl.BlockSpec(shape, lambda i, place: (0, 0))

    return pl.pallas_call(
        inner_kernel,
        grid_spec=pltpu.PrefetchScalarGridSpec(
            num_scalar_prefetch=1,
            grid=(4,),
            in_specs=[
                pl.BlockSpec((tokens, HALF), lambda i, place: (0, i)),
                whole((tokens, edge)),
                whole((tokens, edge)),
                pl.BlockSpec((HALF, 128), lambda i, place: (i, 0)),
            ],
            out_specs=[pl.BlockSpec((HALF, edge), lambda i, place: (i, 0))] * 2,
        ),
        out_shape=[stored((D, edge), bf16)] * 2,
        compiler_params=pltpu.CompilerParams(vmem_limit_bytes=VMEM),
        cost_estimate=pl.CostEstimate(
            flops=2_000_000_000, bytes_accessed=7_000_000, transcendentals=0
        ),
        name="inner_grads",
    )(place, normed, use_own, use_other, slot)


def split_pair(values, lane, at):
    high = values.astype(bf16).astype(f32)
    return jnp.where(lane == at, high, jnp.where(lane == at + 1, values - high, 0.0))


def receive_kernel(part, one, two, three, feed, target, branch_out, result, scale):
    total = part[...] + one[...].astype(f32) + two[...].astype(f32) + three[...].astype(f32)
    square = total[:, D : D + 1] + total[:, D + 1 : D + 2]
    s_out = lax.rsqrt(square / DI + epsilon)
    branch = s_out * total[:, :D]
    branch_out[...] = branch
    result[...] = (feed[...].astype(f32) + branch).astype(bf16)
    mean = jnp.sum(branch * target[...].astype(f32), axis=1, keepdims=True) / DI
    lane = lanes((PIECE, 128))
    scale[...] = (split_pair(s_out, lane, 0) + split_pair(mean, lane, 2)).astype(bf16)


def receive(parts, feed, target):
    return pl.pallas_call(
        receive_kernel,
        out_shape=[
            stored((PIECE, D), f32),
            jax.ShapeDtypeStruct((PIECE, D), bf16),
            jax.ShapeDtypeStruct((PIECE, 128), bf16),
        ],
        compiler_params=pltpu.CompilerParams(vmem_limit_bytes=VMEM),
        cost_estimate=pl.CostEstimate(
            flops=3_000_000, bytes_accessed=4_500_000, transcendentals=1000
        ),
        name="receive",
    )(*parts, feed, target)


def receive_back_kernel(
    part, one, two, three, feed, grad_new, gain, branch, scale_in, grad_out, scale_out
):
    total = part[...] + one[...].astype(f32) + two[...].astype(f32) + three[...].astype(f32)
    values = feed[...].astype(f32)
    s_in = lax.rsqrt(jnp.mean(values * values, axis=1, keepdims=True) + epsilon)
    unit = values * s_in
    grad_unit = total * gain[0:1]
    grad = grad_new[...].astype(f32) + s_in * (
        grad_unit - unit * jnp.mean(unit * grad_unit, axis=1, keepdims=True)
    )
    low = grad.astype(bf16)
    grad_out[...] = low
    mean = jnp.sum(branch[...] * low.astype(f32), axis=1, keepdims=True) / DI
    lane = lanes((PIECE, 128))
    kept = jnp.where(lane < 2, scale_in[...].astype(f32), 0.0)
    scale_out[...] = (kept + split_pair(mean, lane, 2)).astype(bf16)


def receive_back(parts, feed, grad_new, gain, branch, scale):
    return pl.pallas_call(
        receive_back_kernel,
        out_shape=[
            jax.ShapeDtypeStruct((PIECE, D), bf16),
            jax.ShapeDtypeStruct((PIECE, 128), bf16),
        ],
        compiler_params=pltpu.CompilerParams(vmem_limit_bytes=VMEM),
        cost_estimate=pl.CostEstimate(
            flops=4_000_000, bytes_accessed=4_500_000, transcendentals=1000
        ),
        name="receive_back",
    )(*parts, feed, grad_new, gain, branch, scale)


def pick(core, first, second):
    return jnp.where(core == 0, first, second)


def spread_weights(core, head, gate_inner, shared_bc, step_proj):
    gate = gate_inner[:, :DI].reshape(24, 4, 2, HALF)
    inner = gate_inner[:, DI:].reshape(24, 4, 2, HALF)
    heads = step_proj.reshape(24, 4, HEADS)
    fill = jnp.zeros((24, 128 - HEADS), bf16)
    halves = []
    for q in range(2):
        pieces = []
        for g in range(4):
            own = heads[:, g]
            slot = [own, fill, own[:, 6:], own[:, :6], fill]
            extra = [shared_bc] if q == 0 else slot
            pieces.append(jnp.concatenate([inner[:, g, q]] + extra + [gate[:, g, q]], axis=1))
        halves.append(jnp.stack(pieces))
    kept = pick(core, halves[0], halves[1])
    got = swap(pick(core, halves[1], halves[0]))
    layers = [pick(core, kept, got), pick(core, got, kept)]
    return [exchange_head(values, head).reshape(96, WIDE) for values in layers]


def out_pairs():
    pairs = []
    for layer in range(2):
        for z in range(4):
            for y in range(4):
                for x in range(4):
                    source = (layer * 16 + z * 4 + y) * 4 + x
                    place = layer * 8 + (y % 2) * 4 + x
                    pairs.append((source, ((y // 2) * 16 + place) * 4 + z))
    return pairs


def out_back_pairs(part):
    pairs = []
    for core in range(2):
        for place in range(16):
            layer = (place + part) % 2
            for group in range(4):
                j = place // 2
                target = (layer * 16 + group * 4 + 2 * core + j // 4) * 4 + j % 4
                pairs.append(((core * 16 + place) * 4 + group, target))
    return pairs


EVERY = ("section", "seq", "head")


def gather_seq(a):
    return lax.all_gather(a, "seq", axis=0, tiled=True)


def gather_small(core, a):
    other = swap(a)
    both = jnp.concatenate([pick(core, a, other), pick(core, other, a)], axis=1)
    width = a.shape[1]
    both = jnp.pad(both.reshape(2 * width // 128, 128), ((0, 8 - 2 * width // 128), (0, 0)))
    sent = jnp.broadcast_to(both[None], (64, 8, 128)).reshape(512, 128)
    got = lax.all_to_all(sent, ("seq", "head"), 0, 0, tiled=True).reshape(64, 1024)
    return got[:, :width], got[:, width : 2 * width]


def layer_params(core, head, small, per_head):
    gain_in = small[:, :24].reshape(1, D)
    conv = small[:, 24:232].reshape(64, 4, 52).transpose(1, 0, 2).reshape(4, DI + 2 * N)
    bias = small[:, 232:284].reshape(1, DI + 2 * N)
    gain = small[:, 284:332].reshape(1, DI)
    taps = jnp.concatenate([conv, bias, jnp.zeros((3, DI + 2 * N), f32)], axis=0)

    def grouped(values, width):
        own = lax.dynamic_slice_in_dim(values, (2 * head + core) * width, width, 1)
        other = lax.dynamic_slice_in_dim(values, (2 * head + 1 - core) * width, width, 1)
        return [own, other]

    taps = jnp.concatenate(grouped(taps, HALF) + [taps[:, DI:]], axis=1)
    gain = jnp.broadcast_to(jnp.concatenate(grouped(gain, HALF), axis=1), (8, GROUP))
    per_head = jnp.concatenate(grouped(per_head, 6), axis=1)
    hp = jnp.pad(per_head, ((0, 5), (0, 128 - HEADS)))
    skip = jnp.broadcast_to(jnp.repeat(per_head[2:3], 64, axis=1), (8, GROUP))
    return dict(
        taps=taps, gain=gain, hp=hp, skip=skip, gain_in=jnp.broadcast_to(gain_in, (8, D))
    )


def tied(values, anchor):
    return lax.optimization_barrier((values, anchor))[0]


def layer_forward(core, head, feed, feed_all, weights, out_weights, first):
    place = jnp.stack([head, core])
    own, other = weights["own"], weights["other"]
    normed, conv_in, step, gate = project(core.reshape(1), feed_all, weights["gain_in"], own, other, first
    )
    last_row = PIECE * lax.rem(7 - head, 4) + PIECE - 8
    rim = lax.ppermute(
        lax.dynamic_slice_in_dim(conv_in, last_row, 8, 0), "seq", [(i, i + 1) for i in range(15)]
    )
    pre, mixed0, query, run, starts, last, packed = scan_local(
        place, conv_in, step, rim, weights["taps"], weights["hp"], weights["skip"], first
    )
    entering = carried(packed, -1)
    entering, out_own, out_other, product = out_weights(packed, entering)
    mixed, *sums_and_sent = gate_out(
        mixed0, run, query, entering, gate, weights["gain"], out_own, out_other,
        mixed0 if product is None else product,
    )
    kept = dict(
        feed=feed, normed=normed, gate=gate, conv_in=conv_in, rim=rim, step=step, pre=pre,
        mixed=mixed, query=query, run=run, starts=starts, last=last, entering=entering,
        packed=packed, out_own=out_own, out_other=out_other,
    )
    return sums_and_sent[:4], sums_and_sent[4:], kept


def layer_backward(
    core, head, incoming, gathered, product, scale, kept, below, weights, after_gate, before_receive,
    inner_first,
):
    place = jnp.stack([head, core])
    own, other = weights["own"], weights["other"]
    decay = jnp.broadcast_to(
        kept["packed"][N : N + 1].astype(f32) + kept["packed"][N + 1 : N + 2].astype(f32),
        (8, GROUP),
    )
    grad_scan, grad_gate, normed_out, packed = gate_back(
        product, kept["gate"], kept["mixed"], scale, kept["run"], kept["query"], weights["gain"],
        decay, not inner_first,
    )
    leaving = carried(packed, 1)
    normed = kept["normed"]
    early, leaving = after_gate(
        early_grads(normed, grad_gate, normed_out, gathered), packed, leaving
    )
    use_own, use_other, tail, rim_grad, slot = scan_back(
        place, kept["conv_in"], kept["pre"], kept["step"], kept["run"], grad_scan, grad_gate,
        kept["mixed"], kept["starts"], kept["last"], kept["entering"], leaving, kept["rim"],
        weights["taps"], weights["hp"], weights["skip"], inner_first,
    )
    from_next = lax.ppermute(rim_grad, "seq", [(i + 1, i) for i in range(15)])
    last_row = PIECE * lax.rem(7 - head, 4) + PIECE - 8
    tail = (tail + from_next).astype(bf16)
    use_own = lax.dynamic_update_slice_in_dim(use_own, tail[:, :WIDE], last_row, 0)
    use_other = lax.dynamic_update_slice_in_dim(use_other, tail[:, WIDE:], last_row, 0)
    if inner_first:
        grad_x = summed(*inner_grads(place, normed, use_own, use_other, slot))
        use_own, use_other = tied((use_own, use_other), grad_x)
        sent = project_back(use_own, use_other, own, other, inner_first)
    else:
        sent = project_back(use_own, use_other, own, other, inner_first)
    grad_feed, scale_below = receive_back(
        before_receive(scatter_head(sent)), kept["feed"], incoming, weights["gain_in"], below["branch"],
        below["scale"],
    )
    if not inner_first:
        grad_x = inner_grads(place, normed, *tied((use_own, use_other), grad_feed), slot)
    return grad_feed, scale_below, grad_x, early


def summed(own, other):
    return (own.astype(f32) + swap(other).astype(f32)).astype(bf16)


def scatter_seq(a):
    return lax.psum_scatter(a, "seq", scatter_dimension=0, tiled=True)


def scatter_seq_now(a):
    got = lax.all_to_all(a, "seq", 0, 0, tiled=True).astype(f32)
    return jnp.sum(got.reshape(16, 96, a.shape[1]), axis=0).astype(bf16)


def per_device(
    tokens_in, cotangent, input_gain, gate_inner, shared_bc, step_proj, conv_weight, conv_bias,
    step_bias, decay_log, skip_gain, output_gain, out_proj
):
    core = lax.axis_index("section")
    head = lax.axis_index("head")
    tokens = lax.dynamic_index_in_dim(tokens_in, core, 0, False)
    grad_top = lax.dynamic_index_in_dim(cotangent, core, 0, False)
    edge = HALF + EXTRA

    pieces = spread_weights(core, head, gate_inner[0], shared_bc[0], step_proj[0])
    own0 = gather_seq(pieces[0])
    out_piece = lax.ppermute(out_proj[0], EVERY, out_pairs())
    small = jnp.concatenate(
        [input_gain, conv_weight[0].reshape(1, 208), conv_bias, output_gain], axis=1
    ).astype(f32)
    small = gather_small(core, tied(jnp.pad(small, ((0, 0), (0, 52))), pieces[0]))
    per_head = jnp.concatenate([step_bias, decay_log, skip_gain], axis=0)
    other_head = swap(tied(per_head, pieces[0]))
    head_values = [pick(core, per_head, other_head), pick(core, other_head, per_head)]
    weights = [layer_params(core, head, small[l], head_values[l]) for l in range(2)]
    feed_all = jnp.concatenate(gather_head(tied(tokens, pieces[0])), axis=0)
    feed_all, weights, own0, out_piece = lax.optimization_barrier(
        (feed_all, weights, own0, out_piece)
    )
    weights[0].update(own=own0, other=swap(own0))
    out = gather_seq(out_piece)
    own1 = gather_seq(tied(pieces[1], weights[0]["other"]))

    later = {}

    def out_first(packed, entering):
        mine = tied(out, packed)
        later["out"] = (mine, swap(mine))
        grad_all = jnp.concatenate(gather_head(tied(grad_top, packed)), axis=0)
        entering, later["grad_all"] = lax.optimization_barrier((entering, grad_all))
        return [entering] + [a[:HALF] for a in later["out"]] + [None]

    def out_second(packed, entering):
        mine, theirs = [a[HALF:] for a in later["out"]]
        later["product"] = out_back(tied(later["grad_all"], packed), mine, theirs)
        return [entering, mine, theirs, later["product"]]

    _, sent, kept0 = layer_forward(core, head, tokens, feed_all, weights[0], out_first, True)
    branch, hidden, scale = receive(scatter_head(sent), tokens, tokens)
    kept0.update(branch=branch, scale=scale)
    feed_all = jnp.concatenate(gather_head(hidden), axis=0)
    own1 = tied(own1, hidden)
    weights[1].update(own=own1, other=swap(own1))
    sums, sent, kept1 = layer_forward(core, head, hidden, feed_all, weights[1], out_second, False)
    sums = [sums[0]] + [from_head(sums[k], k) for k in (1, 3, 2)]
    scale = scales(sums)

    def after_gate1(values, packed, leaving):
        _, result, _ = receive(scatter_head(tied(sent, packed)), hidden, hidden)
        leaving, later["result"], values = lax.optimization_barrier(
            (leaving, result, summed(*values))
        )
        return values, leaving

    def before_receive1(sent):
        return sent

    grad_hidden, scale, grad_x1, early1 = layer_backward(
        core, head, grad_top, later["grad_all"], later["product"], scale, kept1, kept0, weights[1],
        after_gate1, before_receive1, False,
    )
    chunks = gather_head(jnp.concatenate([grad_hidden, scale], axis=1))
    later["early"] = scatter_seq_now(tied(early1, grad_hidden))
    chunks, grad_x1, later["early"] = lax.optimization_barrier((chunks, grad_x1, later["early"]))
    grad_all = jnp.concatenate([a[:, :D] for a in chunks], axis=0)
    scale = jnp.concatenate([a[:, D:] for a in chunks], axis=0)

    def after_gate0(values, packed, leaving):
        values = [jnp.concatenate([grad_x1[i], values[i]], axis=1) for i in range(2)]
        later["sum"] = summed(*values)
        return scatter_seq(later["sum"]), leaving

    def before_receive0(sent):
        return tied(sent, later["sum"])

    product = out_back(grad_all, kept0["out_own"], kept0["out_other"])
    grad_feed, _, grad_x0, early0 = layer_backward(
        core, head, grad_hidden, grad_all, product, scale, kept0, kept0, weights[0], after_gate0,
        before_receive0, True,
    )
    early1 = later["early"]
    x0 = scatter_seq_now(grad_x0)
    result = later["result"]
    got = swap(pick(core, result, hidden))
    layer_out = jnp.stack([pick(core, hidden, got), pick(core, got, result)])
    got = swap(pick(core, grad_hidden, grad_feed))
    grad_in = jnp.stack([pick(core, grad_feed, got), pick(core, got, grad_hidden)])

    def out_rows(a):
        return a.reshape(4, 24, HALF).transpose(1, 0, 2).reshape(24, D)

    out0, out1 = out_rows(early0[:, WIDE:]), out_rows(early1[:, HALF:])
    even = lax.rem(lax.axis_index("seq"), 2)
    rows_out = [
        lax.ppermute(pick(even, out0, out1), EVERY, out_back_pairs(0)),
        lax.ppermute(pick(even, out1, out0), EVERY, out_back_pairs(1)),
    ]
    grad_out = jnp.concatenate(
        [pick(core, rows_out[0], rows_out[1]), pick(core, rows_out[1], rows_out[0])], axis=0
    ).astype(f32)
    both = jnp.concatenate(
        [x0, early0[:, edge:WIDE], early0[:, :edge], early1[:, :HALF]], axis=1
    ).reshape(4, 24, 2 * WIDE)
    both = exchange_head(both, head)
    first, second = both[:, :, :WIDE], both[:, :, WIDE:]
    mine = pick(core, first, second)
    theirs = swap(pick(core, second, first))
    low, high = pick(core, mine, theirs).astype(f32), pick(core, theirs, mine).astype(f32)
    columns = []
    for start in (edge, 0):
        for g in range(4):
            for half in (low, high):
                columns.append(half[g, :, start : start + HALF])
    grad_gate_inner = jnp.concatenate(columns, axis=1)
    grad_shared = jnp.sum(low[:, :, HALF:edge], axis=0)
    slot, turned_slot = high[:, :, HALF : HALF + 128], high[:, :, HALF + 128 : edge]
    steps = slot[:, :, :HEADS] + jnp.concatenate(
        [turned_slot[:, :, 6:HEADS], turned_slot[:, :, :6]], axis=2
    )
    grad_step = jnp.concatenate([steps[g] for g in range(4)], axis=1)
    taps = jnp.sum(slot[:, :5, SMALL_AT : SMALL_AT + 52], axis=0)
    sums = slot[:, 5:8, SMALL_AT : SMALL_AT + HEADS].transpose(1, 0, 2).reshape(3, 48)
    grad_output_gain = jnp.sum(grad_out * out_proj[0].astype(f32), axis=1) / output_gain[0].astype(
        f32
    )
    grad_input_gain = (
        jnp.sum(grad_gate_inner * gate_inner[0].astype(f32), axis=1)
        + jnp.sum(grad_shared * shared_bc[0].astype(f32), axis=1)
        + jnp.sum(grad_step * step_proj[0].astype(f32), axis=1)
    ) / input_gain[0].astype(f32)
    return (
        layer_out[None],
        grad_in[None],
        grad_input_gain[None],
        grad_gate_inner[None],
        grad_shared[None],
        grad_step[None],
        taps[None, :4],
        taps[4:5],
        sums[0:1],
        sums[1:2],
        sums[2:3],
        grad_output_gain[None],
        grad_out[None],
    )


def solution(mesh):
    both = ("seq", "head")
    return jax.shard_map(
        per_device,
        mesh=mesh,
        in_specs=(
            P(None, both, None),
            P(None, both, None),
            P("section", both),
            P("section", both, None),
            P("section", both, None),
            P("section", both, None),
            P("section", None, both),
            P("section", both),
            P("section", None),
            P("section", None),
            P("section", None),
            P("section", both),
            P("section", both, None),
        ),
        out_specs=(
            P("section", None, both, None),
            P("section", None, both, None),
            P("section", both),
            P("section", both, None),
            P("section", both, None),
            P("section", both, None),
            P("section", None, both),
            P("section", both),
            P("section", None),
            P("section", None),
            P("section", None),
            P("section", both),
            P("section", both, None),
        ),
        check_vma=False,
    )
```

```python
import jax
import jax.numpy as jnp
from jax import lax
from jax.experimental import pallas as pl
from jax.experimental.pallas import tpu as pltpu
from jax.sharding import PartitionSpec as P

bf16 = jnp.bfloat16
f32 = jnp.float32
HIGHEST = lax.Precision.HIGHEST

D = 1536
DI = 3072
N = 128
GROUP = 768
HALF = 384
HEADS = 12
PIECE = 128
PAIRS = 6
EXTRA = 256
ACT = GROUP + 2 * N
WIDE = HALF + EXTRA + HALF
SMALL_AT = 32
VMEM = 24 * 1024 * 1024
epsilon = 1e-05


def from_head(a, k):
    return lax.ppermute(a, "head", [(i, (i - k) % 4) for i in range(4)])


def from_seq(a, dz, dy, wrap):
    pairs = []
    for z in range(4):
        for y in range(4):
            sz, sy = z + dz, y + dy
            if wrap:
                sz, sy = sz % 4, sy % 4
            if 0 <= sz < 4 and 0 <= sy < 4:
                pairs.append((sz * 4 + sy, z * 4 + y))
    return lax.ppermute(a, "seq", pairs)


def swap(a):
    return lax.ppermute(a, "section", [(0, 1), (1, 0)])


def gather_head(a):
    one, three = from_head(a, 1), from_head(a, 3)
    two = from_head(a, 2)
    return [a, one, two, three]


def scatter_head(parts):
    one, three = from_head(parts[1], 3), from_head(parts[3], 1)
    two = from_head(parts[2], 2)
    return [parts[0], one, two, three]


def exchange_head(parts, place):
    got = [lax.dynamic_index_in_dim(parts, place, 0, False)]
    for k in (1, 3, 2):
        sent = lax.dynamic_index_in_dim(parts, lax.rem(place + 4 - k, 4), 0, False)
        got.append(from_head(sent, k))
    got = [got[0], got[1], got[3], got[2]]
    twice = jnp.stack(got + got)
    return lax.dynamic_slice_in_dim(twice, lax.rem(4 - place, 4), 4, 0)


def unpack_state(a):
    decay = a[N : N + 1].astype(f32) + a[N + 1 : N + 2].astype(f32)
    return decay, a[:N].astype(f32)


def join(earlier, later):
    return earlier[0] * later[0], earlier[1] * later[0] + later[1]


def carried(packed, sign):
    seq = lax.axis_index("seq")
    y = lax.rem(seq, 4)
    ahead = y if sign < 0 else 3 - y
    near = {k: unpack_state(from_seq(packed, 0, sign * k, True)) for k in (1, 3, 2)}
    own = unpack_state(packed)
    before = (jnp.ones_like(own[0]), jnp.zeros_like(own[1]))
    after = own
    for k in (3, 2, 1):
        decay, state = near[k]
        use = k <= ahead
        before = join(before, (jnp.where(use, decay, 1.0), jnp.where(use, state, 0.0)))
        after = join(after, (jnp.where(use, 1.0, decay), jnp.where(use, 0.0, state)))
    whole = join(before, after)
    packed_whole = pack_state(whole[0], whole[1])
    far = {k: unpack_state(from_seq(packed_whole, sign * k, 0, False)) for k in (1, 3, 2)}
    total = jnp.zeros_like(own[1])
    for k in (3, 2, 1):
        decay, state = far[k]
        total = total * decay + state
    return total * before[0] + before[1]


def pack_state(decay, state):
    high = decay.astype(bf16)
    low = (decay - high.astype(f32)).astype(bf16)
    fill = jnp.zeros((14, state.shape[1]), bf16)
    return jnp.concatenate([state.astype(bf16), high, low, fill], axis=0)


def stored(shape, dtype):
    return pltpu.HBM(shape, dtype)


def far(pinned, *arrays):
    if not pinned:
        return list(arrays)
    return [pltpu.with_memory_space_constraint(a, pltpu.HBM) for a in arrays]


def dot(a, b):
    return jnp.dot(a.astype(bf16), b.astype(bf16), preferred_element_type=f32)


def dot_nt(a, b):
    return lax.dot_general(
        a.astype(bf16), b.astype(bf16), (((1,), (1,)), ((), ())), preferred_element_type=f32
    )


def dot_tn(a, b):
    return lax.dot_general(
        a.astype(bf16), b.astype(bf16), (((0,), (0,)), ((), ())), preferred_element_type=f32
    )


def dot_split(a, b):
    high = a.astype(bf16)
    low = (a - high.astype(f32)).astype(bf16)
    return dot(high, b) + dot(low, b)


def lanes(shape):
    return lax.broadcasted_iota(jnp.int32, shape, 1)


def rows(shape):
    return lax.broadcasted_iota(jnp.int32, shape, 0)


def spread(values, j, first):
    return jnp.where(first, values[:, 2 * j : 2 * j + 1], values[:, 2 * j + 1 : 2 * j + 2])


def apart(values, first):
    return jnp.concatenate(
        [jnp.where(first, values, 0.0), jnp.where(first, 0.0, values)], axis=0
    ).astype(bf16)


def step_parts(step, hp):
    raw = step + hp[0:1]
    live = lanes(raw.shape) < HEADS
    sizes = jnp.maximum(raw, 0.0) + jnp.log1p(jnp.exp(-jnp.abs(raw)))
    sizes = jnp.where(live, sizes, 0.0)
    return raw, sizes, -jnp.exp(hp[1:2]) * sizes


def scan_kernel(
    place, conv_in, step, rim, taps, hp, skip, pre_out, mixed, query, run, starts, last, packed,
    padded, act, state, carry, entered, weighted
):
    k = pl.program_id(0)

    @pl.when(k == 0)
    def _():
        state[...] = jnp.zeros_like(state)
        carry[...] = jnp.zeros_like(carry)
        padded[0:8] = rim[...].astype(f32)

    @pl.when(k > 0)
    def _():
        padded[0:8] = padded[PIECE : PIECE + 8]

    padded[8 : PIECE + 8] = conv_in[...].astype(f32)
    for j in range(ACT // 128):
        cols = slice(128 * j, 128 * j + 128)
        pre = taps[4:5, cols] + taps[0:1, cols] * padded[5 : PIECE + 5, cols]
        for t in range(1, 4):
            pre = pre + taps[t : t + 1, cols] * padded[5 + t : PIECE + 5 + t, cols]
        pre_out[:, cols] = pre
        act[:, cols] = pre * jax.nn.sigmoid(pre)
    raw, sizes, log_decay = step_parts(step[...], hp[...])
    lower = rows((PIECE, PIECE)) >= lanes((PIECE, PIECE))
    start = carry[0:1]
    running = start + jnp.dot(
        lower.astype(f32), log_decay, precision=HIGHEST, preferred_element_type=f32
    )
    run[...] = running
    end = running[PIECE - 1 : PIECE]
    carry[...] = jnp.broadcast_to(end, carry.shape)
    running_t = running.T
    keys = act[:, GROUP : GROUP + N]
    queries = act[:, GROUP + N :].astype(bf16)
    query[...] = queries
    affinity = jnp.where(lower, dot_nt(queries, keys), 0.0)
    keys_t = keys.T.astype(bf16)
    from_start = jnp.exp(running - start)
    to_end = jnp.exp(end - running)
    whole = jnp.exp(end - start)
    total = jnp.exp(end)
    first = lanes((PIECE, 128)) < 64
    first_row = lanes((1, 128)) < 64
    row16 = rows((16, 128))
    entered[...] = dot(queries, state[...])
    for j in range(PAIRS):
        cols = slice(128 * j, 128 * j + 128)
        x = act[:, cols]
        scaled = x * spread(sizes, j, first)
        weighted[:, cols] = (scaled * spread(to_end, j, first)).astype(bf16)
        gaps = []
        for h in (2 * j, 2 * j + 1):
            gap = jnp.exp(jnp.minimum(running[:, h : h + 1] - running_t[h : h + 1, :], 0.0))
            gaps.append(gap * affinity)
        y = spread(from_start, j, first) * entered[:, cols] + dot(
            jnp.concatenate(gaps, axis=1), apart(scaled, first)
        )
        mixed[:, cols] = y + skip[0:1, cols] * x
    entered[...] = dot(keys_t, weighted[...])
    for j in range(PAIRS):
        cols = slice(128 * j, 128 * j + 128)
        before = state[:, cols]
        starts[0, :, cols] = before.astype(bf16)
        after = spread(whole, j, first_row) * before + entered[:, cols]
        state[:, cols] = after
        last[:, cols] = after
        packed[0:N, cols] = after.astype(bf16)
        decay = jnp.broadcast_to(spread(total, j, first_row), (16, 128))
        high = decay.astype(bf16).astype(f32)
        packed[N : N + 16, cols] = jnp.where(
            row16 == 0, high, jnp.where(row16 == 1, decay - high, 0.0)
        ).astype(bf16)


def turned(k, place):
    return lax.rem(k + 4 - place[0], 4)


def scan_local(place, conv_in, step, rim, taps, hp, skip, pinned):
    tokens = conv_in.shape[0]
    kept = stored if pinned else jax.ShapeDtypeStruct

    def whole(shape):
        return pl.BlockSpec(shape, lambda k, place: (0,) * len(shape))

    def piece(width):
        return pl.BlockSpec((PIECE, width), lambda k, place: (turned(k, place), 0))

    return pl.pallas_call(
        scan_kernel,
        grid_spec=pltpu.PrefetchScalarGridSpec(
            num_scalar_prefetch=1,
            grid=(tokens // PIECE,),
            in_specs=[
                piece(ACT),
                piece(128),
                whole((8, ACT)),
                whole((8, ACT)),
                whole((8, 128)),
                whole((8, GROUP)),
            ],
            out_specs=[
                piece(ACT),
                piece(GROUP),
                piece(N),
                piece(128),
                pl.BlockSpec((1, N, GROUP), lambda k, place: (k, 0, 0)),
                whole((N, GROUP)),
                whole((N + 16, GROUP)),
            ],
            scratch_shapes=[
                pltpu.VMEM((PIECE + 8, ACT), f32),
                pltpu.VMEM((PIECE, ACT), f32),
                pltpu.VMEM((N, GROUP), f32),
                pltpu.VMEM((8, 128), f32),
                pltpu.VMEM((PIECE, GROUP), f32),
                pltpu.VMEM((PIECE, GROUP), bf16),
            ],
        ),
        out_shape=[
            kept((tokens, ACT), f32),
            jax.ShapeDtypeStruct((tokens, GROUP), f32),
            jax.ShapeDtypeStruct((tokens, N), bf16),
            jax.ShapeDtypeStruct((tokens, 128), f32),
            kept((tokens // PIECE, N, GROUP), bf16),
            kept((N, GROUP), f32),
            stored((N + 16, GROUP), bf16),
        ],
        compiler_params=pltpu.CompilerParams(vmem_limit_bytes=VMEM),
        cost_estimate=pl.CostEstimate(
            flops=1_000_000_000, bytes_accessed=8_000_000, transcendentals=1_500_000
        ),
        name="scan_local",
    )(place, conv_in, step, rim, taps, hp, skip)


def project_kernel(core, feed, gain, own, other, normed, conv_in, step, gate):
    values = feed[...].astype(f32)
    scale = lax.rsqrt(jnp.mean(values * values, axis=1, keepdims=True) + epsilon)
    low = (values * scale * gain[0:1]).astype(bf16)
    normed[...] = low
    mine = dot(low, own[...])
    theirs = dot(low, other[...])
    is_first = core[0] == 0
    edge = HALF + EXTRA
    conv_in[:, :HALF] = mine[:, :HALF].astype(bf16)
    conv_in[:, HALF:GROUP] = theirs[:, :HALF].astype(bf16)
    conv_in[:, GROUP:] = jnp.where(is_first, mine[:, HALF:edge], theirs[:, HALF:edge]).astype(bf16)
    slot = jnp.where(is_first, theirs[:, HALF : HALF + 128], mine[:, HALF + 128 : edge])
    step[...] = slot.astype(bf16).astype(f32)
    gate[:, :HALF] = mine[:, edge:].astype(bf16)
    gate[:, HALF:] = theirs[:, edge:].astype(bf16)


def project(core, feed, gain, own, other, pinned):
    tokens = feed.shape[0]

    def whole(shape):
        return pl.BlockSpec(shape, lambda k, core: (0, 0))

    def piece(width):
        return pl.BlockSpec((2 * PIECE, width), lambda k, core: (k, 0))

    return pl.pallas_call(
        project_kernel,
        grid_spec=pltpu.PrefetchScalarGridSpec(
            num_scalar_prefetch=1,
            grid=(tokens // (2 * PIECE),),
            in_specs=[piece(D), whole((8, D)), whole((D, WIDE)), whole((D, WIDE))],
            out_specs=[piece(D), piece(ACT), piece(128), piece(GROUP)],
        ),
        out_shape=[
            stored((tokens, D), bf16),
            jax.ShapeDtypeStruct((tokens, ACT), bf16),
            jax.ShapeDtypeStruct((tokens, 128), f32),
            stored((tokens, GROUP), bf16),
        ],
        compiler_params=pltpu.CompilerParams(vmem_limit_bytes=VMEM),
        cost_estimate=pl.CostEstimate(
            flops=3_200_000_000, bytes_accessed=12_000_000, transcendentals=1000
        ),
        name="project",
    )(core, feed, gain, *far(pinned, own, other))


def gate_kernel(
    mixed, run, query, entering, gate, gain, out_own, out_other, grad, mixed_out, sums0, sums1,
    sums2, sums3, sent0, sent1, sent2, sent3, entered
):
    k = pl.program_id(0)
    entered[...] = dot(query[...], entering[...])
    inner = jnp.zeros((PIECE, 1), f32)
    decay = jnp.exp(run[...])
    first = lanes((PIECE, 128)) < 64
    total = jnp.zeros((PIECE, 1), f32)
    normed = []
    for j in range(PAIRS):
        cols = slice(128 * j, 128 * j + 128)
        y = mixed[:, cols] + spread(decay, j, first) * entered[:, cols]
        mixed_out[:, cols] = y
        pre = gate[:, cols].astype(f32)
        gated = y.astype(bf16).astype(f32) * (pre * jax.nn.sigmoid(pre))
        total = total + jnp.sum(gated * gated, axis=1, keepdims=True)
        scaled = gated * gain[0:1, cols]
        inner = inner + jnp.sum(scaled * grad[:, cols], axis=1, keepdims=True)
        normed.append(scaled.astype(bf16))
    lane = lanes((PIECE, 128))
    both = jnp.where(lane == 0, total, jnp.where(lane == 1, inner, 0.0)).T[0:8]
    for sums in (sums0, sums1, sums2, sums3):
        sums[...] = both
    part = dot(jnp.concatenate(normed[:3], axis=1), out_own[...])
    part = part + dot(jnp.concatenate(normed[3:], axis=1), out_other[...])
    high = total.astype(bf16).astype(f32)
    split = jnp.where(lane == 0, high, jnp.where(lane == 1, total - high, 0.0))
    for index, sent in enumerate((sent0, sent1, sent2, sent3)):

        @pl.when(k == index)
        def _():
            sent[:, :D] = part.astype(sent.dtype)
            sent[:, D:] = split.astype(sent.dtype)


def gate_out(mixed, run, query, entering, gate, gain, out_own, out_other, grad):
    tokens = mixed.shape[0]

    def whole(shape):
        return pl.BlockSpec(shape, lambda k: (0, 0))

    def piece(width):
        return pl.BlockSpec((PIECE, width), lambda k: (k, 0))

    return pl.pallas_call(
        gate_kernel,
        grid=(tokens // PIECE,),
        in_specs=[
            piece(GROUP),
            piece(128),
            piece(N),
            whole((N, GROUP)),
            piece(GROUP),
            whole((8, GROUP)),
            whole((HALF, D)),
            whole((HALF, D)),
            piece(GROUP),
        ],
        out_specs=[piece(GROUP)]
        + [pl.BlockSpec((8, PIECE), lambda k, by=by: (0, lax.rem(k + by, 4))) for by in range(4)]
        + [whole((PIECE, D + 128))] * 4,
        out_shape=[stored((tokens, GROUP), f32)]
        + [stored((8, tokens), f32)] * 4
        + [stored((PIECE, D + 128), f32 if k == 0 else bf16) for k in range(4)],
        scratch_shapes=[pltpu.VMEM((PIECE, GROUP), f32)],
        compiler_params=pltpu.CompilerParams(vmem_limit_bytes=VMEM),
        cost_estimate=pl.CostEstimate(
            flops=1_300_000_000, bytes_accessed=9_000_000, transcendentals=400_000
        ),
        name="gate_out",
    )(mixed, run, query, entering, gate, gain, out_own, out_other, grad)


def scales_kernel(one, two, three, four, scale):
    total = one[...] + two[...] + three[...] + four[...]
    lane = lanes((PIECE, 128))
    for k in range(total.shape[1] // PIECE):
        block = total[:, PIECE * k : PIECE * k + PIECE]
        columns = jnp.concatenate([block, jnp.zeros((120, PIECE), f32)], axis=0).T
        s_out = lax.rsqrt(columns[:, 0:1] / DI + epsilon)
        mean = s_out * columns[:, 1:2] / DI
        scale[PIECE * k : PIECE * k + PIECE] = (
            split_pair(s_out, lane, 0) + split_pair(mean, lane, 2)
        ).astype(bf16)


def scales(parts):
    tokens = parts[0].shape[1]
    return pl.pallas_call(
        scales_kernel,
        out_shape=jax.ShapeDtypeStruct((tokens, 128), bf16),
        cost_estimate=pl.CostEstimate(
            flops=1_000_000, bytes_accessed=200_000, transcendentals=1000
        ),
        name="scales",
    )(*parts)


def out_back_kernel(grad_new, out_own, out_other, product):
    product[:, :HALF] = dot_nt(grad_new[...], out_own[...])
    product[:, HALF:] = dot_nt(grad_new[...], out_other[...])


def out_back(grad_new, out_own, out_other):
    tokens = grad_new.shape[0]
    return pl.pallas_call(
        out_back_kernel,
        out_shape=jax.ShapeDtypeStruct((tokens, GROUP), f32),
        compiler_params=pltpu.CompilerParams(vmem_limit_bytes=VMEM),
        cost_estimate=pl.CostEstimate(
            flops=1_200_000_000, bytes_accessed=5_500_000, transcendentals=0
        ),
        name="out_back",
    )(grad_new, out_own, out_other)


def gate_back_kernel(
    product, gate, mixed, scale, run, query, gain, decay, grad_scan, grad_gate, normed, packed, state
):
    k = pl.program_id(0)

    @pl.when(k == 0)
    def _():
        state[...] = jnp.zeros_like(state)
    grown = jnp.exp(run[...])
    queries_t = query[...].astype(f32).T.astype(bf16)
    first = lanes((PIECE, 128)) < 64
    parts = scale[...].astype(f32)
    s_out, mean = parts[:, 0:1] + parts[:, 1:2], parts[:, 2:3] + parts[:, 3:4]
    row16 = rows((16, 128))
    for j in range(PAIRS):
        cols = slice(128 * j, 128 * j + 128)
        grad = product[:, cols]
        pre = gate[:, cols].astype(f32)
        sig = jax.nn.sigmoid(pre)
        out = mixed[:, cols].astype(bf16).astype(f32)
        unit = out * (pre * sig) * s_out
        gain_j = gain[0:1, cols]
        gated = s_out * (grad * gain_j - unit * mean)
        scan = (gated * (pre * sig)).astype(bf16)
        grad_scan[:, cols] = scan
        grad_gate[:, cols] = (gated * out * sig * (1.0 + pre * (1.0 - sig))).astype(bf16)
        normed[:, cols] = (unit * gain_j).astype(bf16)
        total = state[:, cols] + dot(queries_t, spread(grown, j, first) * scan.astype(f32))
        state[:, cols] = total
        packed[0:N, cols] = total.astype(bf16)
        fall = jnp.broadcast_to(decay[0:1, cols], (16, 128))
        high = fall.astype(bf16).astype(f32)
        packed[N : N + 16, cols] = jnp.where(
            row16 == 0, high, jnp.where(row16 == 1, fall - high, 0.0)
        ).astype(bf16)


def gate_back(product, gate, mixed, scale, run, query, gain, decay, pinned):
    tokens = mixed.shape[0]

    def whole(shape):
        return pl.BlockSpec(shape, lambda k: (0, 0))

    def piece(width):
        return pl.BlockSpec((PIECE, width), lambda k: (k, 0))

    return pl.pallas_call(
        gate_back_kernel,
        grid=(tokens // PIECE,),
        in_specs=[
            piece(GROUP),
            piece(GROUP),
            piece(GROUP),
            piece(128),
            piece(128),
            piece(N),
            whole((8, GROUP)),
            whole((8, GROUP)),
        ],
        out_specs=[piece(GROUP), piece(GROUP), piece(GROUP), whole((N + 16, GROUP))],
        out_shape=[
            jax.ShapeDtypeStruct((tokens, GROUP), bf16),
            jax.ShapeDtypeStruct((tokens, GROUP), bf16),
            jax.ShapeDtypeStruct((tokens, GROUP), bf16),
            stored((N + 16, GROUP), bf16),
        ],
        scratch_shapes=[pltpu.VMEM((N, GROUP), f32)],
        compiler_params=pltpu.CompilerParams(vmem_limit_bytes=VMEM),
        cost_estimate=pl.CostEstimate(
            flops=120_000_000, bytes_accessed=8_000_000, transcendentals=400_000
        ),
        name="gate_back",
    )(product, *far(pinned, gate, mixed), scale, *far(pinned, run, query), gain, decay)


def scan_back_kernel(
    place, conv_in, pre_in, step, run, grad, grad_gate, mixed, starts, last, entering, leaving, rim,
    taps, hp, skip, use_own, use_other, tail, rim_grad, laid, act, delta, state, after, skip_sum,
    product, flows, weighted, ended, grad_taps, grad_hp, spots
):
    k = pl.program_id(0)
    count = pl.num_programs(0)
    first = lanes((PIECE, 128)) < 64
    first_row = lanes((1, 128)) < 64
    raw, sizes, log_decay = step_parts(step[...], hp[...])
    running = run[...]
    start = running[0:1] - log_decay[0:1]
    end = running[PIECE - 1 : PIECE]
    from_start = jnp.exp(running - start)
    to_end = jnp.exp(end - running)
    whole = jnp.exp(end - start)
    before_all = jnp.exp(start)
    until_end = jnp.exp(end)

    @pl.when(k == 0)
    def _():
        delta[PIECE : PIECE + 8] = jnp.zeros((8, ACT), f32)
        grad_taps[...] = jnp.zeros_like(grad_taps)
        grad_hp[...] = jnp.zeros_like(grad_hp)
        skip_sum[...] = jnp.zeros_like(skip_sum)
        for j in range(PAIRS):
            cols = slice(128 * j, 128 * j + 128)
            state[:, cols] = leaving[:, cols]
            after[:, cols] = spread(until_end, j, first_row) * entering[:, cols] + last[:, cols]

    @pl.when(k > 0)
    def _():
        delta[PIECE : PIECE + 8] = delta[0:8]

    for j in range(ACT // 128):
        cols = slice(128 * j, 128 * j + 128)
        pre = pre_in[:, cols]
        act[:, cols] = pre * jax.nn.sigmoid(pre)

    upper = rows((PIECE, PIECE)) <= lanes((PIECE, PIECE))
    keys = act[:, GROUP : GROUP + N].astype(bf16)
    queries32 = act[:, GROUP + N :]
    queries = queries32.astype(bf16)
    queries_t = queries32.T.astype(bf16)
    affinity = jnp.where(upper, dot_nt(keys, queries), 0.0)
    running_t = running.T
    grad_affinity = jnp.zeros((PIECE, PIECE), f32)
    product[...] = dot(keys, state[...])
    for j in range(PAIRS):
        cols = slice(128 * j, 128 * j + 128)
        x = act[:, cols]
        sizes_j = spread(sizes, j, first)
        scaled = x * sizes_j
        dm = grad[:, cols]
        dm32 = dm.astype(f32)
        to_end_j = spread(to_end, j, first)
        gaps = [
            jnp.exp(jnp.minimum(running_t[h : h + 1, :] - running[:, h : h + 1], 0.0))
            for h in (2 * j, 2 * j + 1)
        ]
        z = to_end_j * product[:, cols] + dot(
            jnp.concatenate([gap * affinity for gap in gaps], axis=1), apart(dm32, first)
        )
        crossed = dot_nt(apart(scaled, first), dm)
        grad_affinity = grad_affinity + gaps[0] * crossed[:PIECE] + gaps[1] * crossed[PIECE:]
        skip_j = skip[0:1, cols]
        delta[0:PIECE, cols] = sizes_j * z + skip_j * dm32
        skip_sum[0:1, cols] += jnp.sum(dm32 * x, axis=0, keepdims=True)
        flows[0:PIECE, cols] = x * z
        flows[PIECE : 2 * PIECE, cols] = dm32 * (mixed[:, cols] - skip_j * x)
        inside = jnp.sum(state[:, cols] * after[:, cols], axis=0, keepdims=True)
        flows[2 * PIECE :, cols] = jnp.broadcast_to(inside, (16, 128))
        after[:, cols] = spread(before_all, j, first_row) * entering[:, cols] + starts[
            0, :, cols
        ].astype(f32)
        weighted[:, cols] = (spread(from_start, j, first) * dm32).astype(bf16)
        ended[:, cols] = (scaled * to_end_j).astype(bf16)
    heads = (lanes((GROUP, 128)) == lax.shift_right_logical(rows((GROUP, 128)), 6)).astype(bf16)
    sums = dot_split(flows[...], heads)
    inner_sum, outer_sum = sums[:PIECE], sums[PIECE : 2 * PIECE]
    bound = sums[2 * PIECE :]
    grad_queries = dot_nt(weighted[...], after[...])
    grad_keys = dot_nt(ended[...], state[...])
    product[...] = dot(queries_t, weighted[...])
    for j in range(PAIRS):
        cols = slice(128 * j, 128 * j + 128)
        state[:, cols] = spread(whole, j, first_row) * state[:, cols] + product[:, cols]
    grad_affinity = jnp.where(upper, grad_affinity, 0.0)
    delta[0:PIECE, GROUP : GROUP + N] = grad_keys + dot(grad_affinity, queries)
    delta[0:PIECE, GROUP + N :] = grad_queries + dot(grad_affinity.T, keys)

    flow = outer_sum - sizes * inner_sum
    grad_log = bound[0:1] + jnp.dot(
        upper.astype(f32), flow, precision=HIGHEST, preferred_element_type=f32
    )
    rate = jnp.exp(hp[1:2])
    live = lanes((PIECE, 128)) < HEADS
    grad_raw = jnp.where(live, (inner_sum - rate * grad_log) * jax.nn.sigmoid(raw), 0.0)
    is_first = place[1] == 0
    edge = HALF + EXTRA
    step_first = jnp.where(is_first, grad_raw, 0.0)
    step_second = jnp.where(is_first, 0.0, grad_raw)
    for use, gate_cols in ((use_own, slice(0, HALF)), (use_other, slice(HALF, GROUP))):
        use[:, edge:] = grad_gate[:, gate_cols]

    @pl.when(k == 0)
    def _():
        for side, gate_cols in ((0, slice(0, HALF)), (1, slice(HALF, GROUP))):
            tail[:, WIDE * side + edge : WIDE * side + WIDE] = grad_gate[
                PIECE - 16 :, gate_cols
            ].astype(f32)[8:]
    grad_hp[0:1] += jnp.sum(grad_raw, axis=0, keepdims=True)
    grad_hp[1:2] += jnp.sum(jnp.where(live, grad_log * log_decay, 0.0), axis=0, keepdims=True)

    for j in range(ACT // 128):
        cols = slice(128 * j, 128 * j + 128)
        pre = pre_in[:, cols]
        sig = jax.nn.sigmoid(pre)
        grown = delta[0:PIECE, cols] * sig * (1.0 + pre * (1.0 - sig))
        delta[0:PIECE, cols] = grown
        grad_taps[4:5, cols] += jnp.sum(grown, axis=0, keepdims=True)
        taken = conv_in[:, cols].astype(f32)
        total = jnp.zeros((PIECE, 128), f32)
        for t in range(4):
            moved = delta[3 - t : 3 - t + PIECE, cols]
            total = total + taps[t : t + 1, cols] * moved
            grad_taps[t : t + 1, cols] += jnp.sum(taken * moved, axis=0, keepdims=True)
        if j < PAIRS:
            use = use_own if j < 3 else use_other
            at = 128 * (j % 3)
            use[:, at : at + 128] = total.astype(bf16)
            targets = [(WIDE * (j // 3) + at, total)]
        else:
            at = HALF + 128 * (j - PAIRS)
            slot = step_first if j == PAIRS else step_second
            first_use = jnp.where(is_first, total, slot)
            second_use = jnp.where(is_first, slot, total)
            use_own[:, at : at + 128] = first_use.astype(bf16)
            use_other[:, at : at + 128] = second_use.astype(bf16)
            targets = [(at, first_use), (WIDE + at, second_use)]

        @pl.when(k == 0)
        def _():
            for at, values in targets:
                tail[:, at : at + 128] = values[PIECE - 8 :]

    @pl.when(k == count - 1)
    def _():
        for j in range(PAIRS):
            cols = slice(128 * j, 128 * j + 128)
            heads = (lanes((128, 128)) == 2 * j + (rows((128, 128)) >= 64)).astype(bf16)
            sums = dot_split(jnp.broadcast_to(skip_sum[0:1, cols], (8, 128)), heads)
            grad_hp[2:3] += sums[0:1]
        for j in range(ACT // 128):
            cols = slice(128 * j, 128 * j + 128)
            border = jnp.concatenate([jnp.zeros((8, 128), f32), delta[0:8, cols]], axis=0)
            taken = rim[:, cols].astype(f32)
            total = jnp.zeros((8, 128), f32)
            for t in range(4):
                moved = border[3 - t : 11 - t]
                total = total + taps[t : t + 1, cols] * moved
                grad_taps[t : t + 1, cols] += jnp.sum(taken * moved, axis=0, keepdims=True)
            if j < PAIRS:
                at = WIDE * (j // 3) + 128 * (j % 3)
                rim_grad[:, at : at + 128] = total
            else:
                at = HALF + 128 * (j - PAIRS)
                rim_grad[:, at : at + 128] = jnp.where(is_first, total, 0.0)
                rim_grad[:, WIDE + at : WIDE + at + 128] = jnp.where(is_first, 0.0, total)
        for side in range(2):
            rim_grad[:, WIDE * side + edge : WIDE * side + WIDE] = jnp.zeros((8, HALF), f32)
        spots[...] = jnp.zeros_like(spots)
        for j in range(PAIRS):
            half = 2 * place[0] + (place[1] if j < 3 else 1 - place[1])
            at = pl.ds(pl.multiple_of(half * HALF + 128 * (j % 3), 128), 128)
            spots[:, at] = grad_taps[:, 128 * j : 128 * j + 128]
        spots[:, DI : DI + 2 * N] = grad_taps[:, GROUP:]
        lane = lanes((8, 128))
        sums = grad_hp[...]
        crossed = jnp.where(lane < 6, pltpu.roll(sums, 122, 1), pltpu.roll(sums, 6, 1))
        sums = pltpu.roll(jnp.where(is_first, sums, crossed), SMALL_AT, 1)
        sums = pltpu.roll(sums, 5, 0)
        is_sum = (rows((8, 128)) >= 5) & (lane >= SMALL_AT) & (lane < SMALL_AT + HEADS)
        is_tap = (rows((8, 128)) < 5) & (lane >= SMALL_AT) & (lane < SMALL_AT + 52)
        sums = jnp.where(is_sum, sums, 0.0)
        laid[...] = jnp.zeros_like(laid)
        for d in range(64):
            at = 52 * d // 128 * 128
            window = pltpu.roll(spots[:, at : at + 256], (256 + SMALL_AT - 52 * d + at) % 256, 1)
            laid[24 * d : 24 * d + 8] = jnp.where(is_tap, window[:, :128], sums)


def scan_back(
    place, conv_in, pre, step, run, grad, grad_gate, mixed, starts, last, entering, leaving, rim,
    taps, hp, skip, pinned
):
    tokens = conv_in.shape[0]
    count = tokens // PIECE

    def whole(shape):
        return pl.BlockSpec(shape, lambda k, place: (0,) * len(shape))

    def piece(width):
        return pl.BlockSpec((PIECE, width), lambda k, place: (turned(count - 1 - k, place), 0))

    return pl.pallas_call(
        scan_back_kernel,
        grid_spec=pltpu.PrefetchScalarGridSpec(
            num_scalar_prefetch=1,
            grid=(count,),
            in_specs=[
                piece(ACT),
                piece(ACT),
                piece(128),
                piece(128),
                piece(GROUP),
                piece(GROUP),
                piece(GROUP),
                pl.BlockSpec((1, N, GROUP), lambda k, place: (count - 1 - k, 0, 0)),
                whole((N, GROUP)),
                whole((N, GROUP)),
                whole((N, GROUP)),
                whole((8, ACT)),
                whole((8, ACT)),
                whole((8, 128)),
                whole((8, GROUP)),
            ],
            out_specs=[
                piece(WIDE),
                piece(WIDE),
                whole((8, 2 * WIDE)),
                whole((8, 2 * WIDE)),
                whole((D, 128)),
            ],
            scratch_shapes=[
                pltpu.VMEM((PIECE, ACT), f32),
                pltpu.VMEM((PIECE + 8, ACT), f32),
                pltpu.VMEM((N, GROUP), f32),
                pltpu.VMEM((N, GROUP), f32),
                pltpu.VMEM((8, GROUP), f32),
                pltpu.VMEM((PIECE, GROUP), f32),
                pltpu.VMEM((2 * PIECE + 16, GROUP), f32),
                pltpu.VMEM((PIECE, GROUP), bf16),
                pltpu.VMEM((PIECE, GROUP), bf16),
                pltpu.VMEM((8, ACT), f32),
                pltpu.VMEM((8, 128), f32),
                pltpu.VMEM((8, DI + 2 * N + 128), f32),
            ],
        ),
        out_shape=[
            jax.ShapeDtypeStruct((tokens, WIDE), bf16),
            jax.ShapeDtypeStruct((tokens, WIDE), bf16),
            jax.ShapeDtypeStruct((8, 2 * WIDE), f32),
            jax.ShapeDtypeStruct((8, 2 * WIDE), f32),
            jax.ShapeDtypeStruct((D, 128), f32),
        ],
        compiler_params=pltpu.CompilerParams(vmem_limit_bytes=VMEM),
        cost_estimate=pl.CostEstimate(
            flops=2_000_000_000, bytes_accessed=9_000_000, transcendentals=2_500_000
        ),
        name="scan_back",
    )(place, *far(pinned, conv_in, pre, step, run), grad, grad_gate,
      *far(pinned, mixed, starts, last, entering), leaving, rim, taps, hp, skip)


def parts_kernel(use_own, use_other, own, other, sent0, sent1, sent2, sent3):
    part = dot_nt(use_own[...], own[...]) + dot_nt(use_other[...], other[...])
    for index, sent in enumerate((sent0, sent1, sent2, sent3)):
        sent[...] = part[PIECE * index : PIECE * index + PIECE].astype(sent.dtype)


def project_back(use_own, use_other, own, other, pinned):
    tokens = use_own.shape[0]
    width = 256

    def whole(shape):
        return pl.BlockSpec(shape, lambda k: (0, 0))

    return pl.pallas_call(
        parts_kernel,
        grid=(D // width,),
        in_specs=[whole((tokens, WIDE))] * 2 + [pl.BlockSpec((width, WIDE), lambda k: (k, 0))] * 2,
        out_specs=[pl.BlockSpec((PIECE, width), lambda k: (0, k))] * 4,
        out_shape=[stored((PIECE, D), f32 if k == 0 else bf16) for k in range(4)],
        compiler_params=pltpu.CompilerParams(vmem_limit_bytes=VMEM),
        cost_estimate=pl.CostEstimate(
            flops=3_200_000_000, bytes_accessed=9_000_000, transcendentals=0
        ),
        name="project_back",
    )(use_own, use_other, *far(pinned, own, other))


def early_kernel(normed, grad_gate, normed_out, grad_new, own, other, sums):
    i = pl.program_id(0)

    @pl.when(i == 0)
    def _():
        sums[0] = dot_tn(normed_out[:, :HALF], grad_new[...])
        sums[1] = dot_tn(normed_out[:, HALF:], grad_new[...])

    block = dot_tn(normed[...], grad_gate[...])
    for side, sent in enumerate((own, other)):
        sent[:, :HALF] = block[:, HALF * side : HALF * side + HALF].astype(bf16)
        for s in range(4):
            row = pl.ds(pl.multiple_of(96 * i + 24 * s, 8), 24)
            pieces = [sums[side, row, HALF * q : HALF * q + HALF] for q in range(4)]
            sent[96 * s : 96 * s + 96, HALF:] = jnp.concatenate(pieces, axis=0).astype(bf16)


def early_grads(normed, grad_gate, normed_out, grad_new):
    tokens = normed.shape[0]

    def whole(shape):
        return pl.BlockSpec(shape, lambda i: (0, 0))

    return pl.pallas_call(
        early_kernel,
        grid=(4,),
        in_specs=[
            pl.BlockSpec((tokens, HALF), lambda i: (0, i)),
            whole((tokens, GROUP)),
            whole((tokens, GROUP)),
            whole((tokens, D)),
        ],
        out_specs=[pl.BlockSpec((HALF, GROUP), lambda i: (i, 0))] * 2,
        out_shape=[stored((D, GROUP), bf16)] * 2,
        scratch_shapes=[pltpu.VMEM((2, HALF, D), f32)],
        compiler_params=pltpu.CompilerParams(vmem_limit_bytes=VMEM),
        cost_estimate=pl.CostEstimate(
            flops=2_400_000_000, bytes_accessed=9_000_000, transcendentals=0
        ),
        name="early_grads",
    )(normed, grad_gate, normed_out, grad_new)


def inner_kernel(place, normed, use_own, use_other, slot, own, other):
    is_first = place[1] == 0
    for use, sent, holds in ((use_own, own, ~is_first), (use_other, other, is_first)):
        block = dot_tn(normed[...], use[...])
        sent[:, :HALF] = block[:, :HALF].astype(bf16)
        middle = block[:, HALF : HALF + 128] + jnp.where(holds, slot[...], 0.0)
        sent[:, HALF : HALF + 128] = middle.astype(bf16)
        sent[:, HALF + 128 :] = block[:, HALF + 128 :].astype(bf16)


def inner_grads(place, normed, use_own, use_other, slot):
    tokens = normed.shape[0]
    edge = HALF + EXTRA

    def whole(shape):
        return pl.BlockSpec(shape, lambda i, place: (0, 0))

    return pl.pallas_call(
        inner_kernel,
        grid_spec=pltpu.PrefetchScalarGridSpec(
            num_scalar_prefetch=1,
            grid=(4,),
            in_specs=[
                pl.BlockSpec((tokens, HALF), lambda i, place: (0, i)),
                whole((tokens, edge)),
                whole((tokens, edge)),
                pl.BlockSpec((HALF, 128), lambda i, place: (i, 0)),
            ],
            out_specs=[pl.BlockSpec((HALF, edge), lambda i, place: (i, 0))] * 2,
        ),
        out_shape=[stored((D, edge), bf16)] * 2,
        compiler_params=pltpu.CompilerParams(vmem_limit_bytes=VMEM),
        cost_estimate=pl.CostEstimate(
            flops=2_000_000_000, bytes_accessed=7_000_000, transcendentals=0
        ),
        name="inner_grads",
    )(place, normed, use_own, use_other, slot)


def split_pair(values, lane, at):
    high = values.astype(bf16).astype(f32)
    return jnp.where(lane == at, high, jnp.where(lane == at + 1, values - high, 0.0))


def receive_kernel(part, one, two, three, feed, target, branch_out, result, scale):
    total = part[...] + one[...].astype(f32) + two[...].astype(f32) + three[...].astype(f32)
    square = total[:, D : D + 1] + total[:, D + 1 : D + 2]
    s_out = lax.rsqrt(square / DI + epsilon)
    branch = s_out * total[:, :D]
    branch_out[...] = branch
    result[...] = (feed[...].astype(f32) + branch).astype(bf16)
    mean = jnp.sum(branch * target[...].astype(f32), axis=1, keepdims=True) / DI
    lane = lanes((PIECE, 128))
    scale[...] = (split_pair(s_out, lane, 0) + split_pair(mean, lane, 2)).astype(bf16)


def receive(parts, feed, target):
    return pl.pallas_call(
        receive_kernel,
        out_shape=[
            stored((PIECE, D), f32),
            jax.ShapeDtypeStruct((PIECE, D), bf16),
            jax.ShapeDtypeStruct((PIECE, 128), bf16),
        ],
        compiler_params=pltpu.CompilerParams(vmem_limit_bytes=VMEM),
        cost_estimate=pl.CostEstimate(
            flops=3_000_000, bytes_accessed=4_500_000, transcendentals=1000
        ),
        name="receive",
    )(*parts, feed, target)


def receive_back_kernel(
    part, one, two, three, feed, grad_new, gain, branch, scale_in, grad_out, scale_out
):
    total = part[...] + one[...].astype(f32) + two[...].astype(f32) + three[...].astype(f32)
    values = feed[...].astype(f32)
    s_in = lax.rsqrt(jnp.mean(values * values, axis=1, keepdims=True) + epsilon)
    unit = values * s_in
    grad_unit = total * gain[0:1]
    grad = grad_new[...].astype(f32) + s_in * (
        grad_unit - unit * jnp.mean(unit * grad_unit, axis=1, keepdims=True)
    )
    low = grad.astype(bf16)
    grad_out[...] = low
    mean = jnp.sum(branch[...] * low.astype(f32), axis=1, keepdims=True) / DI
    lane = lanes((PIECE, 128))
    kept = jnp.where(lane < 2, scale_in[...].astype(f32), 0.0)
    scale_out[...] = (kept + split_pair(mean, lane, 2)).astype(bf16)


def receive_back(parts, feed, grad_new, gain, branch, scale):
    return pl.pallas_call(
        receive_back_kernel,
        out_shape=[
            jax.ShapeDtypeStruct((PIECE, D), bf16),
            jax.ShapeDtypeStruct((PIECE, 128), bf16),
        ],
        compiler_params=pltpu.CompilerParams(vmem_limit_bytes=VMEM),
        cost_estimate=pl.CostEstimate(
            flops=4_000_000, bytes_accessed=4_500_000, transcendentals=1000
        ),
        name="receive_back",
    )(*parts, feed, grad_new, gain, branch, scale)


def pick(core, first, second):
    return jnp.where(core == 0, first, second)


def spread_weights(core, head, gate_inner, shared_bc, step_proj):
    gate = gate_inner[:, :DI].reshape(24, 4, 2, HALF)
    inner = gate_inner[:, DI:].reshape(24, 4, 2, HALF)
    heads = step_proj.reshape(24, 4, HEADS)
    fill = jnp.zeros((24, 128 - HEADS), bf16)
    halves = []
    for q in range(2):
        pieces = []
        for g in range(4):
            own = heads[:, g]
            slot = [own, fill, own[:, 6:], own[:, :6], fill]
            extra = [shared_bc] if q == 0 else slot
            pieces.append(jnp.concatenate([inner[:, g, q]] + extra + [gate[:, g, q]], axis=1))
        halves.append(jnp.stack(pieces))
    kept = pick(core, halves[0], halves[1])
    got = swap(pick(core, halves[1], halves[0]))
    layers = [pick(core, kept, got), pick(core, got, kept)]
    return [exchange_head(values, head).reshape(96, WIDE) for values in layers]


def out_pairs():
    pairs = []
    for layer in range(2):
        for z in range(4):
            for y in range(4):
                for x in range(4):
                    source = (layer * 16 + z * 4 + y) * 4 + x
                    place = layer * 8 + (y % 2) * 4 + x
                    pairs.append((source, ((y // 2) * 16 + place) * 4 + z))
    return pairs


def out_back_pairs(part):
    pairs = []
    for core in range(2):
        for place in range(16):
            layer = (place + part) % 2
            for group in range(4):
                j = place // 2
                target = (layer * 16 + group * 4 + 2 * core + j // 4) * 4 + j % 4
                pairs.append(((core * 16 + place) * 4 + group, target))
    return pairs


EVERY = ("section", "seq", "head")


def gather_seq(a):
    return lax.all_gather(a, "seq", axis=0, tiled=True)


def gather_small(core, a):
    other = swap(a)
    both = jnp.concatenate([pick(core, a, other), pick(core, other, a)], axis=1)
    width = a.shape[1]
    both = jnp.pad(both.reshape(2 * width // 128, 128), ((0, 8 - 2 * width // 128), (0, 0)))
    sent = jnp.broadcast_to(both[None], (64, 8, 128)).reshape(512, 128)
    got = lax.all_to_all(sent, ("seq", "head"), 0, 0, tiled=True).reshape(64, 1024)
    return got[:, :width], got[:, width : 2 * width]


def layer_params(core, head, small, per_head):
    gain_in = small[:, :24].reshape(1, D)
    conv = small[:, 24:232].reshape(64, 4, 52).transpose(1, 0, 2).reshape(4, DI + 2 * N)
    bias = small[:, 232:284].reshape(1, DI + 2 * N)
    gain = small[:, 284:332].reshape(1, DI)
    taps = jnp.concatenate([conv, bias, jnp.zeros((3, DI + 2 * N), f32)], axis=0)

    def grouped(values, width):
        own = lax.dynamic_slice_in_dim(values, (2 * head + core) * width, width, 1)
        other = lax.dynamic_slice_in_dim(values, (2 * head + 1 - core) * width, width, 1)
        return [own, other]

    taps = jnp.concatenate(grouped(taps, HALF) + [taps[:, DI:]], axis=1)
    gain = jnp.broadcast_to(jnp.concatenate(grouped(gain, HALF), axis=1), (8, GROUP))
    per_head = jnp.concatenate(grouped(per_head, 6), axis=1)
    hp = jnp.pad(per_head, ((0, 5), (0, 128 - HEADS)))
    skip = jnp.broadcast_to(jnp.repeat(per_head[2:3], 64, axis=1), (8, GROUP))
    return dict(
        taps=taps, gain=gain, hp=hp, skip=skip, gain_in=jnp.broadcast_to(gain_in, (8, D))
    )


def tied(values, anchor):
    return lax.optimization_barrier((values, anchor))[0]


def layer_forward(core, head, feed, feed_all, weights, out_weights, first):
    place = jnp.stack([head, core])
    own, other = weights["own"], weights["other"]
    normed, conv_in, step, gate = project(core.reshape(1), feed_all, weights["gain_in"], own, other, first
    )
    last_row = PIECE * lax.rem(7 - head, 4) + PIECE - 8
    rim = lax.ppermute(
        lax.dynamic_slice_in_dim(conv_in, last_row, 8, 0), "seq", [(i, i + 1) for i in range(15)]
    )
    pre, mixed0, query, run, starts, last, packed = scan_local(
        place, conv_in, step, rim, weights["taps"], weights["hp"], weights["skip"], first
    )
    entering = carried(packed, -1)
    entering, out_own, out_other, product = out_weights(packed, entering)
    mixed, *sums_and_sent = gate_out(
        mixed0, run, query, entering, gate, weights["gain"], out_own, out_other,
        mixed0 if product is None else product,
    )
    kept = dict(
        feed=feed, normed=normed, gate=gate, conv_in=conv_in, rim=rim, step=step, pre=pre,
        mixed=mixed, query=query, run=run, starts=starts, last=last, entering=entering,
        packed=packed, out_own=out_own, out_other=out_other,
    )
    return sums_and_sent[:4], sums_and_sent[4:], kept


def layer_backward(
    core, head, incoming, gathered, product, scale, kept, below, weights, after_gate, before_receive,
    inner_first,
):
    place = jnp.stack([head, core])
    own, other = weights["own"], weights["other"]
    decay = jnp.broadcast_to(
        kept["packed"][N : N + 1].astype(f32) + kept["packed"][N + 1 : N + 2].astype(f32),
        (8, GROUP),
    )
    grad_scan, grad_gate, normed_out, packed = gate_back(
        product, kept["gate"], kept["mixed"], scale, kept["run"], kept["query"], weights["gain"],
        decay, not inner_first,
    )
    leaving = carried(packed, 1)
    normed = kept["normed"]
    early_operands = (normed, grad_gate, normed_out, gathered)
    if inner_first:
        early, leaving = after_gate(early_grads(*early_operands), packed, leaving)
    else:
        _, leaving = after_gate(None, packed, leaving)
    use_own, use_other, tail, rim_grad, slot = scan_back(
        place, kept["conv_in"], kept["pre"], kept["step"], kept["run"], grad_scan, grad_gate,
        kept["mixed"], kept["starts"], kept["last"], kept["entering"], leaving, kept["rim"],
        weights["taps"], weights["hp"], weights["skip"], inner_first,
    )
    from_next = lax.ppermute(rim_grad, "seq", [(i + 1, i) for i in range(15)])
    last_row = PIECE * lax.rem(7 - head, 4) + PIECE - 8
    tail = (tail + from_next).astype(bf16)
    use_own = lax.dynamic_update_slice_in_dim(use_own, tail[:, :WIDE], last_row, 0)
    use_other = lax.dynamic_update_slice_in_dim(use_other, tail[:, WIDE:], last_row, 0)
    if inner_first:
        grad_x = summed(*inner_grads(place, normed, use_own, use_other, slot))
        use_own, use_other = tied((use_own, use_other), grad_x)
        sent = project_back(use_own, use_other, own, other, inner_first)
    else:
        sent = project_back(use_own, use_other, own, other, inner_first)
    parts = before_receive(scatter_head(sent))
    if not inner_first:
        early = early_grads(*tied(early_operands, slot))
    grad_feed, scale_below = receive_back(
        parts, kept["feed"], incoming, weights["gain_in"], below["branch"],
        below["scale"],
    )
    if not inner_first:
        grad_x = inner_grads(place, normed, *tied((use_own, use_other), grad_feed), slot)
    return grad_feed, scale_below, grad_x, early


def summed(own, other):
    return (own.astype(f32) + swap(other).astype(f32)).astype(bf16)


def scatter_seq(a):
    return lax.psum_scatter(a, "seq", scatter_dimension=0, tiled=True)


def scatter_seq_now(a):
    got = lax.all_to_all(a, "seq", 0, 0, tiled=True).astype(f32)
    return jnp.sum(got.reshape(16, 96, a.shape[1]), axis=0).astype(bf16)


def per_device(
    tokens_in, cotangent, input_gain, gate_inner, shared_bc, step_proj, conv_weight, conv_bias,
    step_bias, decay_log, skip_gain, output_gain, out_proj
):
    core = lax.axis_index("section")
    head = lax.axis_index("head")
    tokens = lax.dynamic_index_in_dim(tokens_in, core, 0, False)
    grad_top = lax.dynamic_index_in_dim(cotangent, core, 0, False)
    edge = HALF + EXTRA

    pieces = spread_weights(core, head, gate_inner[0], shared_bc[0], step_proj[0])
    own0 = gather_seq(pieces[0])
    out_piece = lax.ppermute(out_proj[0], EVERY, out_pairs())
    small = jnp.concatenate(
        [input_gain, conv_weight[0].reshape(1, 208), conv_bias, output_gain], axis=1
    ).astype(f32)
    small = gather_small(core, tied(jnp.pad(small, ((0, 0), (0, 52))), pieces[0]))
    per_head = jnp.concatenate([step_bias, decay_log, skip_gain], axis=0)
    other_head = swap(tied(per_head, pieces[0]))
    head_values = [pick(core, per_head, other_head), pick(core, other_head, per_head)]
    weights = [layer_params(core, head, small[l], head_values[l]) for l in range(2)]
    feed_all = jnp.concatenate(gather_head(tied(tokens, pieces[0])), axis=0)
    feed_all, weights, own0, out_piece = lax.optimization_barrier(
        (feed_all, weights, own0, out_piece)
    )
    weights[0].update(own=own0, other=swap(own0))
    out = gather_seq(out_piece)
    own1 = gather_seq(tied(pieces[1], weights[0]["other"]))

    later = {}

    def out_first(packed, entering):
        mine = tied(out, packed)
        later["out"] = (mine, swap(mine))
        grad_all = jnp.concatenate(gather_head(tied(grad_top, packed)), axis=0)
        entering, later["grad_all"] = lax.optimization_barrier((entering, grad_all))
        return [entering] + [a[:HALF] for a in later["out"]] + [None]

    def out_second(packed, entering):
        mine, theirs = [a[HALF:] for a in later["out"]]
        return [entering, mine, theirs, later["product"]]

    _, sent, kept0 = layer_forward(core, head, tokens, feed_all, weights[0], out_first, True)
    parts = scatter_head(sent)
    later["product"] = out_back(
        tied(later["grad_all"], sent[0]), later["out"][0][HALF:], later["out"][1][HALF:]
    )
    parts, later["product"] = lax.optimization_barrier((parts, later["product"]))
    branch, hidden, scale = receive(parts, tokens, tokens)
    kept0.update(branch=branch, scale=scale)
    feed_all = jnp.concatenate(gather_head(hidden), axis=0)
    own1 = tied(own1, hidden)
    weights[1].update(own=own1, other=swap(own1))
    sums, sent, kept1 = layer_forward(core, head, hidden, feed_all, weights[1], out_second, False)
    sums = [sums[0]] + [from_head(sums[k], k) for k in (1, 3, 2)]
    scale = scales(sums)

    def after_gate1(values, packed, leaving):
        _, result, _ = receive(scatter_head(tied(sent, packed)), hidden, hidden)
        leaving, later["result"] = lax.optimization_barrier((leaving, result))
        return None, leaving

    def before_receive1(sent):
        return sent

    grad_hidden, scale, grad_x1, early1 = layer_backward(
        core, head, grad_top, later["grad_all"], later["product"], scale, kept1, kept0, weights[1],
        after_gate1, before_receive1, False,
    )
    chunks = gather_head(jnp.concatenate([grad_hidden, scale], axis=1))
    pieces1 = [(own, swap(other)) for own, other in (grad_x1, early1)]
    chunks, pieces1 = lax.optimization_barrier((chunks, pieces1))
    grad_all = jnp.concatenate([a[:, :D] for a in chunks], axis=0)
    scale = jnp.concatenate([a[:, D:] for a in chunks], axis=0)

    def after_gate0(values, packed, leaving):
        both = [pieces1[0], (values[0], swap(values[1])), pieces1[1]]
        later["sum"] = jnp.concatenate(
            [(own.astype(f32) + got.astype(f32)).astype(bf16) for own, got in both], axis=1
        )
        return scatter_seq(later["sum"]), leaving

    def before_receive0(sent):
        return tied(sent, later["sum"])

    product = out_back(grad_all, kept0["out_own"], kept0["out_other"])
    grad_feed, _, grad_x0, early0 = layer_backward(
        core, head, grad_hidden, grad_all, product, scale, kept0, kept0, weights[0], after_gate0,
        before_receive0, True,
    )
    early0, early1 = early0[:, : edge + GROUP], early0[:, edge + GROUP :]
    x0 = scatter_seq_now(grad_x0)
    result = later["result"]
    got = swap(pick(core, result, hidden))
    layer_out = jnp.stack([pick(core, hidden, got), pick(core, got, result)])
    got = swap(pick(core, grad_hidden, grad_feed))
    grad_in = jnp.stack([pick(core, grad_feed, got), pick(core, got, grad_hidden)])

    both = jnp.concatenate(
        [x0, early0[:, edge:WIDE], early0[:, :edge], early1[:, :HALF]], axis=1
    ).reshape(4, 24, 2 * WIDE)
    both = exchange_head(both, head)

    def out_rows(a):
        return a.reshape(4, 24, HALF).transpose(1, 0, 2).reshape(24, D)

    out0, out1 = out_rows(early0[:, WIDE:]), out_rows(early1[:, HALF:])
    out0, out1 = tied((out0, out1), both)
    even = lax.rem(lax.axis_index("seq"), 2)
    rows_out = [
        lax.ppermute(pick(even, out0, out1), EVERY, out_back_pairs(0)),
        lax.ppermute(pick(even, out1, out0), EVERY, out_back_pairs(1)),
    ]
    grad_out = jnp.concatenate(
        [pick(core, rows_out[0], rows_out[1]), pick(core, rows_out[1], rows_out[0])], axis=0
    ).astype(f32)
    first, second = both[:, :, :WIDE], both[:, :, WIDE:]
    mine = pick(core, first, second)
    theirs = swap(pick(core, second, first))
    low, high = pick(core, mine, theirs).astype(f32), pick(core, theirs, mine).astype(f32)
    columns = []
    for start in (edge, 0):
        for g in range(4):
            for half in (low, high):
                columns.append(half[g, :, start : start + HALF])
    grad_gate_inner = jnp.concatenate(columns, axis=1)
    grad_shared = jnp.sum(low[:, :, HALF:edge], axis=0)
    slot, turned_slot = high[:, :, HALF : HALF + 128], high[:, :, HALF + 128 : edge]
    steps = slot[:, :, :HEADS] + jnp.concatenate(
        [turned_slot[:, :, 6:HEADS], turned_slot[:, :, :6]], axis=2
    )
    grad_step = jnp.concatenate([steps[g] for g in range(4)], axis=1)
    taps = jnp.sum(slot[:, :5, SMALL_AT : SMALL_AT + 52], axis=0)
    sums = slot[:, 5:8, SMALL_AT : SMALL_AT + HEADS].transpose(1, 0, 2).reshape(3, 48)
    grad_output_gain = jnp.sum(grad_out * out_proj[0].astype(f32), axis=1) / output_gain[0].astype(
        f32
    )
    grad_input_gain = (
        jnp.sum(grad_gate_inner * gate_inner[0].astype(f32), axis=1)
        + jnp.sum(grad_shared * shared_bc[0].astype(f32), axis=1)
        + jnp.sum(grad_step * step_proj[0].astype(f32), axis=1)
    ) / input_gain[0].astype(f32)
    return (
        layer_out[None],
        grad_in[None],
        grad_input_gain[None],
        grad_gate_inner[None],
        grad_shared[None],
        grad_step[None],
        taps[None, :4],
        taps[4:5],
        sums[0:1],
        sums[1:2],
        sums[2:3],
        grad_output_gain[None],
        grad_out[None],
    )


def solution(mesh):
    both = ("seq", "head")
    return jax.shard_map(
        per_device,
        mesh=mesh,
        in_specs=(
            P(None, both, None),
            P(None, both, None),
            P("section", both),
            P("section", both, None),
            P("section", both, None),
            P("section", both, None),
            P("section", None, both),
            P("section", both),
            P("section", None),
            P("section", None),
            P("section", None),
            P("section", both),
            P("section", both, None),
        ),
        out_specs=(
            P("section", None, both, None),
            P("section", None, both, None),
            P("section", both),
            P("section", both, None),
            P("section", both, None),
            P("section", both, None),
            P("section", None, both),
            P("section", both),
            P("section", None),
            P("section", None),
            P("section", None),
            P("section", both),
            P("section", both, None),
        ),
        check_vma=False,
    )
```
